32 devices in a mesh: wide: 8 (over z, x), narrow: 4 (over y, core).
Axes of the slice: x: 2, y: 2, z: 4, core: 2. Of those that a mesh axis runs over, the one named last changes fastest.
Arguments:
- tokens: bfloat16 [32768, 512], P(('wide', 'narrow')), may hold values from -8 to 8
- image: bfloat16 [75264, 512], P(('wide', 'narrow')), may hold values from -6 to 6
- segments: int32 [32, 1024], P(('wide', 'narrow')), may hold values from 0 to 2, never falling along the last dimension, each value on 1 to 512 neighbouring positions
- valid_len: int32 [32], P(('wide', 'narrow')), may hold values from 768 to 1024
- cotangent: bfloat16 [32768, 512], P(('wide', 'narrow')), may hold values from -6 to 6
- w_attn: float32 [8, 512, 512], P(None, ('wide', 'narrow')), may hold values from -1.41421356 to 1.41421356
- w_ffn: float32 [2, 512, 1024], P(None, ('wide', 'narrow')), may hold values from -0.35355339 to 0.35355339
- norm_params: float32 [6, 512], P(None, ('wide', 'narrow')), may hold values from -1.2 to 2.8
- momentum_attn: float32 [8, 512, 512], P(None, ('wide', 'narrow')), may hold values from -162.9174 to 162.9174
- variance_attn: float32 [8, 512, 512], P(None, ('wide', 'narrow')), may hold values from 32.44032 to 134.3488
- momentum_ffn: float32 [2, 512, 1024], P(None, ('wide', 'narrow')), may hold values from -162.9174 to 162.9174
- variance_ffn: float32 [2, 512, 1024], P(None, ('wide', 'narrow')), may hold values from 32.44032 to 134.3488
- momentum_norm: float32 [6, 512], P(None, ('wide', 'narrow')), may hold values from -325.8348 to 325.8348
- variance_norm: float32 [6, 512], P(None, ('wide', 'narrow')), may hold values from 127.7952 to 527.5648
Outputs:
- result: bfloat16 [32768, 512], P(('wide', 'narrow'))
- token_grad: float32 [32768, 512], P(('wide', 'narrow'))
- image_grad: float32 [75264, 512], P(('wide', 'narrow'))
- grad_attn: float32 [8, 512, 512], P(None, ('wide', 'narrow'))
- grad_ffn: float32 [2, 512, 1024], P(None, ('wide', 'narrow'))
- grad_norm: float32 [6, 512], P(None, ('wide', 'narrow'))
- new_attn: float32 [8, 512, 512], P(None, ('wide', 'narrow'))
- new_ffn: float32 [2, 512, 1024], P(None, ('wide', 'narrow'))
- new_norm: float32 [6, 512], P(None, ('wide', 'narrow'))
- new_momentum_attn: float32 [8, 512, 512], P(None, ('wide', 'narrow'))
- new_variance_attn: float32 [8, 512, 512], P(None, ('wide', 'narrow'))
- new_momentum_ffn: float32 [2, 512, 1024], P(None, ('wide', 'narrow'))
- new_variance_ffn: float32 [2, 512, 1024], P(None, ('wide', 'narrow'))
- new_momentum_norm: float32 [6, 512], P(None, ('wide', 'narrow'))
- new_variance_norm: float32 [6, 512], P(None, ('wide', 'narrow'))
- weight_norms: float32 [16], replicated
- update_norms: float32 [16], replicated
The draws below stay inside these ranges and needn't reach their ends.
Inputs may be any that keep to these rules, and one draw needn't show every extreme that they name: `segments`: each row holds its 3 tables in order, each 1 to 512 tags long.
All inputs are finite; a program needn't handle non-finite values.
Results may differ from the reference program's by a relative error of at most 0.04.
The reference program's roundings to bfloat16 on the way count: a program that leaves them out, or rounds other values in their place, can miss the bound.
Values may be sent and summed in bfloat16 or wider, within the bound.
No kernel may reach another device: no remote copies, remote signals or barrier semaphores. Data moves between devices by JAX's collectives and lax.ppermute only.
A program may use at most 256 MiB of HBM per device.

```python
import math
import jax
import jax.numpy as jnp
import numpy as np
from jax import lax

D = 512
H = 8
HD = 64
FF = 1024
IMG = 784
ROW = 1024
TABLES_ROW = 3
STEP = 10
ROWS_ALL = 32
TOKENS = 32768
IMGTOK = 75264


def rise_vector(lower, upper, length):
    place = jnp.arange(length, dtype=jnp.float32) / (length - 1)
    return lower + (upper - lower) * place


def bounded_normal(key, dims):
    return jax.random.truncated_normal(key, -4.0, 4.0, dims, jnp.float32)


def attn_grad_sizes():
    return jnp.ones((8,), jnp.float32) * math.sqrt(TOKENS)


def second_moment(key, dims, grad_size):
    factor = jnp.exp(jax.random.uniform(key, dims, jnp.float32, math.log(0.5), math.log(2.0)))
    return (1.0 - 0.999) / 0.999 * grad_size * grad_size * 2.0 * factor


def draw_tokens(key, part):
    key = jax.random.fold_in(key, 1)
    lower, upper = (0.6, 1.8)
    values = bounded_normal(key, (TOKENS, D)) * rise_vector(lower, upper, D)[None, :]
    return values.astype(jnp.bfloat16)


def draw_w_attn(key, part):
    key = jax.random.fold_in(key, 2)
    lower, upper = (0.6, 1.8)
    scales = jnp.array([1.0, 1.0, 1.0, 4.0, 1.0, 1.0, 1.0, 4.0], jnp.float32) * D ** (-0.5)
    values = bounded_normal(key, (8, D, D)) * rise_vector(lower, upper, D)[None, :, None]
    return values * scales[:, None, None]


def draw_w_ffn(key, part):
    key = jax.random.fold_in(key, 3)
    lower, upper = (0.6, 1.8)
    scales = jnp.array([D ** (-0.5), FF ** (-0.5)], jnp.float32)
    values = bounded_normal(key, (2, D, FF)) * rise_vector(lower, upper, D)[None, :, None]
    return values * scales[:, None, None]


def draw_norm_params(key, part):
    key = jax.random.fold_in(key, 4)
    lower, upper = (0.6, 1.8)
    noise = bounded_normal(key, (6, D))
    gains = rise_vector(lower, upper, D)[None, :] * (1.0 + 0.1 * noise[0:3])
    shifts = 0.3 * noise[3:6]
    return jnp.concatenate([gains, shifts], axis=0)


def draw_momentum_attn(key, part):
    key = jax.random.fold_in(key, 5)
    lower, upper = (0.6, 1.8)
    values = bounded_normal(key, (8, D, D)) * rise_vector(lower, upper, D)[None, :, None]
    return (1.0 - 0.9) / 0.9 * attn_grad_sizes()[:, None, None] * values


def draw_variance_attn(key, part):
    key = jax.random.fold_in(key, 6)
    return second_moment(key, (8, D, D), attn_grad_sizes()[:, None, None])


def draw_momentum_ffn(key, part):
    key = jax.random.fold_in(key, 7)
    lower, upper = (0.6, 1.8)
    grad_size = math.sqrt(TOKENS)
    values = bounded_normal(key, (2, D, FF)) * rise_vector(lower, upper, D)[None, :, None]
    return (1.0 - 0.9) / 0.9 * grad_size * values


def draw_variance_ffn(key, part):
    key = jax.random.fold_in(key, 8)
    return second_moment(key, (2, D, FF), math.sqrt(TOKENS))


def draw_momentum_norm(key, part):
    key = jax.random.fold_in(key, 9)
    lower, upper = (0.6, 1.8)
    grad_size = 2.0 * math.sqrt(TOKENS)
    values = bounded_normal(key, (6, D)) * rise_vector(lower, upper, D)[None, :]
    return (1.0 - 0.9) / 0.9 * grad_size * values


def draw_variance_norm(key, part):
    key = jax.random.fold_in(key, 10)
    return second_moment(key, (6, D), 2.0 * math.sqrt(TOKENS))


def place_ends(drawn, own_key, low, high):
    shape = drawn.shape
    index_at = [jax.random.randint(jax.random.fold_in(own_key, axis), (), 0, shape[axis]) for axis in range(len(shape))]
    drawn = drawn.at[tuple(index_at)].set(low)
    longest = shape.index(max(shape))
    index_at[longest] = (index_at[longest] + 1) % shape[longest]
    return drawn.at[tuple(index_at)].set(high)


def block_levels(own_key, shape, cuts, smallest, top_value):
    def one(position, parts):
        draws = jax.random.uniform(jax.random.fold_in(jax.random.fold_in(own_key, 6), position), (parts,), jnp.float32, smallest / len(cuts), top_value / len(cuts))
        return jnp.repeat(jnp.exp(draws), shape[position] // parts).reshape((-1,) + (1,) * (len(shape) - position - 1))

    level = one(*cuts[0])
    for cut in cuts[1:]:
        level = level * one(*cut)
    return level


def length_profile(amount, total, limit, lean):
    portions = [(1 << 20) // math.isqrt(standing ** lean) + 1 for standing in range(2, amount + 1)]
    surplus, given = total - limit - (amount - 1), [1] * (amount - 1)
    while surplus > 0:
        candidates = [i for i in range(amount - 1) if given[i] < limit]
        whole, left = sum([portions[i] for i in candidates]), surplus
        for i in candidates:
            more = min(limit - given[i], max(1, left * portions[i] // whole), surplus)
            given[i] = given[i] + more
            surplus = surplus - more
    return np.array([limit] + given)


def ragged(own_key, count, total, reach, lean):
    if count == 2:
        one = jax.random.randint(own_key, (), max(1, total - reach), min(reach, total - 1) + 1)
        return jnp.stack([one, total - one])
    lengths = jnp.asarray(length_profile(count, total, reach, lean), jnp.int32)
    pairs = (count - 1) // 2
    source_of, sink = lengths[1:1 + 2 * pairs:2], lengths[2:2 + 2 * pairs:2]
    margin = jnp.minimum(source_of - 1, reach - sink)
    moved = jax.random.randint(jax.random.fold_in(own_key, 1), (pairs,), 0, 1 << 20) % (margin + 1)
    lengths = lengths.at[1:1 + 2 * pairs:2].set(source_of - moved).at[2:2 + 2 * pairs:2].set(sink + moved)
    return lengths[jax.random.permutation(jax.random.fold_in(own_key, 2), count)]


def bell_draw(own_key, shape, scale, bound, shards=(), kind=jnp.bfloat16):
    drawn = scale * jax.random.normal(own_key, shape, jnp.float32)
    if shards:
        drawn = drawn * block_levels(own_key, shape, shards, -0.22, 0.18)
    return jnp.clip(drawn, -bound, bound).astype(kind)


def setup_inputs(seed: int = 0) -> dict:
    seeds = jax.random.split(jax.random.key(seed), 15)
    tokens = draw_tokens(jax.random.fold_in(seeds[14], 71), 0)
    image = bell_draw(seeds[1], (IMGTOK, D), 1.0, 6.0, ((0, 32),))
    segments = jax.vmap(lambda own: jnp.searchsorted(jnp.cumsum(ragged(own, TABLES_ROW, ROW, ROW // 2, 1)), jnp.arange(ROW), side="right"))(jax.random.split(seeds[2], ROWS_ALL)).reshape((ROWS_ALL, ROW)).astype(jnp.int32)
    valid_len = place_ends(jax.random.randint(seeds[3], (ROWS_ALL,), 3 * ROW // 4, ROW + 1), jax.random.fold_in(seeds[3], 1), 3 * ROW // 4, ROW).astype(jnp.int32)
    cotangent = bell_draw(seeds[4], (TOKENS, D), 1.0, 6.0, ((0, 32),))
    w_attn = draw_w_attn(jax.random.fold_in(seeds[14], 71), 0)
    w_ffn = draw_w_ffn(jax.random.fold_in(seeds[14], 71), 0)
    norm_params = draw_norm_params(jax.random.fold_in(seeds[14], 71), 0)
    momentum_attn = draw_momentum_attn(jax.random.fold_in(seeds[14], 71), 0)
    variance_attn = draw_variance_attn(jax.random.fold_in(seeds[14], 71), 0)
    momentum_ffn = draw_momentum_ffn(jax.random.fold_in(seeds[14], 71), 0)
    variance_ffn = draw_variance_ffn(jax.random.fold_in(seeds[14], 71), 0)
    momentum_norm = draw_momentum_norm(jax.random.fold_in(seeds[14], 71), 0)
    variance_norm = draw_variance_norm(jax.random.fold_in(seeds[14], 71), 0)
    return {"tokens": tokens, "image": image, "segments": segments, "valid_len": valid_len, "cotangent": cotangent, "w_attn": w_attn, "w_ffn": w_ffn, "norm_params": norm_params, "momentum_attn": momentum_attn, "variance_attn": variance_attn, "momentum_ffn": momentum_ffn, "variance_ffn": variance_ffn, "momentum_norm": momentum_norm, "variance_norm": variance_norm}


HIGHEST_PRECISION = lax.Precision.HIGHEST
MASKED_SCORE = -1000000000.0
BETA_FIRST = 0.9
BETA_SECOND = 0.999
LEARN_RATE = 0.3
WEIGHT_DECAY = 0.01
ADAM_EPSILON = 1e-06
NORM_EPSILON = 1e-05

@jax.custom_vjp
def low(v):
    return lax.optimization_barrier(v.astype(jnp.bfloat16)).astype(jnp.float32)

@jax.custom_vjp
def low_back(v):
    return v

def low_keep(v):
    return (low(v), None)

def low_pass(kept, grad):
    return (grad,)

def back_keep(v):
    return (v, None)

def back_low(kept, grad):
    return (low(grad),)
low.defvjp(low_keep, low_pass)
low_back.defvjp(back_keep, back_low)

def rounded_both(value):
    return low(low_back(value))

def product(left, right):
    return jnp.dot(left, right, precision=HIGHEST_PRECISION)

def layer_norm(hidden, gain, shift):
    centre = hidden - lax.optimization_barrier(jnp.mean(hidden, axis=-1, keepdims=True))
    spread = lax.optimization_barrier(jnp.mean(centre * centre, axis=-1, keepdims=True))
    return centre * lax.rsqrt(spread + NORM_EPSILON) * gain + shift

def attend(query, keys, values, allowed):
    count = query.shape[0]
    query_heads = query.reshape(count, H, HD)
    key_heads = keys.reshape(keys.shape[0], H, HD)
    value_heads = values.reshape(values.shape[0], H, HD)
    scores = low_back(jnp.einsum('qhd,khd->hqk', query_heads, key_heads, precision=HIGHEST_PRECISION)) * HD ** (-0.5)
    scores = jnp.where(allowed[None], scores, MASKED_SCORE)
    probs = low(jax.nn.softmax(scores, axis=-1))
    mixed = jnp.einsum('hqk,khd->qhd', probs, value_heads, precision=HIGHEST_PRECISION)
    return mixed.reshape(count, H * HD)

def row_pass(inputs, pictures, segment, valid, attn, ffn, norms):
    places = jnp.arange(ROW)
    self_allowed = (segment[:, None] == segment[None, :]) & (places[None, :] <= places[:, None])
    self_allowed = self_allowed & ((places[None, :] < valid) | (places[None, :] == places[:, None]))
    tables = jnp.arange(TABLES_ROW * IMG) // IMG
    cross_allowed = segment[:, None] == tables[None, :]
    query = rounded_both(product(inputs, attn[0]))
    keys = rounded_both(product(inputs, attn[1]))
    values = rounded_both(product(inputs, attn[2]))
    mixed = rounded_both(attend(query, keys, values, self_allowed))
    branch = low_back(product(mixed, attn[3]))
    normed_one = layer_norm(inputs + branch, norms[0], norms[3])
    normed_one_low = low(normed_one)
    cross_query = rounded_both(product(normed_one_low, attn[4]))
    cross_keys = rounded_both(product(pictures, attn[5]))
    cross_values = rounded_both(product(pictures, attn[6]))
    cross_mixed = rounded_both(attend(cross_query, cross_keys, cross_values, cross_allowed))
    cross_branch = low_back(product(cross_mixed, attn[7]))
    normed_two = layer_norm(normed_one + cross_branch, norms[1], norms[4])
    normed_two_low = low(normed_two)
    hidden = low_back(product(normed_two_low, ffn[0]))
    active = low(jax.nn.gelu(hidden, approximate=True))
    down = low_back(product(active, ffn[1].T))
    return layer_norm(normed_two + down, norms[2], norms[5])

def lamb_moments(weight, grad, first, second, decay):
    first_new = BETA_FIRST * first + (1.0 - BETA_FIRST) * grad
    second_new = BETA_SECOND * second + (1.0 - BETA_SECOND) * grad * grad
    first_hat = first_new / (1.0 - BETA_FIRST ** STEP)
    second_hat = second_new / (1.0 - BETA_SECOND ** STEP)
    update = first_hat / (jnp.sqrt(second_hat) + ADAM_EPSILON) + decay * weight
    return (first_new, second_new, update)

def squares(tensor):
    return lax.optimization_barrier(jnp.sum(tensor * tensor, axis=tuple(range(1, tensor.ndim))))

def reference(tokens, image, segments, valid_len, cotangent, w_attn, w_ffn, norm_params, momentum_attn, variance_attn, momentum_ffn, variance_ffn, momentum_norm, variance_norm):
    inputs = tokens.astype(jnp.float32).reshape(ROWS_ALL, ROW, D)
    pictures = image.astype(jnp.float32).reshape(ROWS_ALL, TABLES_ROW * IMG, D)
    live = (jnp.arange(ROW)[None, :] < valid_len[:, None]).astype(jnp.float32)
    upstream = cotangent.astype(jnp.float32).reshape(ROWS_ALL, ROW, D) * live[:, :, None]

    def forward(inputs, pictures, attn, ffn, norms):
        attn = low(attn)
        ffn = low(ffn)
        norms = low(norms)

        def one_row(item):
            return row_pass(item[0], item[1], item[2], item[3], attn, ffn, norms)
        return lax.map(jax.checkpoint(one_row), (inputs, pictures, segments, valid_len))
    outcome, pullback = jax.vjp(forward, inputs, pictures, w_attn, w_ffn, norm_params)
    token_grad, image_grad, grad_attn, grad_ffn, grad_norm = pullback(upstream)
    first_attn, second_attn, update_attn = lamb_moments(w_attn, grad_attn, momentum_attn, variance_attn, WEIGHT_DECAY)
    first_ffn, second_ffn, update_ffn = lamb_moments(w_ffn, grad_ffn, momentum_ffn, variance_ffn, WEIGHT_DECAY)
    first_norm, second_norm, update_norm = lamb_moments(norm_params, grad_norm, momentum_norm, variance_norm, 0.0)
    weight_norms = jnp.sqrt(jnp.concatenate([squares(w_attn), squares(w_ffn), squares(norm_params)]))
    update_norms = jnp.sqrt(jnp.concatenate([squares(update_attn), squares(update_ffn), squares(update_norm)]))
    ratio = weight_norms / update_norms
    new_attn = w_attn - LEARN_RATE * ratio[0:8, None, None] * update_attn
    new_ffn = w_ffn - LEARN_RATE * ratio[8:10, None, None] * update_ffn
    new_norm = norm_params - LEARN_RATE * ratio[10:16, None] * update_norm
    result = outcome.reshape(TOKENS, D).astype(jnp.bfloat16)
    return (result, token_grad.reshape(TOKENS, D), image_grad.reshape(IMGTOK, D), grad_attn, grad_ffn, grad_norm, new_attn, new_ffn, new_norm, first_attn, second_attn, first_ffn, second_ffn, first_norm, second_norm, weight_norms, update_norms)
```

```python
import jax
import jax.numpy as jnp
from jax import lax
from jax.experimental import pallas as pl
from jax.experimental.pallas import tpu as pltpu
from jax.sharding import PartitionSpec as P

HD = 64
HEADS = 8
IMG = 784
TABLES = 3
STEP = 10
QB = 256

MASKED_SCORE = -1000000000.0
BETA_FIRST = 0.9
BETA_SECOND = 0.999
LEARN_RATE = 0.3
WEIGHT_DECAY = 0.01
ADAM_EPSILON = 1e-06
NORM_EPSILON = 1e-05

AXES = ("wide", "narrow")
F32 = jnp.float32
BF16 = jnp.bfloat16
VMEM = pl.BlockSpec(memory_space=pltpu.VMEM)
SMEM = pl.BlockSpec(memory_space=pltpu.SMEM)


def dot(left, right, left_dim, right_dim):
    return lax.dot_general(
        left, right, (((left_dim,), (right_dim,)), ((), ())), preferred_element_type=F32
    )


def params(mib):
    return pltpu.CompilerParams(vmem_limit_bytes=mib * 2**20)


def normalise(hidden):
    centre = hidden - jnp.mean(hidden, axis=-1, keepdims=True)
    scale = lax.rsqrt(jnp.mean(centre * centre, axis=-1, keepdims=True) + NORM_EPSILON)
    return centre * scale, scale


def norm_back(grad, gain, normed, scale):
    inner = grad * gain
    return scale * (
        inner
        - jnp.mean(inner, axis=-1, keepdims=True)
        - normed * jnp.mean(inner * normed, axis=-1, keepdims=True)
    )


def column_sum(value):
    return jnp.sum(value, axis=0, keepdims=True)


def project_kernel(x_ref, w_ref, q_ref, k_ref, v_ref):
    width = x_ref.shape[1]
    for block in range(x_ref.shape[0] // QB):
        cols = slice(block * QB, (block + 1) * QB)
        x = x_ref[cols, :]
        q_ref[:, cols] = (dot(w_ref[:, 0:width], x, 0, 1).astype(BF16) * 0.125).astype(BF16)
        k_ref[:, cols] = dot(w_ref[:, width : 2 * width], x, 0, 1).astype(BF16)
        v_ref[:, cols] = dot(w_ref[:, 2 * width : 3 * width], x, 0, 1).astype(BF16)


def self_mask(info_ref, block, first, count):
    second, third, valid = info_ref[0], info_ref[1], info_ref[2]
    place = block * QB + lax.broadcasted_iota(jnp.int32, (1, QB), 1)
    low = jnp.where(place < second, 0, jnp.where(place < third, second, third))
    high = jnp.minimum(place, valid - 1)
    key = first + lax.broadcasted_iota(jnp.int32, (count, QB), 0)
    return (key >= low) & ((key <= high) | (key == place))


def self_first(info_ref, block):
    second, third = info_ref[0], info_ref[1]
    place = block * QB
    return jnp.where(place < second, 0, jnp.where(place < third, second, third))


def self_blocks(info_ref, rows, run):
    for block in range(rows // QB):
        first = self_first(info_ref, block)
        for back in range(min(block, 2) + 1):
            start = (block - back) * QB
            enough = first >= start if back < min(block, 2) else True
            more = first < start + QB if back > 0 else True

            @pl.when(jnp.logical_and(enough, more))
            def _():
                run(block, start, (back + 1) * QB)


def self_forward_kernel(info_ref, q_ref, k_ref, v_ref, o_ref, log_ref):
    def run(block, start, count):
        cols = slice(block * QB, (block + 1) * QB)
        keys = slice(start, start + count)
        allowed = self_mask(info_ref, block, start, count)

        def head(index, carry):
            rows = pl.ds(pl.multiple_of(index * HD, HD), HD)
            scores = dot(k_ref[rows, keys], q_ref[rows, cols], 0, 0)
            scores = jnp.where(allowed, scores, MASKED_SCORE)
            highest = jnp.max(scores, axis=0, keepdims=True)
            expo = jnp.exp(scores - highest)
            total = jnp.sum(expo, axis=0, keepdims=True)
            mixed = dot(v_ref[rows, keys], expo.astype(BF16), 1, 0)
            o_ref[rows, cols] = (mixed / total).astype(BF16)
            log_ref[index, :, cols] = highest + jnp.log(total)
            return carry

        lax.fori_loop(0, HEADS, head, 0, unroll=2)

    self_blocks(info_ref, q_ref.shape[1], run)


def self_backward_kernel(
    info_ref, q_ref, k_ref, v_ref, o_ref, log_ref, do_ref, dq_ref, dk_ref, dv_ref, sum_k, sum_v
):
    sum_k[...] = jnp.zeros(sum_k.shape, F32)
    sum_v[...] = jnp.zeros(sum_v.shape, F32)

    def run(block, start, count):
        cols = slice(block * QB, (block + 1) * QB)
        keys = slice(start, start + count)
        allowed = self_mask(info_ref, block, start, count)

        def head(index, carry):
            rows = pl.ds(pl.multiple_of(index * HD, HD), HD)
            query = q_ref[rows, cols]
            grad = do_ref[rows, cols]
            scores = dot(k_ref[rows, keys], query, 0, 0)
            scores = jnp.where(allowed, scores, MASKED_SCORE)
            probs = jnp.exp(scores - log_ref[index, :, cols])
            level = column_sum(grad.astype(F32) * o_ref[rows, cols].astype(F32))
            grad_probs = dot(v_ref[rows, keys], grad, 0, 0)
            grad_scores = (probs * (grad_probs - level)).astype(BF16)
            sum_v[rows, keys] += dot(grad, probs.astype(BF16), 1, 1)
            sum_k[rows, keys] += dot(query, grad_scores, 1, 1)
            dq_ref[rows, cols] = (dot(k_ref[rows, keys], grad_scores, 1, 0) * 0.125).astype(BF16)
            return carry

        lax.fori_loop(0, HEADS, head, 0, unroll=2)

    self_blocks(info_ref, q_ref.shape[1], run)
    dk_ref[...] = sum_k[...].astype(BF16)
    dv_ref[...] = sum_v[...].astype(BF16)


def mid_kernel(x_ref, o_ref, wo_ref, cq_ref, norm_ref, n_ref, r_ref, q_ref):
    gain, shift = norm_ref[0:1, :], norm_ref[3:4, :]

    def step(block, carry):
        rows = pl.ds(pl.multiple_of(block * QB, QB), QB)
        branch = dot(o_ref[:, rows], wo_ref[...], 0, 0)
        normed, scale = normalise(x_ref[rows, :].astype(F32) + branch)
        n_ref[rows, :] = normed
        r_ref[rows, :] = scale
        low = (normed * gain + shift).astype(BF16)
        q_ref[:, rows] = (dot(cq_ref[...], low, 0, 1).astype(BF16) * 0.125).astype(BF16)
        return carry

    lax.fori_loop(0, x_ref.shape[0] // QB, step, 0)


def image_kernel(image_ref, ck_ref, cv_ref, k_ref, v_ref):
    def step(table, carry):
        rows = pl.ds(pl.multiple_of(table * IMG, 16), IMG)
        image = image_ref[rows, :]
        k_ref[table] = dot(ck_ref[...], image, 0, 1).astype(BF16)
        v_ref[table] = dot(cv_ref[...], image, 0, 1).astype(BF16)
        return carry

    lax.fori_loop(0, TABLES, step, 0)


def cross_blocks(info_ref, rows, run):
    def pair(index, carry):
        block = index // TABLES
        table = index % TABLES
        second, third = info_ref[0], info_ref[1]
        begin = jnp.where(table == 0, 0, jnp.where(table == 1, second, third))
        end = jnp.where(table == 0, second, jnp.where(table == 1, third, rows))
        start = block * QB

        @pl.when(jnp.logical_and(begin < start + QB, end > start))
        def _():
            place = start + lax.broadcasted_iota(jnp.int32, (1, QB), 1)
            run(pl.ds(pl.multiple_of(start, QB), QB), table, (place >= begin) & (place < end))

        return carry

    lax.fori_loop(0, rows // QB * TABLES, pair, 0)


def cross_forward_kernel(info_ref, q_ref, k_ref, v_ref, o_ref, log_ref):
    def run(cols, table, here):
        def head(index, carry):
            rows = pl.ds(pl.multiple_of(index * HD, HD), HD)
            scores = dot(k_ref[table, rows, :], q_ref[rows, cols], 0, 0)
            highest = jnp.max(scores, axis=0, keepdims=True)
            expo = jnp.exp(scores - highest)
            total = jnp.sum(expo, axis=0, keepdims=True)
            mixed = dot(v_ref[table, rows, :], expo.astype(BF16), 1, 0)
            o_ref[rows, cols] = jnp.where(here, (mixed / total).astype(BF16), o_ref[rows, cols])
            log_ref[index, :, cols] = jnp.where(
                here, highest + jnp.log(total), log_ref[index, :, cols]
            )
            return carry

        lax.fori_loop(0, HEADS, head, 0, unroll=2)

    cross_blocks(info_ref, q_ref.shape[1], run)


def cross_backward_kernel(
    info_ref, q_ref, k_ref, v_ref, o_ref, log_ref, do_ref, dq_ref, dk_ref, dv_ref, sum_k, sum_v
):
    sum_k[...] = jnp.zeros(sum_k.shape, F32)
    sum_v[...] = jnp.zeros(sum_v.shape, F32)

    def run(cols, table, here):
        def head(index, carry):
            rows = pl.ds(pl.multiple_of(index * HD, HD), HD)
            query = q_ref[rows, cols]
            grad = jnp.where(here, do_ref[rows, cols], jnp.zeros((), BF16))
            scores = dot(k_ref[table, rows, :], query, 0, 0)
            probs = jnp.exp(scores - jnp.where(here, log_ref[index, :, cols], -MASKED_SCORE))
            level = column_sum(grad.astype(F32) * o_ref[rows, cols].astype(F32))
            grad_probs = dot(v_ref[table, rows, :], grad, 0, 0)
            grad_scores = (probs * (grad_probs - level)).astype(BF16)
            sum_v[table, rows, :] += dot(grad, probs.astype(BF16), 1, 1)
            sum_k[table, rows, :] += dot(query, grad_scores, 1, 1)
            grad_query = (dot(k_ref[table, rows, :], grad_scores, 1, 0) * 0.125).astype(BF16)
            dq_ref[rows, cols] = jnp.where(here, grad_query, dq_ref[rows, cols])
            return carry

        lax.fori_loop(0, HEADS, head, 0, unroll=2)

    cross_blocks(info_ref, q_ref.shape[1], run)
    dk_ref[...] = sum_k[...].astype(BF16)
    dv_ref[...] = sum_v[...].astype(BF16)


def feed_kernel(
    info_ref, o_ref, n1_ref, cot_ref, co_ref, up_ref, down_ref, norm_ref,
    result_ref, dh_ref, do_ref, grad_ref, dnorm_ref, sum_up, sum_down, sum_out, sum_norm,
):
    valid = info_ref[2]
    width = cot_ref.shape[1]
    hidden_width = up_ref.shape[1]
    sum_up[...] = jnp.zeros(sum_up.shape, F32)
    sum_down[...] = jnp.zeros(sum_down.shape, F32)
    sum_out[...] = jnp.zeros(sum_out.shape, F32)
    sum_norm[...] = jnp.zeros(sum_norm.shape, F32)
    root = 0.7978845608028654

    def step(block, carry):
        rows = pl.ds(pl.multiple_of(block * QB, QB), QB)
        mixed = o_ref[:, rows]
        first = n1_ref[rows, :] * norm_ref[0:1, :] + norm_ref[3:4, :]
        n2, r2 = normalise(first + dot(mixed, co_ref[...], 0, 0))
        x2 = n2 * norm_ref[1:2, :] + norm_ref[4:5, :]
        x2_low = x2.astype(BF16)
        u = dot(x2_low, up_ref[...], 1, 0)
        square = u * u
        curve = jnp.tanh(root * u * (1.0 + 0.044715 * square))
        half = 0.5 * (1.0 + curve)
        active = (u * half).astype(BF16)
        slope = half + 0.5 * u * (1.0 - curve * curve) * (root * (1.0 + 3 * 0.044715 * square))
        n3, r3 = normalise(x2 + dot(active, down_ref[...], 1, 1))
        result_ref[rows, :] = (n3 * norm_ref[2:3, :] + norm_ref[5:6, :]).astype(BF16)
        place = block * QB + lax.broadcasted_iota(jnp.int32, (QB, 1), 0)
        dy = jnp.where(place < valid, cot_ref[rows, :].astype(F32), 0.0)
        sum_norm[2:3, :] += column_sum(dy * n3)
        sum_norm[5:6, :] += column_sum(dy)
        dh3 = norm_back(dy, norm_ref[2:3, :], n3, r3)
        dz = dh3.astype(BF16)
        sum_down[...] += dot(dz, active, 0, 0)
        du = (dot(dz, down_ref[...], 1, 0) * slope).astype(BF16)
        sum_up[...] += dot(x2_low, du, 0, 0)
        dx2 = dh3 + dot(du, up_ref[...], 1, 1)
        sum_norm[1:2, :] += column_sum(dx2 * n2)
        sum_norm[4:5, :] += column_sum(dx2)
        dh2 = norm_back(dx2, norm_ref[1:2, :], n2, r2)
        dh_ref[rows, :] = dh2
        dac = dh2.astype(BF16)
        sum_out[...] += dot(mixed, dac, 1, 0)
        do_ref[:, rows] = dot(co_ref[...], dac, 1, 1).astype(BF16)
        return carry

    lax.fori_loop(0, cot_ref.shape[0] // QB, step, 0)
    grad_ref[:, 0:hidden_width] = sum_up[...].astype(BF16)
    grad_ref[:, hidden_width : 2 * hidden_width] = sum_down[...].astype(BF16)
    grad_ref[:, 2 * hidden_width : 2 * hidden_width + width] = sum_out[...].astype(BF16)
    dnorm_ref[...] = sum_norm[...]


def inner_kernel(
    dq_ref, dh2_ref, n1_ref, r1_ref, o_ref, cq_ref, wo_ref, norm_ref,
    dh_ref, do_ref, grad_ref, dnorm_ref, sum_q, sum_o, sum_norm,
):
    sum_q[...] = jnp.zeros(sum_q.shape, F32)
    sum_o[...] = jnp.zeros(sum_o.shape, F32)
    sum_norm[...] = jnp.zeros(sum_norm.shape, F32)
    width = sum_q.shape[0]
    gain, shift = norm_ref[0:1, :], norm_ref[3:4, :]

    def step(block, carry):
        rows = pl.ds(pl.multiple_of(block * QB, QB), QB)
        dq = dq_ref[:, rows]
        normed = n1_ref[rows, :]
        low = (normed * gain + shift).astype(BF16)
        sum_q[...] += dot(low, dq, 0, 1)
        dx1 = dh2_ref[rows, :] + dot(dq, cq_ref[...], 0, 1)
        sum_norm[0:1, :] += column_sum(dx1 * normed)
        sum_norm[1:2, :] += column_sum(dx1)
        dh1 = norm_back(dx1, gain, normed, r1_ref[rows, :])
        dh_ref[rows, :] = dh1
        da = dh1.astype(BF16)
        sum_o[...] += dot(o_ref[:, rows], da, 1, 0)
        do_ref[:, rows] = dot(wo_ref[...], da, 1, 1).astype(BF16)
        return carry

    lax.fori_loop(0, dh2_ref.shape[0] // QB, step, 0)
    grad_ref[:, 0:width] = sum_q[...].astype(BF16)
    grad_ref[:, width : 2 * width] = sum_o[...].astype(BF16)
    dnorm_ref[...] = sum_norm[...]


def image_weight_kernel(image_ref, dk_ref, dv_ref, grad_ref, sum_k, sum_v):
    sum_k[...] = jnp.zeros(sum_k.shape, F32)
    sum_v[...] = jnp.zeros(sum_v.shape, F32)
    width = sum_k.shape[0]

    def step(table, carry):
        rows = pl.ds(pl.multiple_of(table * IMG, 16), IMG)
        image = image_ref[rows, :]
        sum_k[...] += dot(image, dk_ref[table], 0, 1)
        sum_v[...] += dot(image, dv_ref[table], 0, 1)
        return carry

    lax.fori_loop(0, TABLES, step, 0)
    grad_ref[:, 0:width] = sum_k[...].astype(BF16)
    grad_ref[:, width : 2 * width] = sum_v[...].astype(BF16)


def image_grad_kernel(dk_ref, dv_ref, ck_ref, cv_ref, out_ref):
    def step(table, carry):
        rows = pl.ds(pl.multiple_of(table * IMG, 16), IMG)
        out_ref[rows, :] = dot(dk_ref[table], ck_ref[...], 0, 1) + dot(
            dv_ref[table], cv_ref[...], 0, 1
        )
        return carry

    lax.fori_loop(0, TABLES, step, 0)


def project_weight_kernel(x_ref, dq_ref, dk_ref, dv_ref, grad_ref):
    width = x_ref.shape[1]
    for index, ref in enumerate((dq_ref, dk_ref, dv_ref)):
        grad_ref[:, index * width : (index + 1) * width] = dot(x_ref[...], ref[...], 0, 1).astype(
            BF16
        )


def token_grad_kernel(dq_ref, dk_ref, dv_ref, w_ref, dh_ref, out_ref):
    width = dh_ref.shape[1]

    def step(block, carry):
        rows = pl.ds(pl.multiple_of(block * QB, QB), QB)
        out_ref[rows, :] = (
            dh_ref[rows, :]
            + dot(dq_ref[:, rows], w_ref[:, 0:width], 0, 1)
            + dot(dk_ref[:, rows], w_ref[:, width : 2 * width], 0, 1)
            + dot(dv_ref[:, rows], w_ref[:, 2 * width : 3 * width], 0, 1)
        )
        return carry

    lax.fori_loop(0, dh_ref.shape[0] // QB, step, 0)


def shaped(*dims, kind=BF16):
    return jax.ShapeDtypeStruct(dims, kind)


def call(kernel, out_shape, operands, name, info=False, scratch=(), mib=48):
    specs = [VMEM] * len(operands)
    if info:
        specs[0] = SMEM
    return pl.pallas_call(
        kernel,
        out_shape=out_shape,
        in_specs=specs,
        out_specs=jax.tree.map(lambda _: VMEM, out_shape),
        scratch_shapes=[pltpu.VMEM(dims, F32) for dims in scratch],
        compiler_params=params(mib),
        name=name,
    )(*operands)


def device_index():
    return lax.axis_index("wide") * lax.axis_size("narrow") + lax.axis_index("narrow")


def swap(value, bit, count):
    return lax.ppermute(value, AXES, [(i, i ^ (1 << bit)) for i in range(count)])


def gather_rows(part, count):
    bits = count.bit_length() - 1
    me = device_index()
    order = list(range(3, bits)) + [2, 1, 0]
    value = part.reshape((1,) * bits + part.shape)
    for bit in order:
        axis = bits - 1 - bit
        other = swap(value, bit, count)
        mine_first = (me >> bit) & 1 == 0
        value = jnp.concatenate(
            [jnp.where(mine_first, value, other), jnp.where(mine_first, other, value)], axis=axis
        )
    return value.reshape((count * part.shape[0],) + part.shape[1:])


def scatter_rows(full, count, order):
    bits = count.bit_length() - 1
    me = device_index()
    value = full.reshape((2,) * bits + (full.shape[0] // count,) + full.shape[1:])
    for bit in order:
        axis = bits - 1 - bit
        mine = (me >> bit) & 1
        keep = lax.dynamic_index_in_dim(value, mine, axis, True)
        other = swap(lax.dynamic_index_in_dim(value, 1 - mine, axis, True), bit, count)
        value = keep.astype(F32) + other.astype(F32)
        if bit != order[-1]:
            value = value.astype(BF16)
    return value.reshape((full.shape[0] // count,) + full.shape[1:])


def sum_all(value, count):
    for bit in range(count.bit_length() - 1):
        value = value + swap(value, bit, count)
    return value


def lamb_moments(weight, grad, first, second, decay):
    first_new = BETA_FIRST * first + (1.0 - BETA_FIRST) * grad
    second_new = BETA_SECOND * second + (1.0 - BETA_SECOND) * grad * grad
    first_hat = first_new / (1.0 - BETA_FIRST**STEP)
    second_hat = second_new / (1.0 - BETA_SECOND**STEP)
    update = first_hat / (jnp.sqrt(second_hat) + ADAM_EPSILON) + decay * weight
    return (first_new, second_new, update)


def tensor_squares(first_part, second_part, third_part):
    return jnp.concatenate(
        [
            jnp.sum(first_part * first_part, axis=(1, 2)),
            jnp.sum(second_part * second_part, axis=(1, 2)),
            jnp.sum(third_part * third_part, axis=1),
        ]
    )


def pack(stack):
    return jnp.swapaxes(stack, 0, 1).reshape(stack.shape[1], -1)


def unpack(flat, count):
    return jnp.swapaxes(flat.reshape(flat.shape[0], count, -1), 0, 1)


def local(
    tokens,
    image,
    segments,
    valid_len,
    cotangent,
    w_attn,
    w_ffn,
    norm_params,
    momentum_attn,
    variance_attn,
    momentum_ffn,
    variance_ffn,
    momentum_norm,
    variance_norm,
):
    count = lax.axis_size("wide") * lax.axis_size("narrow")
    bits = count.bit_length() - 1
    tags, width = tokens.shape
    hidden_width = w_ffn.shape[2]
    segment = segments[0]
    info = jnp.stack(
        [jnp.sum(segment < 1), jnp.sum(segment < 2), valid_len[0], valid_len[0]]
    ).astype(jnp.int32)

    attn_low = w_attn.astype(BF16)
    norm_low = jnp.pad(norm_params.astype(BF16).T, ((0, 0), (0, 122)))
    first_part = jnp.concatenate([pack(attn_low[0:3]), norm_low], axis=1)
    rest_part = jnp.concatenate([pack(attn_low[3:8]), pack(w_ffn.astype(BF16))], axis=1)
    first_full = gather_rows(first_part, count)
    rest_full = lax.all_gather(rest_part, AXES, axis=0, tiled=True)
    w_qkv = first_full[:, 0 : 3 * width]
    norms = jnp.pad(first_full[:, 3 * width : 3 * width + 6].T, ((0, 2), (0, 0))).astype(F32)
    wo, cq, ck, cv, co = [rest_full[:, i * width : (i + 1) * width] for i in range(5)]
    up = rest_full[:, 5 * width : 5 * width + hidden_width]
    down = rest_full[:, 5 * width + hidden_width :]

    wide_shape = shaped(width, tags)
    log_shape = shaped(HEADS, 1, tags, kind=F32)
    q, k, v = call(project_kernel, [wide_shape] * 3, (tokens, w_qkv), "project")
    o, log_self = call(
        self_forward_kernel, [wide_shape, log_shape], (info, q, k, v), "self_forward", True
    )
    n1, r1, qc = call(
        mid_kernel,
        [shaped(tags, width, kind=F32), shaped(tags, 1, kind=F32), wide_shape],
        (tokens, o, wo, cq, norms),
        "mid",
    )
    image_shape = shaped(TABLES, width, IMG)
    kc, vc = call(image_kernel, [image_shape] * 2, (image, ck, cv), "image_project")
    oc, log_cross = call(
        cross_forward_kernel, [wide_shape, log_shape], (info, qc, kc, vc), "cross_forward", True
    )
    result, dh2, doc, grad_feed, norm_feed = call(
        feed_kernel,
        [
            shaped(tags, width),
            shaped(tags, width, kind=F32),
            wide_shape,
            shaped(width, 2 * hidden_width + width),
            shaped(8, width, kind=F32),
        ],
        (info, oc, n1, cotangent, co, up, down, norms),
        "feed",
        True,
        [(width, hidden_width), (width, hidden_width), (width, width), (8, width)],
        56,
    )
    reduced_feed = scatter_rows(grad_feed, count, [0, 2, 1] + list(range(bits - 1, 2, -1)))
    dqc, dkc, dvc = call(
        cross_backward_kernel,
        [wide_shape, image_shape, image_shape],
        (info, qc, kc, vc, oc, log_cross, doc),
        "cross_backward",
        True,
        [(TABLES, width, IMG), (TABLES, width, IMG)],
        56,
    )
    grad_image_weight = call(
        image_weight_kernel,
        shaped(width, 2 * width),
        (image, dkc, dvc),
        "image_weight",
        False,
        [(width, width), (width, width)],
    )
    reduced_image = scatter_rows(grad_image_weight, count, [0, 1, 2] + list(range(bits - 1, 2, -1)))
    dh1, do, grad_inner, norm_inner = call(
        inner_kernel,
        [
            shaped(tags, width, kind=F32),
            wide_shape,
            shaped(width, 2 * width),
            shaped(8, width, kind=F32),
        ],
        (dqc, dh2, n1, r1, o, cq, wo, norms),
        "inner",
        False,
        [(width, width), (width, width), (8, width)],
    )
    reduced_inner = scatter_rows(grad_inner, count, [0, 2, 1] + list(range(bits - 1, 2, -1)))
    dq, dk, dv = call(
        self_backward_kernel,
        [wide_shape] * 3,
        (info, q, k, v, o, log_self, do),
        "self_backward",
        True,
        [(width, tags), (width, tags)],
    )
    grad_project = call(
        project_weight_kernel, shaped(width, 3 * width), (tokens, dq, dk, dv), "project_weight"
    )
    norm_grads = jnp.stack(
        [norm_inner[0], norm_feed[1], norm_feed[2], norm_inner[1], norm_feed[4], norm_feed[5]],
        axis=1,
    )
    norm_grads = jnp.pad(norm_grads, ((0, 0), (0, 122))).astype(BF16)
    reduced_last = scatter_rows(
        jnp.concatenate([grad_project, norm_grads], axis=1),
        count,
        [0, 1, 2] + list(range(bits - 1, 2, -1)),
    )
    token_grad = call(
        token_grad_kernel,
        shaped(tags, width, kind=F32),
        (dq, dk, dv, w_qkv, dh1),
        "token_grad",
    )
    image_grad = call(
        image_grad_kernel, shaped(image.shape[0], width, kind=F32), (dkc, dvc, ck, cv), "image_grad"
    )

    parts = unpack(reduced_last[:, 0 : 3 * width], 3)
    inner_parts = unpack(reduced_inner, 2)
    grad_attn = jnp.concatenate(
        [
            parts,
            inner_parts[1:2],
            inner_parts[0:1],
            unpack(reduced_image, 2),
            reduced_feed[None, :, 2 * hidden_width :],
        ],
        axis=0,
    )
    grad_ffn = unpack(reduced_feed[:, 0 : 2 * hidden_width], 2)
    grad_norm = reduced_last[:, 3 * width : 3 * width + 6].T

    first_attn, second_attn, update_attn = lamb_moments(
        w_attn, grad_attn, momentum_attn, variance_attn, WEIGHT_DECAY
    )
    first_ffn, second_ffn, update_ffn = lamb_moments(
        w_ffn, grad_ffn, momentum_ffn, variance_ffn, WEIGHT_DECAY
    )
    first_norm, second_norm, update_norm = lamb_moments(
        norm_params, grad_norm, momentum_norm, variance_norm, 0.0
    )
    sums = sum_all(
        jnp.stack(
            [
                tensor_squares(w_attn, w_ffn, norm_params),
                tensor_squares(update_attn, update_ffn, update_norm),
            ]
        ),
        count,
    )
    weight_norms = jnp.sqrt(sums[0])
    update_norms = jnp.sqrt(sums[1])
    ratio = weight_norms / update_norms
    new_attn = w_attn - LEARN_RATE * ratio[0:8, None, None] * update_attn
    new_ffn = w_ffn - LEARN_RATE * ratio[8:10, None, None] * update_ffn
    new_norm = norm_params - LEARN_RATE * ratio[10:16, None] * update_norm
    return (
        result,
        token_grad,
        image_grad,
        grad_attn,
        grad_ffn,
        grad_norm,
        new_attn,
        new_ffn,
        new_norm,
        first_attn,
        second_attn,
        first_ffn,
        second_ffn,
        first_norm,
        second_norm,
        weight_norms,
        update_norms,
    )


def solution(mesh):
    rows = P(AXES, None)
    stack = P(None, AXES, None)
    flat = P(None, AXES)
    in_specs = (rows, rows, rows, P(AXES), rows) + (stack, stack, flat)
    in_specs = in_specs + (stack, stack, stack, stack, flat, flat)
    out_specs = (rows, rows, rows, stack, stack, flat, stack, stack, flat)
    out_specs = out_specs + (stack, stack, stack, stack, flat, flat, P(), P())
    return jax.shard_map(local, mesh=mesh, in_specs=in_specs, out_specs=out_specs, check_vma=False)
```

```python
import jax
import jax.numpy as jnp
from jax import lax
from jax.experimental import pallas as pl
from jax.experimental.pallas import tpu as pltpu
from jax.sharding import PartitionSpec as P

HD = 64
HEADS = 8
IMG = 784
TABLES = 3
STEP = 10
QB = 256

MASKED_SCORE = -1000000000.0
BETA_FIRST = 0.9
BETA_SECOND = 0.999
LEARN_RATE = 0.3
WEIGHT_DECAY = 0.01
ADAM_EPSILON = 1e-06
NORM_EPSILON = 1e-05

AXES = ("wide", "narrow")
F32 = jnp.float32
BF16 = jnp.bfloat16
VMEM = pl.BlockSpec(memory_space=pltpu.VMEM)
SMEM = pl.BlockSpec(memory_space=pltpu.SMEM)


def dot(left, right, left_dim, right_dim):
    return lax.dot_general(
        left, right, (((left_dim,), (right_dim,)), ((), ())), preferred_element_type=F32
    )


def normalise(hidden):
    centre = hidden - jnp.mean(hidden, axis=-1, keepdims=True)
    scale = lax.rsqrt(jnp.mean(centre * centre, axis=-1, keepdims=True) + NORM_EPSILON)
    return centre * scale, scale


def norm_back(grad, gain, normed, scale):
    inner = grad * gain
    return scale * (
        inner
        - jnp.mean(inner, axis=-1, keepdims=True)
        - normed * jnp.mean(inner * normed, axis=-1, keepdims=True)
    )


def column_sum(value):
    return jnp.sum(value, axis=0, keepdims=True)


def pipeline(chains):
    done = object()
    live = []
    waiting = list(chains)
    while live or waiting:
        if waiting:
            live.insert(0, waiting.pop(0))
        live = [chain for chain in live if next(chain, done) is not done]


def place_blocks(me, near_ref, far_ref, out_ref):
    if near_ref.shape == out_ref.shape:
        out_ref[...] = near_ref[...]
        return
    size = near_ref.shape[1]
    for k in range(2 * near_ref.shape[0]):
        ref = far_ref if k & 1 else near_ref
        row = pl.multiple_of((me ^ k) * size, size)
        out_ref[pl.ds(row, size), :] = ref[exchange_slot(k)]


def spread_blocks(me, source, near_ref, far_ref, col):
    cols = slice(col, col + source.shape[1])
    if near_ref.shape[0] == source.shape[0]:
        near_ref[:, cols] = source[...].astype(BF16)
        far_ref[...] = jnp.zeros(far_ref.shape, BF16)
        return
    size = near_ref.shape[1]
    for k in range(2 * near_ref.shape[0]):
        ref = far_ref if k & 1 else near_ref
        row = pl.multiple_of((me ^ k) * size, size)
        ref[exchange_slot(k), :, cols] = source[pl.ds(row, size), :].astype(BF16)


def project_kernel(info_ref, x_ref, near_ref, far_ref, w_ref, norm_ref, q_ref, k_ref, v_ref):
    place_blocks(info_ref[3], near_ref, far_ref, w_ref)
    width = x_ref.shape[1]
    norm_ref[...] = jnp.transpose(w_ref[:, 3 * width :].astype(F32))[0:8, :]
    for block in range(x_ref.shape[0] // QB):
        cols = slice(block * QB, (block + 1) * QB)
        x = x_ref[cols, :]
        q_ref[:, cols] = (dot(w_ref[:, 0:width], x, 0, 1).astype(BF16) * 0.125).astype(BF16)
        k_ref[:, cols] = dot(w_ref[:, width : 2 * width], x, 0, 1).astype(BF16)
        v_ref[:, cols] = dot(w_ref[:, 2 * width : 3 * width], x, 0, 1).astype(BF16)


def head_rows(index):
    return slice(index * HD, (index + 1) * HD)


def forward_heads(query, key, value, finish, heads, count, bias, score_ref, prob_ref):
    def chain(index):
        slot = index % 2
        scores = dot(key(index), query(index), 0, 0)
        score_ref[slot, 0:count] = scores if bias is None else scores + bias[0:count]
        yield
        scores = score_ref[slot, 0:count]
        highest = jnp.max(scores, axis=0, keepdims=True)
        prob_ref[slot, 0:count] = jnp.exp(scores - highest).astype(BF16)
        yield
        ones = jnp.ones((16, count), BF16)
        mixed = dot(jnp.concatenate([value(index), ones], axis=0), prob_ref[slot, 0:count], 1, 0)
        total = mixed[HD : HD + 1]
        finish(index, (mixed[0:HD] / total).astype(BF16), highest + jnp.log(total))

    pipeline([chain(index) for index in range(heads)])


def backward_heads(
    query, key, value, grad, mixed, logs, finish, heads, count, bias,
    score_ref, level_ref, prob_ref, delta_ref,
):
    def chain(index):
        slot = index % 2
        scores = dot(key(index), query(index), 0, 0)
        score_ref[slot, 0:count] = scores if bias is None else scores + bias[0:count]
        level_ref[slot, 0:count] = dot(value(index), grad(index), 0, 0)
        yield
        level = column_sum(grad(index).astype(F32) * mixed(index).astype(F32))
        probs = jnp.exp(score_ref[slot, 0:count] - logs(index))
        prob_ref[slot, 0:count] = probs.astype(BF16)
        delta_ref[slot, 0:count] = (probs * (level_ref[slot, 0:count] - level)).astype(BF16)
        yield
        delta = delta_ref[slot, 0:count]
        finish(
            index,
            (dot(key(index), delta, 1, 0) * 0.125).astype(BF16),
            dot(query(index), delta, 1, 1),
            dot(grad(index), prob_ref[slot, 0:count], 1, 1),
        )

    pipeline([chain(index) for index in range(heads)])


def self_blocks(info_ref, rows, bias, run):
    second, third, valid = info_ref[0], info_ref[1], info_ref[2]

    def step(block, carry):
        start = block * QB
        first = jnp.where(start < second, 0, jnp.where(start < third, second, third))
        back = block - first // QB
        for extent in range(3):

            @pl.when(back == extent)
            def _():
                begin = (block - extent) * QB
                count = (extent + 1) * QB
                place = start + lax.broadcasted_iota(jnp.int32, (1, QB), 1)
                low = jnp.where(place < second, 0, jnp.where(place < third, second, third))
                high = jnp.minimum(place, valid - 1)
                key = begin + lax.broadcasted_iota(jnp.int32, (count, QB), 0)
                allowed = (key >= low) & ((key <= high) | (key == place))
                bias[0:count] = jnp.where(allowed, 0.0, MASKED_SCORE)
                run(
                    pl.ds(pl.multiple_of(start, QB), QB),
                    pl.ds(pl.multiple_of(begin, QB), count),
                    count,
                )

        return carry

    lax.fori_loop(0, rows // QB, step, 0)


def self_forward_kernel(
    info_ref, q_ref, k_ref, v_ref, o_ref, log_ref, bias_ref, score_ref, prob_ref
):
    def run(cols, keys, count):
        def finish(index, mixed, logs):
            o_ref[head_rows(index), cols] = mixed
            log_ref[index, :, cols] = logs

        forward_heads(
            lambda index: q_ref[head_rows(index), cols],
            lambda index: k_ref[head_rows(index), keys],
            lambda index: v_ref[head_rows(index), keys],
            finish, q_ref.shape[0] // HD, count, bias_ref, score_ref, prob_ref,
        )

    self_blocks(info_ref, q_ref.shape[1], bias_ref, run)


def self_backward_kernel(
    info_ref, q_ref, k_ref, v_ref, o_ref, log_ref, do_ref, dq_ref, dk_ref, dv_ref,
    sum_k, sum_v, bias_ref, score_ref, level_ref, prob_ref, delta_ref,
):
    sum_k[...] = jnp.zeros(sum_k.shape, F32)
    sum_v[...] = jnp.zeros(sum_v.shape, F32)

    def run(cols, keys, count):
        def finish(index, grad_query, grad_key, grad_value):
            dq_ref[head_rows(index), cols] = grad_query
            sum_k[head_rows(index), keys] += grad_key
            sum_v[head_rows(index), keys] += grad_value

        backward_heads(
            lambda index: q_ref[head_rows(index), cols],
            lambda index: k_ref[head_rows(index), keys],
            lambda index: v_ref[head_rows(index), keys],
            lambda index: do_ref[head_rows(index), cols],
            lambda index: o_ref[head_rows(index), cols],
            lambda index: log_ref[index, :, cols],
            finish, q_ref.shape[0] // HD, count, bias_ref,
            score_ref, level_ref, prob_ref, delta_ref,
        )

    self_blocks(info_ref, q_ref.shape[1], bias_ref, run)
    dk_ref[...] = sum_k[...].astype(BF16)
    dv_ref[...] = sum_v[...].astype(BF16)


def mid_kernel(x_ref, o_ref, w_ref, norm_ref, n_ref, r_ref, q_ref):
    gain, shift = norm_ref[0:1, :], norm_ref[3:4, :]
    width = x_ref.shape[1]

    def chain(block):
        rows = slice(block * QB, (block + 1) * QB)
        branch = dot(o_ref[:, rows], w_ref[:, 0:width], 0, 0)
        yield
        normed, scale = normalise(x_ref[rows, :].astype(F32) + branch)
        n_ref[rows, :] = normed
        r_ref[rows, :] = scale
        low = (normed * gain + shift).astype(BF16)
        yield
        query = dot(w_ref[:, width : 2 * width], low, 0, 1).astype(BF16)
        q_ref[:, rows] = (query * 0.125).astype(BF16)

    pipeline([chain(block) for block in range(x_ref.shape[0] // QB)])


def image_kernel(info_ref, image_ref, near_ref, far_ref, w_ref, k_ref, v_ref):
    place_blocks(info_ref[3], near_ref, far_ref, w_ref)
    width = image_ref.shape[1]
    for table in range(TABLES):
        image = image_ref[table * IMG : (table + 1) * IMG, :]
        k_ref[table] = dot(w_ref[:, 2 * width : 3 * width], image, 0, 1).astype(BF16)
        v_ref[table] = dot(w_ref[:, 3 * width : 4 * width], image, 0, 1).astype(BF16)


def cross_blocks(info_ref, rows, run):
    def pair(index, carry):
        block = index // TABLES
        table = index % TABLES
        second, third = info_ref[0], info_ref[1]
        begin = jnp.where(table == 0, 0, jnp.where(table == 1, second, third))
        end = jnp.where(table == 0, second, jnp.where(table == 1, third, rows))
        start = block * QB

        @pl.when(jnp.logical_and(begin < start + QB, end > start))
        def _():
            place = start + lax.broadcasted_iota(jnp.int32, (1, QB), 1)
            run(pl.ds(pl.multiple_of(start, QB), QB), table, (place >= begin) & (place < end))

        return carry

    lax.fori_loop(0, rows // QB * TABLES, pair, 0)


def cross_forward_kernel(info_ref, q_ref, k_ref, v_ref, o_ref, log_ref, score_ref, prob_ref):
    def run(cols, table, here):
        def finish(index, mixed, logs):
            rows = head_rows(index)
            o_ref[rows, cols] = jnp.where(here, mixed, o_ref[rows, cols])
            log_ref[index, :, cols] = jnp.where(here, logs, log_ref[index, :, cols])

        forward_heads(
            lambda index: q_ref[head_rows(index), cols],
            lambda index: k_ref[table, head_rows(index), :],
            lambda index: v_ref[table, head_rows(index), :],
            finish, q_ref.shape[0] // HD, IMG, None, score_ref, prob_ref,
        )

    cross_blocks(info_ref, q_ref.shape[1], run)


def cross_backward_kernel(
    info_ref, q_ref, k_ref, v_ref, o_ref, log_ref, do_ref, dq_ref, dk_ref, dv_ref,
    sum_k, sum_v, score_ref, level_ref, prob_ref, delta_ref,
):
    sum_k[...] = jnp.zeros(sum_k.shape, F32)
    sum_v[...] = jnp.zeros(sum_v.shape, F32)

    def run(cols, table, here):
        def finish(index, grad_query, grad_key, grad_value):
            rows = head_rows(index)
            dq_ref[rows, cols] = jnp.where(here, grad_query, dq_ref[rows, cols])
            sum_k[table, rows, :] += grad_key
            sum_v[table, rows, :] += grad_value

        zero = jnp.zeros((), BF16)
        backward_heads(
            lambda index: q_ref[head_rows(index), cols],
            lambda index: k_ref[table, head_rows(index), :],
            lambda index: v_ref[table, head_rows(index), :],
            lambda index: jnp.where(here, do_ref[head_rows(index), cols], zero),
            lambda index: o_ref[head_rows(index), cols],
            lambda index: jnp.where(here, log_ref[index, :, cols], -MASKED_SCORE),
            finish, q_ref.shape[0] // HD, IMG, None,
            score_ref, level_ref, prob_ref, delta_ref,
        )

    cross_blocks(info_ref, q_ref.shape[1], run)
    dk_ref[...] = sum_k[...].astype(BF16)
    dv_ref[...] = sum_v[...].astype(BF16)


def feed_kernel(
    info_ref, o_ref, n1_ref, cot_ref, co_ref, up_ref, down_ref, norm_ref,
    result_ref, dh_ref, do_ref, near_ref, far_ref, dnorm_ref,
    sum_up, sum_out, sum_norm, all_x2, all_active, all_du, all_dz, all_dac,
):
    valid = info_ref[2]
    hidden_width = up_ref.shape[1]
    sum_norm[...] = jnp.zeros(sum_norm.shape, F32)
    root = 0.7978845608028654

    def chain(block):
        rows = slice(block * QB, (block + 1) * QB)
        branch = dot(o_ref[:, rows], co_ref[...], 0, 0)
        yield
        first = n1_ref[rows, :] * norm_ref[0:1, :] + norm_ref[3:4, :]
        n2, r2 = normalise(first + branch)
        x2 = n2 * norm_ref[1:2, :] + norm_ref[4:5, :]
        x2_low = x2.astype(BF16)
        all_x2[rows, :] = x2_low
        yield
        u = dot(x2_low, up_ref[...], 1, 0)
        yield
        square = u * u
        curve = jnp.tanh(root * u * (1.0 + 0.044715 * square))
        half = 0.5 * (1.0 + curve)
        active = (u * half).astype(BF16)
        slope = half + 0.5 * u * (1.0 - curve * curve) * (root * (1.0 + 3 * 0.044715 * square))
        all_active[rows, :] = active
        yield
        down = dot(active, down_ref[...], 1, 1)
        yield
        n3, r3 = normalise(x2 + down)
        result_ref[rows, :] = (n3 * norm_ref[2:3, :] + norm_ref[5:6, :]).astype(BF16)
        place = block * QB + lax.broadcasted_iota(jnp.int32, (QB, 1), 0)
        dy = jnp.where(place < valid, cot_ref[rows, :].astype(F32), 0.0)
        sum_norm[2:3, :] += column_sum(dy * n3)
        sum_norm[5:6, :] += column_sum(dy)
        dh3 = norm_back(dy, norm_ref[2:3, :], n3, r3)
        dz = dh3.astype(BF16)
        all_dz[rows, :] = dz
        yield
        df = dot(dz, down_ref[...], 1, 0)
        yield
        du = (df * slope).astype(BF16)
        all_du[rows, :] = du
        yield
        back = dot(du, up_ref[...], 1, 1)
        yield
        dx2 = dh3 + back
        sum_norm[1:2, :] += column_sum(dx2 * n2)
        sum_norm[4:5, :] += column_sum(dx2)
        dh2 = norm_back(dx2, norm_ref[1:2, :], n2, r2)
        dh_ref[rows, :] = dh2
        dac = dh2.astype(BF16)
        all_dac[rows, :] = dac
        yield
        do_ref[:, rows] = dot(co_ref[...], dac, 1, 1).astype(BF16)

    pipeline([chain(block) for block in range(cot_ref.shape[0] // QB)])
    me = info_ref[3]
    sum_up[...] = dot(all_x2[...], all_du[...], 0, 0)
    spread_blocks(me, sum_up, near_ref, far_ref, 0)
    sum_up[...] = dot(all_dz[...], all_active[...], 0, 0)
    spread_blocks(me, sum_up, near_ref, far_ref, hidden_width)
    sum_out[...] = dot(o_ref[...], all_dac[...], 1, 0)
    spread_blocks(me, sum_out, near_ref, far_ref, 2 * hidden_width)
    dnorm_ref[...] = sum_norm[...]


def inner_kernel(
    info_ref, dq0_ref, dq1_ref, dh2_ref, n1_ref, r1_ref, o_ref, w_ref, norm_ref,
    image_ref, dk0_ref, dk1_ref, dv0_ref, dv1_ref,
    dh_ref, do_ref, near_ref, far_ref, dnorm_ref, sum_image, sum_inner, sum_norm, all_low, all_da,
):
    sum_norm[...] = jnp.zeros(sum_norm.shape, F32)
    width = dh_ref.shape[1]
    gain, shift = norm_ref[0:1, :], norm_ref[3:4, :]

    def chain(block):
        rows = slice(block * QB, (block + 1) * QB)
        dq = jnp.concatenate([dq0_ref[:, rows], dq1_ref[:, rows]], axis=0)
        back = dot(dq, w_ref[:, width : 2 * width], 0, 1)
        yield
        normed = n1_ref[rows, :]
        all_low[rows, :] = (normed * gain + shift).astype(BF16)
        dx1 = dh2_ref[rows, :] + back
        sum_norm[0:1, :] += column_sum(dx1 * normed)
        sum_norm[1:2, :] += column_sum(dx1)
        dh1 = norm_back(dx1, gain, normed, r1_ref[rows, :])
        dh_ref[rows, :] = dh1
        da = dh1.astype(BF16)
        all_da[rows, :] = da
        yield
        do_ref[:, rows] = dot(w_ref[:, 0:width], da, 1, 1).astype(BF16)

    pipeline([chain(block) for block in range(dh2_ref.shape[0] // QB)])
    me = info_ref[3]
    total = None
    for table in range(TABLES):
        image = image_ref[table * IMG : (table + 1) * IMG, :]
        grads = jnp.concatenate(
            [dk0_ref[table], dk1_ref[table], dv0_ref[table], dv1_ref[table]], axis=0
        )
        part = dot(image, grads, 0, 1)
        total = part if total is None else total + part
    sum_image[...] = total
    spread_blocks(me, sum_image, near_ref, far_ref, 2 * width)
    sum_inner[...] = dot(o_ref[...], all_da[...], 1, 0)
    spread_blocks(me, sum_inner, near_ref, far_ref, 0)
    dq = jnp.concatenate([dq0_ref[...], dq1_ref[...]], axis=0)
    sum_inner[...] = dot(all_low[...], dq, 0, 1)
    spread_blocks(me, sum_inner, near_ref, far_ref, width)
    dnorm_ref[...] = sum_norm[...]


def image_grad_kernel(info_ref, dk0_ref, dk1_ref, dv0_ref, dv1_ref, w_ref, out_ref):
    width = out_ref.shape[1]
    for table in range(TABLES):
        rows = slice(table * IMG, (table + 1) * IMG)
        grads = jnp.concatenate(
            [dk0_ref[table], dk1_ref[table], dv0_ref[table], dv1_ref[table]], axis=0
        )
        out_ref[rows, :] = dot(grads, w_ref[:, 2 * width : 4 * width], 0, 1)


def project_weight_kernel(
    info_ref, x_ref, dq0_ref, dq1_ref, dk0_ref, dk1_ref, dv0_ref, dv1_ref, inner_ref, feed_ref,
    near_ref, far_ref, total,
):
    width = x_ref.shape[1]
    refs = (dq0_ref, dq1_ref, dk0_ref, dk1_ref, dv0_ref, dv1_ref)
    grads = jnp.concatenate([ref[...] for ref in refs], axis=0)
    total[:, 0 : 3 * width] = dot(x_ref[...], grads, 0, 1)
    order = [inner_ref[0:1], feed_ref[1:2], feed_ref[2:3]]
    order += [inner_ref[1:2], feed_ref[4:5], feed_ref[5:6], jnp.zeros((122, width), F32)]
    total[:, 3 * width :] = jnp.transpose(jnp.concatenate(order, axis=0))
    spread_blocks(info_ref[3], total, near_ref, far_ref, 0)


def token_grad_kernel(
    info_ref, dq0_ref, dq1_ref, dk0_ref, dk1_ref, dv0_ref, dv1_ref, w_ref, dh_ref, out_ref
):
    width = dh_ref.shape[1]
    refs = (dq0_ref, dq1_ref, dk0_ref, dk1_ref, dv0_ref, dv1_ref)
    for block in range(dh_ref.shape[0] // QB):
        rows = slice(block * QB, (block + 1) * QB)
        grads = jnp.concatenate([ref[:, rows] for ref in refs], axis=0)
        out_ref[rows, :] = dh_ref[rows, :] + dot(grads, w_ref[:, 0 : 3 * width], 0, 1)


def lamb_moments(weight, grad, first, second, decay):
    first_new = BETA_FIRST * first + (1.0 - BETA_FIRST) * grad
    second_new = BETA_SECOND * second + (1.0 - BETA_SECOND) * grad * grad
    first_hat = first_new / (1.0 - BETA_FIRST**STEP)
    second_hat = second_new / (1.0 - BETA_SECOND**STEP)
    update = first_hat / (jnp.sqrt(second_hat) + ADAM_EPSILON) + decay * weight
    return (first_new, second_new, update)


def total_of(value):
    return jnp.sum(jnp.sum(value * value, axis=0, keepdims=True), axis=1, keepdims=True)


def moments_kernel(per, *refs):
    feed, inner, last = refs[0:per], refs[per : 2 * per], refs[2 * per : 3 * per]
    wa, wf, wn, ma, va, mf, vf, mn, vn = refs[3 * per : 3 * per + 9]
    ga, gf, gn, oma, ova, omf, ovf, omn, ovn, ua, uf, un, sums = refs[3 * per + 9 :]
    width, hidden = wa.shape[2], wf.shape[2]
    lane = lax.broadcasted_iota(jnp.int32, (1, 128), 1)
    weights = jnp.zeros((1, 128), F32)
    updates = jnp.zeros((1, 128), F32)

    def grad(pieces, col, size):
        cols = slice(col, col + size)
        near = [ref[:, cols].astype(F32) for ref in pieces]
        total = near[0]
        for part in near[1:]:
            total += part
        return total

    def tensor(slot, value, index, weight, first, second, outs, decay):
        nonlocal weights, updates
        first_new, second_new, update = lamb_moments(
            weight[index], value, first[index], second[index], decay
        )
        for ref, part in zip(outs, (value, first_new, second_new, update)):
            ref[index] = part
        weights = jnp.where(lane == slot, total_of(weight[index]), weights)
        updates = jnp.where(lane == slot, total_of(update), updates)

    for slot in range(8):
        pieces, col = (last, slot) if slot < 3 else (inner, slot - 3)
        if slot == 7:
            pieces, col = feed, 2 * hidden // width
        value = grad(pieces, col * width, width)
        tensor(slot, value, slot, wa, ma, va, (ga, oma, ova, ua), WEIGHT_DECAY)
    for slot in range(2):
        value = grad(feed, slot * hidden, hidden)
        tensor(8 + slot, value, slot, wf, mf, vf, (gf, omf, ovf, uf), WEIGHT_DECAY)
    norms = jnp.transpose(grad(last, 3 * width, 128))
    for slot in range(6):
        row = slice(slot, slot + 1)
        tensor(10 + slot, norms[row, :], row, wn, mn, vn, (gn, omn, ovn, un), 0.0)
    sums[...] = jnp.concatenate([weights, updates, jnp.zeros((6, 128), F32)], axis=0)


def apply_kernel(*refs):
    wa, wf, wn, ua, uf, un, na, nf, nn = refs[-10:-1]
    pieces, norms = refs[0:-10], refs[-1]
    total = pair_sum([ref[...] for ref in pieces])
    root = jnp.sqrt(total)
    norms[...] = root
    ratio = LEARN_RATE * (root[0:1, :] / root[1:2, :])
    for slot in range(8):
        na[slot] = wa[slot] - ratio[:, slot : slot + 1] * ua[slot]
    for slot in range(2):
        nf[slot] = wf[slot] - ratio[:, slot + 8 : slot + 9] * uf[slot]
    for slot in range(6):
        row = slice(slot, slot + 1)
        nn[row] = wn[row] - ratio[:, slot + 10 : slot + 11] * un[row]


def pair_sum(parts):
    while len(parts) > 1:
        parts = [parts[i] + parts[i + 1] for i in range(0, len(parts), 2)]
    return parts[0]


def shaped(*dims, kind=BF16):
    return jax.ShapeDtypeStruct(dims, kind)


def call(kernel, out_shape, operands, name, micros, info=True, scratch=(), mib=32):
    specs = []
    operands = list(operands)
    for position, operand in enumerate(operands):
        if info and position == 0:
            specs.append(SMEM)
        elif isinstance(operand, tuple):
            array, dims, index = operand
            operands[position] = array
            specs.append(
                pl.BlockSpec(
                    dims, lambda _, index=index: index, pipeline_mode=pl.Buffered(buffer_count=1)
                )
            )
        else:
            specs.append(VMEM)
    split = any(spec.block_shape is not None for spec in specs)
    return pl.pallas_call(
        kernel,
        grid=(1,) if split else (),
        out_shape=out_shape,
        in_specs=specs,
        out_specs=jax.tree.map(lambda _: VMEM, out_shape),
        scratch_shapes=[
            pltpu.VMEM(dims[:-1], BF16) if dims[-1] is BF16 else pltpu.VMEM(dims, F32)
            for dims in scratch
        ],
        compiler_params=pltpu.CompilerParams(vmem_limit_bytes=mib * 2**20),
        cost_estimate=pl.CostEstimate(
            flops=int(micros * 1.1e9), bytes_accessed=int(micros * 3.0e6), transcendentals=0
        ),
        name=name,
    )(*operands)


def device_index():
    return lax.axis_index("wide") * lax.axis_size("narrow") + lax.axis_index("narrow")


def device_count():
    return lax.axis_size("wide") * lax.axis_size("narrow")


def exchange_slot(k):
    return (k >> 3) * 4 + ((k >> 1) & 3)


def swap(value, mask):
    count = device_count()
    return lax.ppermute(value, AXES, [(i, i ^ mask) for i in range(count)])


def before(value, *others):
    return lax.optimization_barrier((value, others))[0]


def far_masks():
    return [k << 3 for k in range(1, device_count() >> 3)]


PLANE_MASKS = [2, 4, 6]


def gather_far(part):
    return jnp.stack([part] + [swap(part, mask) for mask in far_masks()])


def gather_plane(part):
    value = jnp.stack([part] + [swap(part, mask) for mask in PLANE_MASKS], axis=1)
    return value.reshape((-1,) + part.shape[1:])


def scatter_core(near, far):
    total = near.astype(F32) + swap(far, 1).astype(F32)
    total = total.reshape((-1, 4) + near.shape[1:])
    return [total[:, k] for k in range(4)]


def scatter_plane(parts):
    sends = [part.astype(BF16) for part in parts[1:]]
    return parts[0], sends


def scatter_plane_end(own, sends):
    total = own
    for mask, send in zip(PLANE_MASKS, sends):
        total = total + swap(send, mask).astype(F32)
    return total[0], [total[k].astype(BF16) for k in range(1, total.shape[0])]


def scatter_far_end(own, sends):
    return [own] + [swap(send, mask) for mask, send in zip(far_masks(), sends)]


def block_order():
    order = [0] * device_count()
    for k in range(device_count()):
        order[exchange_slot(k) + (k & 1) * (device_count() // 2)] = k
    return jnp.array(order, jnp.int32) ^ device_index()


def whole_blocks(near, far):
    if near.shape[1] % 16 == 0:
        return near, far
    blocks = jnp.concatenate([near, far])
    full = jnp.zeros_like(blocks).at[block_order()].set(blocks)
    return full.reshape(-1, near.shape[2]), jnp.zeros((16, 128), BF16)


def spread_shapes(shard, cols):
    if shard % 16 == 0:
        return [shaped(device_count() // 2, shard, cols)] * 2
    return [shaped(device_count() * shard, cols), shaped(16, 128)]


def split_blocks(near, far):
    if near.ndim == 3:
        return near, far
    blocks = near.reshape(device_count(), -1, near.shape[1])[block_order()]
    return blocks[: device_count() // 2], blocks[device_count() // 2 :]


def pack(stack):
    return jnp.swapaxes(stack, 0, 1).reshape(stack.shape[1], -1)


def local(
    tokens,
    image,
    segments,
    valid_len,
    cotangent,
    w_attn,
    w_ffn,
    norm_params,
    momentum_attn,
    variance_attn,
    momentum_ffn,
    variance_ffn,
    momentum_norm,
    variance_norm,
):
    tags, width = tokens.shape
    hidden_width = w_ffn.shape[2]
    shard = w_attn.shape[1]
    segment = segments[0]
    info = jnp.stack(
        [jnp.sum(segment < 1), jnp.sum(segment < 2), valid_len[0], device_index()]
    ).astype(jnp.int32)

    attn_low = w_attn.astype(BF16)
    norm_low = jnp.pad(norm_params.astype(BF16).T, ((0, 0), (0, 122)))
    first_part = jnp.concatenate([pack(attn_low[0:3]), norm_low], axis=1)
    first_far = gather_far(first_part)
    second_part = before(pack(attn_low[3:7]), first_far)
    first_plane = gather_plane(first_far)
    second_far = gather_far(second_part)
    first_core = swap(first_plane, 1)
    rest_part = before(
        jnp.concatenate([pack(attn_low[7:8]), pack(w_ffn.astype(BF16))], axis=1), first_plane
    )
    rest_full = lax.all_gather(rest_part, AXES, axis=0, tiled=True)
    second_plane = gather_plane(second_far)

    wide_shape = shaped(width, tags)
    half_shape = shaped(width // 2, tags)
    log_shape = shaped(HEADS, 1, tags, kind=F32)
    f32_rows = shaped(tags, width, kind=F32)
    w_first, norms, q, k, v = call(
        project_kernel,
        [shaped(width, 3 * width + 128), shaped(8, width, kind=F32)] + [wide_shape] * 3,
        (info, tokens, *whole_blocks(first_plane, first_core)),
        "project",
        3,
    )
    o, log_self = call(
        self_forward_kernel,
        [wide_shape, log_shape],
        (before(info, second_far), q, k, v),
        "self_forward",
        10,
        True,
        [(3 * QB, QB), (2, 3 * QB, QB), (2, 3 * QB, QB, BF16)],
        24,
    )
    second_core = swap(second_plane, 1)
    image_shape = shaped(TABLES, width, IMG)
    image_half = shaped(TABLES, width // 2, IMG)
    w_second, kc, vc = call(
        image_kernel,
        [shaped(width, 4 * width)] + [image_shape] * 2,
        (info, image, *whole_blocks(second_plane, second_core)),
        "image_project",
        6,
    )
    n1, r1, qc = call(
        mid_kernel,
        [f32_rows, shaped(tags, 1, kind=F32), wide_shape],
        (tokens, o, w_second, norms),
        "mid",
        5,
        False,
    )
    oc, log_cross = call(
        cross_forward_kernel,
        [wide_shape, log_shape],
        (info, qc, kc, vc),
        "cross_forward",
        18,
        True,
        [(2, IMG, QB), (2, IMG, QB, BF16)],
        24,
    )
    co = rest_full[:, 0:width]
    up = rest_full[:, width : width + hidden_width]
    down = rest_full[:, width + hidden_width :]
    feed_cols = 2 * hidden_width + width
    result, dh2, doc, feed_near, feed_far, norm_feed = call(
        feed_kernel,
        [
            shaped(tags, width),
            f32_rows,
            wide_shape,
            *spread_shapes(shard, feed_cols),
            shaped(8, width, kind=F32),
        ],
        (info, oc, n1, cotangent, co, up, down, norms),
        "feed",
        15,
        True,
        [(width, hidden_width), (width, width), (8, width), (tags, width, BF16)]
        + [(tags, hidden_width, BF16)] * 2
        + [(tags, width, BF16)] * 2,
        40,
    )

    def half(array, index):
        axis = 1 if array.shape[0] == TABLES else 0
        dims = tuple(size // 2 if i == axis else size for i, size in enumerate(array.shape))
        return array, dims, tuple(index if i == axis else 0 for i in range(len(dims)))

    def cross_backward(index, *deps):
        parts = [half(array, index) for array in (qc, kc, vc, oc, log_cross, doc)]
        return call(
            cross_backward_kernel,
            [half_shape, image_half, image_half],
            [before(info, *deps)] + parts,
            "cross_backward",
            16,
            True,
            [(TABLES, width // 2, IMG)] * 2 + [(2, IMG, QB)] * 2 + [(2, IMG, QB, BF16)] * 2,
        )

    def self_backward(index, *deps):
        parts = [half(array, index) for array in (q, k, v, o, log_self, do)]
        return call(
            self_backward_kernel,
            [half_shape] * 3,
            [before(info, *deps)] + parts,
            "self_backward",
            8,
            True,
            [(width // 2, tags)] * 2
            + [(3 * QB, QB)]
            + [(2, 3 * QB, QB)] * 2
            + [(2, 3 * QB, QB, BF16)] * 2,
            24,
        )

    feed_near, feed_far = split_blocks(feed_near, feed_far)
    dqc0, dkc0, dvc0 = cross_backward(0)
    feed_near = before(feed_near, dqc0)
    own_feed, send_feed = scatter_plane(scatter_core(feed_near, feed_far))
    dqc1, dkc1, dvc1 = cross_backward(1, send_feed)
    own_feed = before(own_feed, dqc1)
    own_feed, send_feed = scatter_plane_end(own_feed, send_feed)
    dh1, do, inner_near, inner_far, norm_inner = call(
        inner_kernel,
        [
            f32_rows,
            wide_shape,
            *spread_shapes(shard, 4 * width),
            shaped(8, width, kind=F32),
        ],
        (before(info, send_feed), dqc0, dqc1, dh2, n1, r1, o, w_second, norms)
        + (image, dkc0, dkc1, dvc0, dvc1),
        "inner",
        10,
        True,
        [(width, 2 * width), (width, width), (8, width)] + [(tags, width, BF16)] * 2,
        36,
    )
    inner_near, inner_far = split_blocks(inner_near, inner_far)
    pieces_feed = scatter_far_end(own_feed, send_feed)
    dq0, dk0, dv0 = self_backward(0)
    inner_near = before(inner_near, dq0)
    own_inner, send_inner = scatter_plane(scatter_core(inner_near, inner_far))
    dq1, dk1, dv1 = self_backward(1, send_inner)
    grads = (dq0, dq1, dk0, dk1, dv0, dv1)
    last_cols = 3 * width + 128
    last_near, last_far = call(
        project_weight_kernel,
        spread_shapes(shard, last_cols),
        (info, tokens) + grads + (norm_inner, norm_feed),
        "project_weight",
        3,
        True,
        [(width, last_cols)],
    )
    last_near, last_far = split_blocks(last_near, last_far)
    own_inner, send_inner = scatter_plane_end(before(own_inner, dq1), send_inner)
    image_grad = call(
        image_grad_kernel,
        shaped(image.shape[0], width, kind=F32),
        (before(info, last_far, send_inner), dkc0, dkc1, dvc0, dvc1, w_second),
        "image_grad",
        7,
    )
    own_last, send_last = scatter_plane(scatter_core(before(last_near, image_grad), last_far))
    token_grad = call(
        token_grad_kernel,
        f32_rows,
        (before(info, send_last),) + grads + (w_first, dh1),
        "token_grad",
        5,
    )
    pieces_inner = scatter_far_end(own_inner, send_inner)
    own_last, send_last = scatter_plane_end(before(own_last, token_grad), send_last)
    pieces_last = scatter_far_end(own_last, send_last)

    weights = (w_attn, w_ffn, norm_params)
    moments = (momentum_attn, variance_attn, momentum_ffn, variance_ffn)
    moments = moments + (momentum_norm, variance_norm)
    like = [shaped(*array.shape, kind=F32) for array in weights + moments + weights]
    pieces = [*pieces_feed, *pieces_inner, *pieces_last]
    per_chunk = len(pieces) // 3
    outs = call(
        lambda *refs: moments_kernel(per_chunk, *refs),
        like + [shaped(8, 128, kind=F32)],
        (*pieces, *weights, *moments),
        "moments",
        3,
        False,
    )
    grad_attn, grad_ffn, grad_norm = outs[0:3]
    first_attn, second_attn, first_ffn, second_ffn, first_norm, second_norm = outs[3:9]
    sums = outs[12]
    sums = sums + swap(sums, 1)
    sums = pair_sum([sums] + [swap(sums, mask) for mask in PLANE_MASKS])
    pieces = [sums] + [swap(sums, mask) for mask in far_masks()]
    new_attn, new_ffn, new_norm, norms_both = call(
        apply_kernel,
        like[0:3] + [shaped(8, 128, kind=F32)],
        (*pieces, *weights, *outs[9:12]),
        "apply",
        2,
        False,
    )
    weight_norms = norms_both[0, 0:16]
    update_norms = norms_both[1, 0:16]
    return (
        result,
        token_grad,
        image_grad,
        grad_attn,
        grad_ffn,
        grad_norm,
        new_attn,
        new_ffn,
        new_norm,
        first_attn,
        second_attn,
        first_ffn,
        second_ffn,
        first_norm,
        second_norm,
        weight_norms,
        update_norms,
    )


def solution(mesh):
    rows = P(AXES, None)
    stack = P(None, AXES, None)
    flat = P(None, AXES)
    in_specs = (rows, rows, rows, P(AXES), rows) + (stack, stack, flat)
    in_specs = in_specs + (stack, stack, stack, stack, flat, flat)
    out_specs = (rows, rows, rows, stack, stack, flat, stack, stack, flat)
    out_specs = out_specs + (stack, stack, stack, stack, flat, flat, P(), P())
    return jax.shard_map(local, mesh=mesh, in_specs=in_specs, out_specs=out_specs, check_vma=False)
```

```python
import functools

import jax
import jax.numpy as jnp
from jax import lax
from jax.experimental import pallas as pl
from jax.experimental.pallas import tpu as pltpu
from jax.sharding import PartitionSpec as P

HD = 64
HEADS = 8
IMG = 784
TABLES = 3
STEP = 10
QB = 256

MASKED_SCORE = -1000000000.0
BETA_FIRST = 0.9
BETA_SECOND = 0.999
LEARN_RATE = 0.3
WEIGHT_DECAY = 0.01
ADAM_EPSILON = 1e-06
NORM_EPSILON = 1e-05

VMEM_GRANT = 28 * 2**20

AXES = ("wide", "narrow")
F32 = jnp.float32
BF16 = jnp.bfloat16
VMEM = pl.BlockSpec(memory_space=pltpu.VMEM)
SMEM = pl.BlockSpec(memory_space=pltpu.SMEM)


def dot(left, right, left_dim, right_dim):
    return lax.dot_general(
        left, right, (((left_dim,), (right_dim,)), ((), ())), preferred_element_type=F32
    )


def normalise(hidden):
    centre = hidden - jnp.mean(hidden, axis=-1, keepdims=True)
    scale = lax.rsqrt(jnp.mean(centre * centre, axis=-1, keepdims=True) + NORM_EPSILON)
    return centre * scale, scale


def norm_back(grad, gain, normed, scale):
    inner = grad * gain
    return scale * (
        inner
        - jnp.mean(inner, axis=-1, keepdims=True)
        - normed * jnp.mean(inner * normed, axis=-1, keepdims=True)
    )


def column_sum(value):
    return jnp.sum(value, axis=0, keepdims=True)


def pipeline(chains):
    done = object()
    live = []
    waiting = list(chains)
    while live or waiting:
        if waiting:
            live.insert(0, waiting.pop(0))
        live = [chain for chain in live if next(chain, done) is not done]


def place_blocks(me, near_ref, far_ref, out_ref):
    if near_ref.shape == out_ref.shape:
        out_ref[...] = near_ref[...]
        return
    size = near_ref.shape[1]
    for k in range(2 * near_ref.shape[0]):
        ref = far_ref if k & 1 else near_ref
        row = pl.multiple_of((me ^ k) * size, size)
        out_ref[pl.ds(row, size), :] = ref[exchange_slot(k)]


def spread_blocks(me, source, near_ref, far_ref, col):
    cols = slice(col, col + source.shape[1])
    if near_ref.shape[0] == source.shape[0]:
        near_ref[:, cols] = source[...].astype(BF16)
        far_ref[...] = jnp.zeros(far_ref.shape, BF16)
        return
    size = near_ref.shape[1]
    for k in range(2 * near_ref.shape[0]):
        ref = far_ref if k & 1 else near_ref
        row = pl.multiple_of((me ^ k) * size, size)
        ref[exchange_slot(k), :, cols] = source[pl.ds(row, size), :].astype(BF16)


def pack_kernel(wa_ref, wf_ref, wn_ref, first_ref, second_ref, rest_ref):
    width, hidden = wa_ref.shape[2], wf_ref.shape[2]
    for slot in range(3):
        first_ref[:, slot * width : (slot + 1) * width] = wa_ref[slot].astype(BF16)
    rows = [wn_ref[...], jnp.zeros((128 - wn_ref.shape[0], wn_ref.shape[1]), F32)]
    first_ref[:, 3 * width :] = jnp.transpose(jnp.concatenate(rows, axis=0)).astype(BF16)
    for slot in range(4):
        second_ref[:, slot * width : (slot + 1) * width] = wa_ref[slot + 3].astype(BF16)
    rest_ref[:, 0:width] = wa_ref[7].astype(BF16)
    for slot in range(2):
        begin = width + slot * hidden
        rest_ref[:, begin : begin + hidden] = wf_ref[slot].astype(BF16)


def project_kernel(info_ref, x_ref, near_ref, far_ref, norm_ref, q_ref, k_ref, v_ref, w_ref):
    place_blocks(info_ref[3], near_ref, far_ref, w_ref)
    width = x_ref.shape[1]
    norm_ref[...] = jnp.transpose(w_ref[:, 3 * width :].astype(F32))[0:8, :]
    for block in range(x_ref.shape[0] // QB):
        cols = slice(block * QB, (block + 1) * QB)
        x = x_ref[cols, :]
        q_ref[:, cols] = (dot(w_ref[:, 0:width], x, 0, 1).astype(BF16) * 0.125).astype(BF16)
        k_ref[:, cols] = dot(w_ref[:, width : 2 * width], x, 0, 1).astype(BF16)
        v_ref[:, cols] = dot(w_ref[:, 2 * width : 3 * width], x, 0, 1).astype(BF16)


def head_rows(index):
    return slice(index * HD, (index + 1) * HD)


def forward_heads(query, key, value, finish, heads, count, bias, score_ref, prob_ref):
    def chain(index):
        slot = index % 2
        scores = dot(key(index), query(index), 0, 0)
        score_ref[slot, 0:count] = scores if bias is None else scores + bias[0:count]
        yield
        scores = score_ref[slot, 0:count]
        highest = jnp.max(scores, axis=0, keepdims=True)
        prob_ref[slot, 0:count] = jnp.exp(scores - highest).astype(BF16)
        yield
        ones = jnp.ones((16, count), BF16)
        mixed = dot(jnp.concatenate([value(index), ones], axis=0), prob_ref[slot, 0:count], 1, 0)
        total = mixed[HD : HD + 1]
        finish(index, (mixed[0:HD] / total).astype(BF16), highest + jnp.log(total))

    pipeline([chain(index) for index in range(heads)])


def backward_heads(
    query, key, value, grad, mixed, logs, finish, heads, count, bias,
    score_ref, level_ref, prob_ref, delta_ref,
):
    def chain(index):
        slot = index % 2
        scores = dot(key(index), query(index), 0, 0)
        score_ref[slot, 0:count] = scores if bias is None else scores + bias[0:count]
        level_ref[slot, 0:count] = dot(value(index), grad(index), 0, 0)
        yield
        level = column_sum(grad(index).astype(F32) * mixed(index).astype(F32))
        probs = jnp.exp(score_ref[slot, 0:count] - logs(index))
        prob_ref[slot, 0:count] = probs.astype(BF16)
        delta_ref[slot, 0:count] = (probs * (level_ref[slot, 0:count] - level)).astype(BF16)
        yield
        delta = delta_ref[slot, 0:count]
        finish(
            index,
            (dot(key(index), delta, 1, 0) * 0.125).astype(BF16),
            dot(query(index), delta, 1, 1),
            dot(grad(index), prob_ref[slot, 0:count], 1, 1),
        )

    pipeline([chain(index) for index in range(heads)])


def self_blocks(info_ref, rows, bias, run):
    second, third, valid = info_ref[0], info_ref[1], info_ref[2]

    def step(block, carry):
        start = block * QB
        first = jnp.where(start < second, 0, jnp.where(start < third, second, third))
        back = block - first // QB
        for extent in range(3):

            @pl.when(back == extent)
            def _():
                begin = (block - extent) * QB
                count = (extent + 1) * QB
                place = start + lax.broadcasted_iota(jnp.int32, (1, QB), 1)
                low = jnp.where(place < second, 0, jnp.where(place < third, second, third))
                high = jnp.minimum(place, valid - 1)
                key = begin + lax.broadcasted_iota(jnp.int32, (count, QB), 0)
                allowed = (key >= low) & ((key <= high) | (key == place))
                bias[0:count] = jnp.where(allowed, 0.0, MASKED_SCORE)
                run(
                    pl.ds(pl.multiple_of(start, QB), QB),
                    pl.ds(pl.multiple_of(begin, QB), count),
                    count,
                )

        return carry

    lax.fori_loop(0, rows // QB, step, 0)


def self_forward_kernel(
    base, info_ref, q_ref, k_ref, v_ref, o_ref, log_ref, bias_ref, score_ref, prob_ref
):
    def run(cols, keys, count):
        def finish(index, mixed, logs):
            o_ref[head_rows(index), cols] = mixed
            log_ref[index, :, cols] = logs

        forward_heads(
            lambda index: q_ref[head_rows(base + index), cols],
            lambda index: k_ref[head_rows(base + index), keys],
            lambda index: v_ref[head_rows(base + index), keys],
            finish, o_ref.shape[0] // HD, count, bias_ref, score_ref, prob_ref,
        )

    self_blocks(info_ref, q_ref.shape[1], bias_ref, run)


def self_backward_kernel(
    base, info_ref, q_ref, k_ref, v_ref, o_ref, log_ref, do_ref, dq_ref, dk_ref, dv_ref,
    sum_k, sum_v, bias_ref, score_ref, level_ref, prob_ref, delta_ref,
):
    sum_k[...] = jnp.zeros(sum_k.shape, F32)
    sum_v[...] = jnp.zeros(sum_v.shape, F32)

    def run(cols, keys, count):
        def finish(index, grad_query, grad_key, grad_value):
            dq_ref[head_rows(index), cols] = grad_query
            sum_k[head_rows(index), keys] += grad_key
            sum_v[head_rows(index), keys] += grad_value

        backward_heads(
            lambda index: q_ref[head_rows(base + index), cols],
            lambda index: k_ref[head_rows(base + index), keys],
            lambda index: v_ref[head_rows(base + index), keys],
            lambda index: do_ref[head_rows(base + index), cols],
            lambda index: o_ref[head_rows(base + index), cols],
            lambda index: log_ref[base + index, :, cols],
            finish, dq_ref.shape[0] // HD, count, bias_ref,
            score_ref, level_ref, prob_ref, delta_ref,
        )

    self_blocks(info_ref, q_ref.shape[1], bias_ref, run)
    dk_ref[...] = sum_k[...].astype(BF16)
    dv_ref[...] = sum_v[...].astype(BF16)


def mid_kernel(x_ref, o_ref, w_ref, norm_ref, n_ref, r_ref, q_ref):
    gain, shift = norm_ref[0:1, :], norm_ref[3:4, :]
    width = x_ref.shape[1]

    def chain(block):
        rows = slice(block * QB, (block + 1) * QB)
        branch = dot(o_ref[:, rows], w_ref[:, 0:width], 0, 0)
        yield
        normed, scale = normalise(x_ref[rows, :].astype(F32) + branch)
        n_ref[rows, :] = normed
        r_ref[:, rows] = jnp.transpose(jnp.broadcast_to(scale, (QB, 128)))[0:8]
        low = (normed * gain + shift).astype(BF16)
        yield
        query = dot(w_ref[:, width : 2 * width], low, 0, 1).astype(BF16)
        q_ref[:, rows] = (query * 0.125).astype(BF16)

    pipeline([chain(block) for block in range(x_ref.shape[0] // QB)])


def image_kernel(info_ref, image_ref, near_ref, far_ref, w_ref, k_ref, v_ref):
    place_blocks(info_ref[3], near_ref, far_ref, w_ref)
    width = image_ref.shape[1]
    for table in range(TABLES):
        image = image_ref[table * IMG : (table + 1) * IMG, :]
        k_ref[table] = dot(w_ref[:, 2 * width : 3 * width], image, 0, 1).astype(BF16)
        v_ref[table] = dot(w_ref[:, 3 * width : 4 * width], image, 0, 1).astype(BF16)


def cross_blocks(info_ref, rows, run):
    def pair(index, carry):
        block = index // TABLES
        table = index % TABLES
        second, third = info_ref[0], info_ref[1]
        begin = jnp.where(table == 0, 0, jnp.where(table == 1, second, third))
        end = jnp.where(table == 0, second, jnp.where(table == 1, third, rows))
        start = block * QB

        @pl.when(jnp.logical_and(begin < start + QB, end > start))
        def _():
            place = start + lax.broadcasted_iota(jnp.int32, (1, QB), 1)
            run(pl.ds(pl.multiple_of(start, QB), QB), table, (place >= begin) & (place < end))

        return carry

    lax.fori_loop(0, rows // QB * TABLES, pair, 0)


def cross_forward_kernel(info_ref, q_ref, k_ref, v_ref, o_ref, log_ref, score_ref, prob_ref):
    def run(cols, table, here):
        def finish(index, mixed, logs):
            rows = head_rows(index)
            o_ref[rows, cols] = jnp.where(here, mixed, o_ref[rows, cols])
            log_ref[index, :, cols] = jnp.where(here, logs, log_ref[index, :, cols])

        forward_heads(
            lambda index: q_ref[head_rows(index), cols],
            lambda index: k_ref[table, head_rows(index), :],
            lambda index: v_ref[table, head_rows(index), :],
            finish, q_ref.shape[0] // HD, IMG, None, score_ref, prob_ref,
        )

    cross_blocks(info_ref, q_ref.shape[1], run)


def cross_backward_kernel(
    base, info_ref, q_ref, k_ref, v_ref, o_ref, log_ref, do_ref, dq_ref, dk_ref, dv_ref,
    sum_k, sum_v, score_ref, level_ref, prob_ref, delta_ref,
):
    sum_k[...] = jnp.zeros(sum_k.shape, F32)
    sum_v[...] = jnp.zeros(sum_v.shape, F32)

    def run(cols, table, here):
        def finish(index, grad_query, grad_key, grad_value):
            rows = head_rows(index)
            dq_ref[rows, cols] = jnp.where(here, grad_query, dq_ref[rows, cols])
            sum_k[table, rows, :] += grad_key
            sum_v[table, rows, :] += grad_value

        zero = jnp.zeros((), BF16)
        backward_heads(
            lambda index: q_ref[head_rows(base + index), cols],
            lambda index: k_ref[table, head_rows(base + index), :],
            lambda index: v_ref[table, head_rows(base + index), :],
            lambda index: jnp.where(here, do_ref[head_rows(base + index), cols], zero),
            lambda index: o_ref[head_rows(base + index), cols],
            lambda index: jnp.where(here, log_ref[base + index, :, cols], -MASKED_SCORE),
            finish, dq_ref.shape[0] // HD, IMG, None,
            score_ref, level_ref, prob_ref, delta_ref,
        )

    cross_blocks(info_ref, q_ref.shape[1], run)
    dk_ref[...] = sum_k[...].astype(BF16)
    dv_ref[...] = sum_v[...].astype(BF16)


def feed_kernel(
    info_ref, o_ref, n1_ref, cot_ref, w_ref, norm_ref,
    result_ref, dh_ref, do_ref, near_ref, far_ref, dnorm_ref,
    sum_up, sum_out, sum_norm, all_x2, all_active, all_du, all_dz, all_dac,
):
    valid = info_ref[2]
    width = cot_ref.shape[1]
    hidden_width = (w_ref.shape[1] - width) // 2
    co_ref = w_ref.at[:, 0:width]
    up_ref = w_ref.at[:, width : width + hidden_width]
    down_ref = w_ref.at[:, width + hidden_width :]
    sum_norm[...] = jnp.zeros(sum_norm.shape, F32)
    root = 0.7978845608028654

    def chain(block):
        rows = slice(block * QB, (block + 1) * QB)
        branch = dot(o_ref[:, rows], co_ref[...], 0, 0)
        yield
        first = n1_ref[rows, :] * norm_ref[0:1, :] + norm_ref[3:4, :]
        n2, r2 = normalise(first + branch)
        x2 = n2 * norm_ref[1:2, :] + norm_ref[4:5, :]
        x2_low = x2.astype(BF16)
        all_x2[rows, :] = x2_low
        yield
        u = dot(x2_low, up_ref[...], 1, 0)
        yield
        square = u * u
        curve = jnp.tanh(root * u * (1.0 + 0.044715 * square))
        half = 0.5 * (1.0 + curve)
        active = (u * half).astype(BF16)
        slope = half + 0.5 * u * (1.0 - curve * curve) * (root * (1.0 + 3 * 0.044715 * square))
        all_active[rows, :] = active
        yield
        down = dot(active, down_ref[...], 1, 1)
        yield
        n3, r3 = normalise(x2 + down)
        result_ref[rows, :] = (n3 * norm_ref[2:3, :] + norm_ref[5:6, :]).astype(BF16)
        place = block * QB + lax.broadcasted_iota(jnp.int32, (QB, 1), 0)
        dy = jnp.where(place < valid, cot_ref[rows, :].astype(F32), 0.0)
        sum_norm[2:3, :] += column_sum(dy * n3)
        sum_norm[5:6, :] += column_sum(dy)
        dh3 = norm_back(dy, norm_ref[2:3, :], n3, r3)
        dz = dh3.astype(BF16)
        all_dz[rows, :] = dz
        yield
        df = dot(dz, down_ref[...], 1, 0)
        yield
        du = (df * slope).astype(BF16)
        all_du[rows, :] = du
        yield
        back = dot(du, up_ref[...], 1, 1)
        yield
        dx2 = dh3 + back
        sum_norm[1:2, :] += column_sum(dx2 * n2)
        sum_norm[4:5, :] += column_sum(dx2)
        dh2 = norm_back(dx2, norm_ref[1:2, :], n2, r2)
        dh_ref[rows, :] = dh2
        dac = dh2.astype(BF16)
        all_dac[rows, :] = dac
        yield
        do_ref[:, rows] = dot(co_ref[...], dac, 1, 1).astype(BF16)

    pipeline([chain(block) for block in range(cot_ref.shape[0] // QB)])
    me = info_ref[3]
    sum_up[...] = dot(all_x2[...], all_du[...], 0, 0)
    spread_blocks(me, sum_up, near_ref, far_ref, 0)
    sum_up[...] = dot(all_dz[...], all_active[...], 0, 0)
    spread_blocks(me, sum_up, near_ref, far_ref, hidden_width)
    sum_out[...] = dot(o_ref[...], all_dac[...], 1, 0)
    spread_blocks(me, sum_out, near_ref, far_ref, 2 * hidden_width)
    dnorm_ref[...] = sum_norm[...]


def inner_kernel(
    info_ref, dq0_ref, dq1_ref, dh2_ref, n1_ref, r1_ref, o_ref, wnear_ref, wfar_ref,
    norm_ref, image_ref, dk0_ref, dk1_ref, dv0_ref, dv1_ref,
    dh_ref, do_ref, near_ref, far_ref, dnorm_ref,
    sum_image, sum_inner, sum_norm, all_low, all_da, w_ref,
):
    place_blocks(info_ref[3], wnear_ref, wfar_ref, w_ref)
    sum_norm[...] = jnp.zeros(sum_norm.shape, F32)
    width = dh_ref.shape[1]
    gain, shift = norm_ref[0:1, :], norm_ref[3:4, :]

    def chain(block):
        rows = slice(block * QB, (block + 1) * QB)
        dq = jnp.concatenate([dq0_ref[:, rows], dq1_ref[:, rows]], axis=0)
        back = dot(dq, w_ref[:, width : 2 * width], 0, 1)
        yield
        normed = n1_ref[rows, :]
        all_low[rows, :] = (normed * gain + shift).astype(BF16)
        dx1 = dh2_ref[rows, :] + back
        sum_norm[0:1, :] += column_sum(dx1 * normed)
        sum_norm[1:2, :] += column_sum(dx1)
        dh1 = norm_back(dx1, gain, normed, jnp.transpose(jnp.broadcast_to(r1_ref[0:1, rows], (128, QB)))[:, 0:1])
        dh_ref[rows, :] = dh1
        da = dh1.astype(BF16)
        all_da[rows, :] = da
        yield
        do_ref[:, rows] = dot(w_ref[:, 0:width], da, 1, 1).astype(BF16)

    pipeline([chain(block) for block in range(dh2_ref.shape[0] // QB)])
    me = info_ref[3]
    total = None
    for table in range(TABLES):
        image = image_ref[table * IMG : (table + 1) * IMG, :]
        grads = jnp.concatenate(
            [dk0_ref[table], dk1_ref[table], dv0_ref[table], dv1_ref[table]], axis=0
        )
        part = dot(image, grads, 0, 1)
        total = part if total is None else total + part
    sum_image[...] = total
    spread_blocks(me, sum_image, near_ref, far_ref, 2 * width)
    sum_inner[...] = dot(o_ref[...], all_da[...], 1, 0)
    spread_blocks(me, sum_inner, near_ref, far_ref, 0)
    dq = jnp.concatenate([dq0_ref[...], dq1_ref[...]], axis=0)
    sum_inner[...] = dot(all_low[...], dq, 0, 1)
    spread_blocks(me, sum_inner, near_ref, far_ref, width)
    dnorm_ref[...] = sum_norm[...]


def image_grad_kernel(
    info_ref, dk0_ref, dk1_ref, dv0_ref, dv1_ref, near_ref, far_ref, out_ref, w_ref
):
    place_blocks(info_ref[3], near_ref, far_ref, w_ref)
    width = out_ref.shape[1]
    for table in range(TABLES):
        rows = slice(table * IMG, (table + 1) * IMG)
        grads = jnp.concatenate(
            [dk0_ref[table], dk1_ref[table], dv0_ref[table], dv1_ref[table]], axis=0
        )
        out_ref[rows, :] = dot(grads, w_ref[:, 2 * width : 4 * width], 0, 1)


def project_weight_kernel(
    info_ref, x_ref, dq0_ref, dq1_ref, dk0_ref, dk1_ref, dv0_ref, dv1_ref, inner_ref, feed_ref,
    near_ref, far_ref, total,
):
    width = x_ref.shape[1]
    refs = (dq0_ref, dq1_ref, dk0_ref, dk1_ref, dv0_ref, dv1_ref)
    grads = jnp.concatenate([ref[...] for ref in refs], axis=0)
    total[:, 0 : 3 * width] = dot(x_ref[...], grads, 0, 1)
    order = [inner_ref[0:1], feed_ref[1:2], feed_ref[2:3]]
    order += [inner_ref[1:2], feed_ref[4:5], feed_ref[5:6], jnp.zeros((122, width), F32)]
    total[:, 3 * width :] = jnp.transpose(jnp.concatenate(order, axis=0))
    spread_blocks(info_ref[3], total, near_ref, far_ref, 0)


def token_grad_kernel(
    info_ref, dq0_ref, dq1_ref, dk0_ref, dk1_ref, dv0_ref, dv1_ref, near_ref, far_ref, dh_ref,
    out_ref, w_ref,
):
    place_blocks(info_ref[3], near_ref, far_ref, w_ref)
    width = dh_ref.shape[1]
    refs = (dq0_ref, dq1_ref, dk0_ref, dk1_ref, dv0_ref, dv1_ref)
    for block in range(dh_ref.shape[0] // QB):
        rows = slice(block * QB, (block + 1) * QB)
        grads = jnp.concatenate([ref[:, rows] for ref in refs], axis=0)
        out_ref[rows, :] = dh_ref[rows, :] + dot(grads, w_ref[:, 0 : 3 * width], 0, 1)


def lamb_moments(weight, grad, first, second, decay):
    first_new = BETA_FIRST * first + (1.0 - BETA_FIRST) * grad
    second_new = BETA_SECOND * second + (1.0 - BETA_SECOND) * grad * grad
    first_hat = first_new / (1.0 - BETA_FIRST**STEP)
    second_hat = second_new / (1.0 - BETA_SECOND**STEP)
    update = first_hat / (jnp.sqrt(second_hat) + ADAM_EPSILON) + decay * weight
    return (first_new, second_new, update)


def total_of(value):
    return jnp.sum(jnp.sum(value * value, axis=0, keepdims=True), axis=1, keepdims=True)


def moments_kernel(per, *refs):
    both, last = refs[0:per], refs[per : 2 * per]
    wa, wf, wn, ma, va, mf, vf, mn, vn = refs[2 * per : 2 * per + 9]
    ga, gf, gn, oma, ova, omf, ovf, omn, ovn, ua, uf, un, sums = refs[2 * per + 9 :]
    width, hidden = wa.shape[2], wf.shape[2]
    lane = lax.broadcasted_iota(jnp.int32, (1, 128), 1)
    weights = jnp.zeros((1, 128), F32)
    updates = jnp.zeros((1, 128), F32)

    def grad(pieces, col, size):
        cols = slice(col, col + size)
        near = [ref[:, cols].astype(F32) for ref in pieces]
        total = near[0]
        for part in near[1:]:
            total += part
        return total

    def tensor(slot, value, index, weight, first, second, outs, decay):
        nonlocal weights, updates
        first_new, second_new, update = lamb_moments(
            weight[index], value, first[index], second[index], decay
        )
        for ref, part in zip(outs, (value, first_new, second_new, update)):
            ref[index] = part
        weights = jnp.where(lane == slot, total_of(weight[index]), weights)
        updates = jnp.where(lane == slot, total_of(update), updates)

    for slot in range(8):
        pieces, col = (last, slot) if slot < 3 else (both, 2 * hidden // width + slot - 2)
        if slot == 7:
            pieces, col = both, 2 * hidden // width
        value = grad(pieces, col * width, width)
        tensor(slot, value, slot, wa, ma, va, (ga, oma, ova, ua), WEIGHT_DECAY)
    for slot in range(2):
        value = grad(both, slot * hidden, hidden)
        tensor(8 + slot, value, slot, wf, mf, vf, (gf, omf, ovf, uf), WEIGHT_DECAY)
    norms = jnp.transpose(grad(last, 3 * width, 128))
    for slot in range(6):
        row = slice(slot, slot + 1)
        tensor(10 + slot, norms[row, :], row, wn, mn, vn, (gn, omn, ovn, un), 0.0)
    sums[...] = jnp.concatenate([weights, updates, jnp.zeros((6, 128), F32)], axis=0)


def apply_kernel(*refs):
    wa, wf, wn, ua, uf, un, na, nf, nn = refs[-10:-1]
    pieces, norms = refs[0:-10], refs[-1]
    total = pair_sum([ref[...] for ref in pieces])
    root = jnp.sqrt(total)
    norms[...] = root
    ratio = LEARN_RATE * (root[0:1, :] / root[1:2, :])
    for slot in range(8):
        na[slot] = wa[slot] - ratio[:, slot : slot + 1] * ua[slot]
    for slot in range(2):
        nf[slot] = wf[slot] - ratio[:, slot + 8 : slot + 9] * uf[slot]
    for slot in range(6):
        row = slice(slot, slot + 1)
        nn[row] = wn[row] - ratio[:, slot + 10 : slot + 11] * un[row]


def pair_sum(parts):
    while len(parts) > 1:
        parts = [parts[i] + parts[i + 1] for i in range(0, len(parts), 2)]
    return parts[0]


def shaped(*dims, kind=BF16):
    return jax.ShapeDtypeStruct(dims, kind)


def call(kernel, out_shape, operands, name, micros, info=True, scratch=(), grant=VMEM_GRANT):
    specs = [VMEM] * len(operands)
    if info:
        specs[0] = SMEM
    return pl.pallas_call(
        kernel,
        out_shape=out_shape,
        in_specs=specs,
        out_specs=jax.tree.map(lambda _: VMEM, out_shape),
        scratch_shapes=[
            pltpu.VMEM(dims[:-1], BF16) if dims[-1] is BF16 else pltpu.VMEM(dims, F32)
            for dims in scratch
        ],
        compiler_params=pltpu.CompilerParams(vmem_limit_bytes=grant),
        cost_estimate=pl.CostEstimate(
            flops=int(micros * 0.02e9), bytes_accessed=0, transcendentals=0
        ),
        name=name,
    )(*operands)


def device_index():
    return lax.axis_index("wide") * lax.axis_size("narrow") + lax.axis_index("narrow")


def device_count():
    return lax.axis_size("wide") * lax.axis_size("narrow")


def exchange_slot(k):
    return (k >> 3) * 4 + ((k >> 1) & 3)


def swap(value, mask):
    count = device_count()
    return lax.ppermute(value, AXES, [(i, i ^ mask) for i in range(count)])


def before(value, *others):
    return lax.optimization_barrier((value, others))[0]


def far_masks():
    return [k << 3 for k in range(1, device_count() >> 3)]


PLANE_MASKS = [2, 4, 6]


def gather_far(part):
    return jnp.stack([part] + [swap(part, mask) for mask in far_masks()])


def join_plane(parts):
    return jnp.stack(parts, axis=1).reshape((-1,) + parts[0].shape[1:])


def scatter_core(near, far):
    total = near.astype(F32) + swap(far, 1).astype(F32)
    total = total.reshape((-1, 4) + near.shape[1:])
    return [total[:, k] for k in range(4)]


def scatter_plane(parts):
    sends = [part.astype(BF16) for part in parts[1:]]
    return parts[0], sends


def scatter_plane_end(own, sends):
    total = own
    for mask, send in zip(PLANE_MASKS, sends):
        total = total + swap(send, mask).astype(F32)
    return total[0], [total[k].astype(BF16) for k in range(1, total.shape[0])]


def scatter_far_end(own, sends):
    return [own] + [swap(send, mask) for mask, send in zip(far_masks(), sends)]


def block_order():
    order = [0] * device_count()
    for k in range(device_count()):
        order[exchange_slot(k) + (k & 1) * (device_count() // 2)] = k
    return jnp.array(order, jnp.int32) ^ device_index()


def whole_blocks(near, far):
    if near.shape[1] % 16 == 0:
        return near, far
    blocks = jnp.concatenate([near, far])
    full = jnp.zeros_like(blocks).at[block_order()].set(blocks)
    return full.reshape(-1, near.shape[2]), jnp.zeros((16, 128), BF16)


def spread_shapes(shard, cols):
    if shard % 16 == 0:
        return [shaped(device_count() // 2, shard, cols)] * 2
    return [shaped(device_count() * shard, cols), shaped(16, 128)]


def split_blocks(near, far):
    if near.ndim == 3:
        return near, far
    blocks = near.reshape(device_count(), -1, near.shape[1])[block_order()]
    return blocks[: device_count() // 2], blocks[device_count() // 2 :]


def local(
    tokens,
    image,
    segments,
    valid_len,
    cotangent,
    w_attn,
    w_ffn,
    norm_params,
    momentum_attn,
    variance_attn,
    momentum_ffn,
    variance_ffn,
    momentum_norm,
    variance_norm,
):
    tags, width = tokens.shape
    hidden_width = w_ffn.shape[2]
    shard = w_attn.shape[1]
    segment = segments[0]
    info = jnp.stack(
        [jnp.sum(segment < 1), jnp.sum(segment < 2), valid_len[0], device_index()]
    ).astype(jnp.int32)

    first_part, second_part, rest_part = call(
        pack_kernel,
        [shaped(shard, 3 * width + 128), shaped(shard, 4 * width)]
        + [shaped(shard, width + 2 * hidden_width)],
        (w_attn, w_ffn, norm_params),
        "pack",
        1,
        False,
        (),
        60 * 2**20,
    )
    rest_full = lax.all_gather(rest_part, AXES, axis=0, tiled=True)
    first_far = gather_far(first_part)
    second_part = before(second_part, first_far)
    first_sent = [swap(first_far, mask) for mask in PLANE_MASKS]
    second_sent = [swap(second_part, mask) for mask in far_masks()]
    first_sent, second_sent, info = lax.optimization_barrier((first_sent, second_sent, info))
    second_far = jnp.stack([second_part] + second_sent)
    first_plane = join_plane([first_far] + before(first_sent, second_far))
    first_core = swap(first_plane, 1)
    second_sent = [swap(second_far, mask) for mask in PLANE_MASKS]

    wide_shape = shaped(width, tags)
    half_shape = shaped(width // 2, tags)
    log_shape = shaped(HEADS, 1, tags, kind=F32)
    f32_rows = shaped(tags, width, kind=F32)
    first_blocks = whole_blocks(first_plane, first_core)
    norms, q, k, v = call(
        project_kernel,
        [shaped(8, width, kind=F32)] + [wide_shape] * 3,
        (info, tokens, *first_blocks),
        "project",
        3,
        True,
        [(width, 3 * width + 128, BF16)],
    )

    o, log_self = call(
        functools.partial(self_forward_kernel, 0),
        [wide_shape, log_shape],
        (before(info, second_far), q, k, v),
        "self_forward",
        8,
        True,
        [(3 * QB, QB), (2, 3 * QB, QB), (2, 3 * QB, QB, BF16)],
    )
    second_plane = join_plane([second_far] + before(second_sent, o))
    second_core = swap(second_plane, 1)
    image_shape = shaped(TABLES, width, IMG)
    image_half = shaped(TABLES, width // 2, IMG)
    second_blocks = whole_blocks(second_plane, second_core)
    w_second, kc, vc = call(
        image_kernel,
        [shaped(width, 4 * width)] + [image_shape] * 2,
        (info, image, *second_blocks),
        "image_project",
        6,
        True,
        (),
    )
    n1, r1, qc = call(
        mid_kernel,
        [f32_rows, shaped(8, tags, kind=F32), wide_shape],
        (tokens, o, w_second, norms),
        "mid",
        3,
        False,
        (),
    )
    oc, log_cross = call(
        cross_forward_kernel,
        [wide_shape, log_shape],
        (info, qc, kc, vc),
        "cross_forward",
        16,
        True,
        [(2, IMG, QB), (2, IMG, QB, BF16)],
    )
    feed_cols = 2 * hidden_width + width
    result, dh2, doc, feed_near, feed_far, norm_feed = call(
        feed_kernel,
        [
            shaped(tags, width),
            f32_rows,
            wide_shape,
            *spread_shapes(shard, feed_cols),
            shaped(8, width, kind=F32),
        ],
        (info, oc, n1, cotangent, rest_full, norms),
        "feed",
        15,
        True,
        [(width, hidden_width), (width, width), (8, width), (tags, width, BF16)]
        + [(tags, hidden_width, BF16)] * 2
        + [(tags, width, BF16)] * 2,
    )

    def cross_backward(index, *deps):
        return call(
            functools.partial(cross_backward_kernel, index * HEADS // 2),
            [half_shape, image_half, image_half],
            [before(info, *deps), qc, kc, vc, oc, log_cross, doc],
            "cross_backward",
            14,
            True,
            [(TABLES, width // 2, IMG)] * 2 + [(2, IMG, QB)] * 2 + [(2, IMG, QB, BF16)] * 2,
        )

    def self_backward(index, *deps):
        return call(
            functools.partial(self_backward_kernel, index * HEADS // 2),
            [half_shape] * 3,
            [before(info, *deps), q, k, v, o, log_self, do],
            "self_backward",
            7,
            True,
            [(width // 2, tags)] * 2
            + [(3 * QB, QB)]
            + [(2, 3 * QB, QB)] * 2
            + [(2, 3 * QB, QB, BF16)] * 2,
        )

    feed_near, feed_far = split_blocks(feed_near, feed_far)
    dqc0, dkc0, dvc0 = cross_backward(0)
    feed_near = before(feed_near, dqc0)
    own_feed, send_feed = scatter_plane(scatter_core(feed_near, feed_far))
    dqc1, dkc1, dvc1 = cross_backward(1, send_feed)
    own_feed = before(own_feed, dqc1)
    own_feed, send_feed = scatter_plane_end(own_feed, send_feed)
    dh1, do, inner_near, inner_far, norm_inner = call(
        inner_kernel,
        [
            f32_rows,
            wide_shape,
            *spread_shapes(shard, 4 * width),
            shaped(8, width, kind=F32),
        ],
        (before(info, send_feed), dqc0, dqc1, dh2, n1, r1, o, *second_blocks, norms)
        + (image, dkc0, dkc1, dvc0, dvc1),
        "inner",
        10,
        True,
        [(width, 2 * width), (width, width), (8, width)]
        + [(tags, width, BF16)] * 2
        + [(width, 4 * width, BF16)],
    )
    inner_near, inner_far = split_blocks(inner_near, inner_far)
    dq0, dk0, dv0 = self_backward(0)
    inner_near = before(inner_near, dq0)
    own_inner, send_inner = scatter_plane(scatter_core(inner_near, inner_far))
    dq1, dk1, dv1 = self_backward(1, send_inner)
    grads = (dq0, dq1, dk0, dk1, dv0, dv1)
    last_cols = 3 * width + 128
    last_near, last_far = call(
        project_weight_kernel,
        spread_shapes(shard, last_cols),
        (info, tokens) + grads + (norm_inner, norm_feed),
        "project_weight",
        3,
        True,
        [(width, last_cols)],
    )
    last_near, last_far = split_blocks(last_near, last_far)
    own_inner, send_inner = scatter_plane_end(before(own_inner, dq1), send_inner)
    send_both = [jnp.concatenate(pair, axis=1) for pair in zip(send_feed, send_inner)]
    pieces_both = scatter_far_end(jnp.concatenate([own_feed, own_inner], axis=1), send_both)
    own_last, send_last = scatter_plane(scatter_core(before(last_near, send_both), last_far))
    image_grad = call(
        image_grad_kernel,
        shaped(image.shape[0], width, kind=F32),
        (before(info, send_last), dkc0, dkc1, dvc0, dvc1, *second_blocks),
        "image_grad",
        6,
        True,
        [(width, 4 * width, BF16)],
    )
    token_grad = call(
        token_grad_kernel,
        f32_rows,
        (before(info, image_grad),) + grads + (*first_blocks, dh1),
        "token_grad",
        4,
        True,
        [(width, 3 * width + 128, BF16)],
    )
    own_last, send_last = scatter_plane_end(before(own_last, token_grad, pieces_both), send_last)
    pieces_last = scatter_far_end(own_last, send_last)

    weights = (w_attn, w_ffn, norm_params)
    moments = (momentum_attn, variance_attn, momentum_ffn, variance_ffn)
    moments = moments + (momentum_norm, variance_norm)
    like = [shaped(*array.shape, kind=F32) for array in weights + moments + weights]
    pieces = [*pieces_both, *pieces_last]
    per_chunk = len(pieces) // 2
    outs = call(
        lambda *refs: moments_kernel(per_chunk, *refs),
        like + [shaped(8, 128, kind=F32)],
        (*pieces, *weights, *moments),
        "moments",
        3,
        False,
    )
    grad_attn, grad_ffn, grad_norm = outs[0:3]
    first_attn, second_attn, first_ffn, second_ffn, first_norm, second_norm = outs[3:9]
    sums = outs[12]
    sums = sums + swap(sums, 1)
    sums = pair_sum([sums] + [swap(sums, mask) for mask in PLANE_MASKS])
    pieces = [sums] + [swap(sums, mask) for mask in far_masks()]
    new_attn, new_ffn, new_norm, norms_both = call(
        apply_kernel,
        like[0:3] + [shaped(8, 128, kind=F32)],
        (*pieces, *weights, *outs[9:12]),
        "apply",
        2,
        False,
    )
    weight_norms = norms_both[0, 0:16]
    update_norms = norms_both[1, 0:16]
    return (
        result,
        token_grad,
        image_grad,
        grad_attn,
        grad_ffn,
        grad_norm,
        new_attn,
        new_ffn,
        new_norm,
        first_attn,
        second_attn,
        first_ffn,
        second_ffn,
        first_norm,
        second_norm,
        weight_norms,
        update_norms,
    )


def solution(mesh):
    rows = P(AXES, None)
    stack = P(None, AXES, None)
    flat = P(None, AXES)
    in_specs = (rows, rows, rows, P(AXES), rows) + (stack, stack, flat)
    in_specs = in_specs + (stack, stack, stack, stack, flat, flat)
    out_specs = (rows, rows, rows, stack, stack, flat, stack, stack, flat)
    out_specs = out_specs + (stack, stack, stack, stack, flat, flat, P(), P())
    return jax.shard_map(local, mesh=mesh, in_specs=in_specs, out_specs=out_specs, check_vma=False)
```

```python
import functools

import jax
import jax.numpy as jnp
from jax import lax
from jax.experimental import pallas as pl
from jax.experimental.pallas import tpu as pltpu
from jax.sharding import PartitionSpec as P

HD = 64
HEADS = 8
IMG = 784
TABLES = 3
STEP = 10
QB = 256

MASKED_SCORE = -1000000000.0
BETA_FIRST = 0.9
BETA_SECOND = 0.999
LEARN_RATE = 0.3
WEIGHT_DECAY = 0.01
ADAM_EPSILON = 1e-06
NORM_EPSILON = 1e-05

VMEM_GRANT = 32 * 2**20

AXES = ("wide", "narrow")
F32 = jnp.float32
BF16 = jnp.bfloat16
VMEM = pl.BlockSpec(memory_space=pltpu.VMEM)
SMEM = pl.BlockSpec(memory_space=pltpu.SMEM)


def dot(left, right, left_dim, right_dim):
    return lax.dot_general(
        left, right, (((left_dim,), (right_dim,)), ((), ())), preferred_element_type=F32
    )


def normalise(hidden):
    centre = hidden - jnp.mean(hidden, axis=-1, keepdims=True)
    scale = lax.rsqrt(jnp.mean(centre * centre, axis=-1, keepdims=True) + NORM_EPSILON)
    return centre * scale, scale


def norm_back(grad, gain, normed, scale):
    inner = grad * gain
    return scale * (
        inner
        - jnp.mean(inner, axis=-1, keepdims=True)
        - normed * jnp.mean(inner * normed, axis=-1, keepdims=True)
    )


def column_sum(value):
    return jnp.sum(value, axis=0, keepdims=True)


def pipeline(chains):
    done = object()
    live = []
    waiting = list(chains)
    while live or waiting:
        if waiting:
            live.insert(0, waiting.pop(0))
        live = [chain for chain in live if next(chain, done) is not done]


def place_blocks(me, near_ref, far_ref, out_ref):
    if near_ref.shape == out_ref.shape:
        out_ref[...] = near_ref[...]
        return
    size = near_ref.shape[1]
    for k in range(2 * near_ref.shape[0]):
        ref = far_ref if k & 1 else near_ref
        row = pl.multiple_of((me ^ k) * size, size)
        out_ref[pl.ds(row, size), :] = ref[exchange_slot(k)]


def spread_blocks(me, source, near_ref, far_ref, col):
    cols = slice(col, col + source.shape[1])
    if near_ref.shape[0] == source.shape[0]:
        near_ref[:, cols] = source[...].astype(BF16)
        far_ref[...] = jnp.zeros(far_ref.shape, BF16)
        return
    size = near_ref.shape[1]
    for k in range(2 * near_ref.shape[0]):
        ref = far_ref if k & 1 else near_ref
        row = pl.multiple_of((me ^ k) * size, size)
        ref[exchange_slot(k), :, cols] = source[pl.ds(row, size), :].astype(BF16)


def pack_kernel(wa_ref, wf_ref, wn_ref, first_ref, rest_ref):
    width, hidden = wa_ref.shape[2], wf_ref.shape[2]
    for slot in range(3):
        first_ref[:, slot * width : (slot + 1) * width] = wa_ref[slot].astype(BF16)
    rows = [wn_ref[...], jnp.zeros((128 - wn_ref.shape[0], wn_ref.shape[1]), F32)]
    first_ref[:, 3 * width :] = jnp.transpose(jnp.concatenate(rows, axis=0)).astype(BF16)
    for slot in range(5):
        rest_ref[:, slot * width : (slot + 1) * width] = wa_ref[slot + 3].astype(BF16)
    for slot in range(2):
        begin = 5 * width + slot * hidden
        rest_ref[:, begin : begin + hidden] = wf_ref[slot].astype(BF16)


def project_kernel(info_ref, x_ref, near_ref, far_ref, norm_ref, q_ref, k_ref, v_ref, w_ref):
    place_blocks(info_ref[3], near_ref, far_ref, w_ref)
    width = x_ref.shape[1]
    norm_ref[...] = jnp.transpose(w_ref[:, 3 * width :].astype(F32))[0:8, :]
    for block in range(x_ref.shape[0] // QB):
        cols = slice(block * QB, (block + 1) * QB)
        x = x_ref[cols, :]
        q_ref[:, cols] = (dot(w_ref[:, 0:width], x, 0, 1).astype(BF16) * 0.125).astype(BF16)
        k_ref[:, cols] = dot(w_ref[:, width : 2 * width], x, 0, 1).astype(BF16)
        v_ref[:, cols] = dot(w_ref[:, 2 * width : 3 * width], x, 0, 1).astype(BF16)


def head_rows(index):
    return slice(index * HD, (index + 1) * HD)


def forward_heads(query, key, value, finish, heads, count, bias, score_ref, prob_ref):
    def chain(index):
        slot = index % 2
        scores = dot(key(index), query(index), 0, 0)
        score_ref[slot, 0:count] = scores if bias is None else scores + bias[0:count]
        yield
        scores = score_ref[slot, 0:count]
        highest = jnp.max(scores, axis=0, keepdims=True)
        prob_ref[slot, 0:count] = jnp.exp(scores - highest).astype(BF16)
        yield
        ones = jnp.ones((16, count), BF16)
        mixed = dot(jnp.concatenate([value(index), ones], axis=0), prob_ref[slot, 0:count], 1, 0)
        total = mixed[HD : HD + 1]
        finish(index, (mixed[0:HD] / total).astype(BF16), highest + jnp.log(total))

    pipeline([chain(index) for index in range(heads)])


def backward_heads(
    query, key, value, grad, mixed, logs, finish, heads, count, bias,
    score_ref, level_ref, prob_ref, delta_ref,
):
    def chain(index):
        slot = index % 2
        scores = dot(key(index), query(index), 0, 0)
        score_ref[slot, 0:count] = scores if bias is None else scores + bias[0:count]
        level_ref[slot, 0:count] = dot(value(index), grad(index), 0, 0)
        yield
        level = column_sum(grad(index).astype(F32) * mixed(index).astype(F32))
        probs = jnp.exp(score_ref[slot, 0:count] - logs(index))
        prob_ref[slot, 0:count] = probs.astype(BF16)
        delta_ref[slot, 0:count] = (probs * (level_ref[slot, 0:count] - level)).astype(BF16)
        yield
        delta = delta_ref[slot, 0:count]
        finish(
            index,
            (dot(key(index), delta, 1, 0) * 0.125).astype(BF16),
            dot(query(index), delta, 1, 1),
            dot(grad(index), prob_ref[slot, 0:count], 1, 1),
        )

    pipeline([chain(index) for index in range(heads)])


def self_blocks(info_ref, rows, bias, run):
    second, third, valid = info_ref[0], info_ref[1], info_ref[2]

    def step(block, carry):
        start = block * QB
        first = jnp.where(start < second, 0, jnp.where(start < third, second, third))
        back = block - first // QB
        for extent in range(3):

            @pl.when(back == extent)
            def _():
                begin = (block - extent) * QB
                count = (extent + 1) * QB
                place = start + lax.broadcasted_iota(jnp.int32, (1, QB), 1)
                low = jnp.where(place < second, 0, jnp.where(place < third, second, third))
                high = jnp.minimum(place, valid - 1)
                key = begin + lax.broadcasted_iota(jnp.int32, (count, QB), 0)
                allowed = (key >= low) & ((key <= high) | (key == place))
                bias[0:count] = jnp.where(allowed, 0.0, MASKED_SCORE)
                run(
                    pl.ds(pl.multiple_of(start, QB), QB),
                    pl.ds(pl.multiple_of(begin, QB), count),
                    count,
                )

        return carry

    lax.fori_loop(0, rows // QB, step, 0)


def self_forward_kernel(
    base, info_ref, q_ref, k_ref, v_ref, o_ref, log_ref, bias_ref, score_ref, prob_ref
):
    def run(cols, keys, count):
        def finish(index, mixed, logs):
            o_ref[head_rows(index), cols] = mixed
            log_ref[index, :, cols] = logs

        forward_heads(
            lambda index: q_ref[head_rows(base + index), cols],
            lambda index: k_ref[head_rows(base + index), keys],
            lambda index: v_ref[head_rows(base + index), keys],
            finish, o_ref.shape[0] // HD, count, bias_ref, score_ref, prob_ref,
        )

    self_blocks(info_ref, q_ref.shape[1], bias_ref, run)


def self_backward_kernel(
    base, info_ref, q_ref, k_ref, v_ref, o_ref, log_ref, do_ref, dq_ref, dk_ref, dv_ref,
    sum_k, sum_v, bias_ref, score_ref, level_ref, prob_ref, delta_ref,
):
    sum_k[...] = jnp.zeros(sum_k.shape, F32)
    sum_v[...] = jnp.zeros(sum_v.shape, F32)

    def run(cols, keys, count):
        def finish(index, grad_query, grad_key, grad_value):
            dq_ref[head_rows(index), cols] = grad_query
            sum_k[head_rows(index), keys] += grad_key
            sum_v[head_rows(index), keys] += grad_value

        backward_heads(
            lambda index: q_ref[head_rows(base + index), cols],
            lambda index: k_ref[head_rows(base + index), keys],
            lambda index: v_ref[head_rows(base + index), keys],
            lambda index: do_ref[head_rows(base + index), cols],
            lambda index: o_ref[head_rows(base + index), cols],
            lambda index: log_ref[base + index, :, cols],
            finish, dq_ref.shape[0] // HD, count, bias_ref,
            score_ref, level_ref, prob_ref, delta_ref,
        )

    self_blocks(info_ref, q_ref.shape[1], bias_ref, run)
    dk_ref[...] = sum_k[...].astype(BF16)
    dv_ref[...] = sum_v[...].astype(BF16)


def mid_kernel(x_ref, o_ref, w_ref, norm_ref, n_ref, r_ref, q_ref):
    gain, shift = norm_ref[0:1, :], norm_ref[3:4, :]
    width = x_ref.shape[1]

    def chain(block):
        rows = slice(block * QB, (block + 1) * QB)
        branch = dot(o_ref[:, rows], w_ref[:, 0:width], 0, 0)
        yield
        normed, scale = normalise(x_ref[rows, :].astype(F32) + branch)
        n_ref[rows, :] = normed
        r_ref[:, rows] = jnp.transpose(jnp.broadcast_to(scale, (QB, 128)))[0:8]
        low = (normed * gain + shift).astype(BF16)
        yield
        query = dot(w_ref[:, width : 2 * width], low, 0, 1).astype(BF16)
        q_ref[:, rows] = (query * 0.125).astype(BF16)

    pipeline([chain(block) for block in range(x_ref.shape[0] // QB)])


def image_kernel(info_ref, image_ref, near_ref, far_ref, w_ref, k_ref, v_ref):
    place_blocks(info_ref[3], near_ref, far_ref, w_ref)
    width = image_ref.shape[1]
    for table in range(TABLES):
        image = image_ref[table * IMG : (table + 1) * IMG, :]
        k_ref[table] = dot(w_ref[:, 2 * width : 3 * width], image, 0, 1).astype(BF16)
        v_ref[table] = dot(w_ref[:, 3 * width : 4 * width], image, 0, 1).astype(BF16)


def cross_blocks(info_ref, rows, run):
    def job(index, carry):
        table = index // 3
        step = index % 3
        second, third = info_ref[0], info_ref[1]
        begin = jnp.where(table == 0, 0, jnp.where(table == 1, second, third))
        end = jnp.where(table == 0, second, jnp.where(table == 1, third, rows))
        first = begin // QB
        last = (end - 1) // QB
        merged = (last > first) & (end % QB > 0) & (end % QB <= begin % QB)
        count = last - first + 1 - merged.astype(jnp.int32)

        @pl.when(step < count)
        def _():
            block = first + step
            other = jnp.where(merged & (step == 0), last, block)
            lane = lax.broadcasted_iota(jnp.int32, (1, QB), 1)
            place = block * QB + lane
            here = (place >= begin) & (place < end)
            place = other * QB + lane
            there = (place < end) & (place >= jnp.where(other == block, rows, begin))
            run(
                pl.ds(pl.multiple_of(block * QB, QB), QB),
                pl.ds(pl.multiple_of(other * QB, QB), QB),
                table, here, there,
            )

        return carry

    lax.fori_loop(0, TABLES * 3, job, 0)


def store_both(ref, index, value, cols, others, here, there):
    ref[index + (cols,)] = jnp.where(here, value, ref[index + (cols,)])
    ref[index + (others,)] = jnp.where(there, value, ref[index + (others,)])


def cross_forward_kernel(info_ref, q_ref, k_ref, v_ref, o_ref, log_ref, score_ref, prob_ref):
    def run(cols, others, table, here, there):
        def finish(index, mixed, logs):
            store_both(o_ref, (head_rows(index),), mixed, cols, others, here, there)
            store_both(log_ref, (index, slice(None)), logs, cols, others, here, there)

        def query(index):
            rows = head_rows(index)
            return jnp.where(there, q_ref[rows, others], q_ref[rows, cols])

        forward_heads(
            query,
            lambda index: k_ref[table, head_rows(index), :],
            lambda index: v_ref[table, head_rows(index), :],
            finish, q_ref.shape[0] // HD, IMG, None, score_ref, prob_ref,
        )

    cross_blocks(info_ref, q_ref.shape[1], run)


def cross_backward_kernel(
    base, info_ref, q_ref, k_ref, v_ref, o_ref, log_ref, do_ref, dq_ref, dk_ref, dv_ref,
    sum_k, sum_v, score_ref, level_ref, prob_ref, delta_ref,
):
    sum_k[...] = jnp.zeros(sum_k.shape, F32)
    sum_v[...] = jnp.zeros(sum_v.shape, F32)

    def run(cols, others, table, here, there):
        def finish(index, grad_query, grad_key, grad_value):
            rows = head_rows(index)
            store_both(dq_ref, (rows,), grad_query, cols, others, here, there)
            sum_k[table, rows, :] += grad_key
            sum_v[table, rows, :] += grad_value

        def both(ref):
            def read(index):
                rows = head_rows(base + index)
                return jnp.where(there, ref[rows, others], ref[rows, cols])

            return read

        def logs(index):
            far = jnp.where(there, log_ref[base + index, :, others], -MASKED_SCORE)
            return jnp.where(here, log_ref[base + index, :, cols], far)

        seen = here | there
        grads = both(do_ref)
        zero = jnp.zeros((), BF16)
        backward_heads(
            both(q_ref),
            lambda index: k_ref[table, head_rows(base + index), :],
            lambda index: v_ref[table, head_rows(base + index), :],
            lambda index: jnp.where(seen, grads(index), zero),
            both(o_ref), logs, finish, dq_ref.shape[0] // HD, IMG, None,
            score_ref, level_ref, prob_ref, delta_ref,
        )

    cross_blocks(info_ref, q_ref.shape[1], run)
    dk_ref[...] = sum_k[...].astype(BF16)
    dv_ref[...] = sum_v[...].astype(BF16)


def feed_kernel(
    info_ref, o_ref, n1_ref, cot_ref, wnear_ref, wfar_ref, norm_ref,
    result_ref, dh_ref, do_ref, near_ref, far_ref, dnorm_ref,
    sum_up, sum_out, sum_norm, all_x2, all_active, all_du, all_dz, all_dac, w_ref,
):
    place_blocks(info_ref[3], wnear_ref, wfar_ref, w_ref)
    valid = info_ref[2]
    width = cot_ref.shape[1]
    hidden_width = (w_ref.shape[1] - width) // 2
    co_ref = w_ref.at[:, 0:width]
    up_ref = w_ref.at[:, width : width + hidden_width]
    down_ref = w_ref.at[:, width + hidden_width :]
    sum_norm[...] = jnp.zeros(sum_norm.shape, F32)
    root = 0.7978845608028654

    def chain(block):
        rows = slice(block * QB, (block + 1) * QB)
        branch = dot(o_ref[:, rows], co_ref[...], 0, 0)
        yield
        first = n1_ref[rows, :] * norm_ref[0:1, :] + norm_ref[3:4, :]
        n2, r2 = normalise(first + branch)
        x2 = n2 * norm_ref[1:2, :] + norm_ref[4:5, :]
        x2_low = x2.astype(BF16)
        all_x2[rows, :] = x2_low
        yield
        u = dot(x2_low, up_ref[...], 1, 0)
        yield
        square = u * u
        curve = jnp.tanh(root * u * (1.0 + 0.044715 * square))
        half = 0.5 * (1.0 + curve)
        active = (u * half).astype(BF16)
        slope = half + 0.5 * u * (1.0 - curve * curve) * (root * (1.0 + 3 * 0.044715 * square))
        all_active[rows, :] = active
        yield
        down = dot(active, down_ref[...], 1, 1)
        yield
        n3, r3 = normalise(x2 + down)
        result_ref[rows, :] = (n3 * norm_ref[2:3, :] + norm_ref[5:6, :]).astype(BF16)
        place = block * QB + lax.broadcasted_iota(jnp.int32, (QB, 1), 0)
        dy = jnp.where(place < valid, cot_ref[rows, :].astype(F32), 0.0)
        sum_norm[2:3, :] += column_sum(dy * n3)
        sum_norm[5:6, :] += column_sum(dy)
        dh3 = norm_back(dy, norm_ref[2:3, :], n3, r3)
        dz = dh3.astype(BF16)
        all_dz[rows, :] = dz
        yield
        df = dot(dz, down_ref[...], 1, 0)
        yield
        du = (df * slope).astype(BF16)
        all_du[rows, :] = du
        yield
        back = dot(du, up_ref[...], 1, 1)
        yield
        dx2 = dh3 + back
        sum_norm[1:2, :] += column_sum(dx2 * n2)
        sum_norm[4:5, :] += column_sum(dx2)
        dh2 = norm_back(dx2, norm_ref[1:2, :], n2, r2)
        dh_ref[rows, :] = dh2
        dac = dh2.astype(BF16)
        all_dac[rows, :] = dac
        yield
        do_ref[:, rows] = dot(co_ref[...], dac, 1, 1).astype(BF16)

    pipeline([chain(block) for block in range(cot_ref.shape[0] // QB)])
    me = info_ref[3]
    sum_up[...] = dot(all_x2[...], all_du[...], 0, 0)
    spread_blocks(me, sum_up, near_ref, far_ref, 0)
    sum_up[...] = dot(all_dz[...], all_active[...], 0, 0)
    spread_blocks(me, sum_up, near_ref, far_ref, hidden_width)
    sum_out[...] = dot(o_ref[...], all_dac[...], 1, 0)
    spread_blocks(me, sum_out, near_ref, far_ref, 2 * hidden_width)
    dnorm_ref[...] = sum_norm[...]


def inner_kernel(
    info_ref, dq0_ref, dq1_ref, dh2_ref, n1_ref, r1_ref, o_ref, wnear_ref, wfar_ref,
    norm_ref, image_ref, dk0_ref, dk1_ref, dv0_ref, dv1_ref,
    dh_ref, do_ref, near_ref, far_ref, dnorm_ref,
    sum_image, sum_inner, sum_norm, all_low, all_da, w_ref,
):
    place_blocks(info_ref[3], wnear_ref, wfar_ref, w_ref)
    sum_norm[...] = jnp.zeros(sum_norm.shape, F32)
    width = dh_ref.shape[1]
    gain, shift = norm_ref[0:1, :], norm_ref[3:4, :]

    def chain(block):
        rows = slice(block * QB, (block + 1) * QB)
        dq = jnp.concatenate([dq0_ref[:, rows], dq1_ref[:, rows]], axis=0)
        back = dot(dq, w_ref[:, width : 2 * width], 0, 1)
        yield
        normed = n1_ref[rows, :]
        all_low[rows, :] = (normed * gain + shift).astype(BF16)
        dx1 = dh2_ref[rows, :] + back
        sum_norm[0:1, :] += column_sum(dx1 * normed)
        sum_norm[1:2, :] += column_sum(dx1)
        dh1 = norm_back(dx1, gain, normed, jnp.transpose(jnp.broadcast_to(r1_ref[0:1, rows], (128, QB)))[:, 0:1])
        dh_ref[rows, :] = dh1
        da = dh1.astype(BF16)
        all_da[rows, :] = da
        yield
        do_ref[:, rows] = dot(w_ref[:, 0:width], da, 1, 1).astype(BF16)

    pipeline([chain(block) for block in range(dh2_ref.shape[0] // QB)])
    me = info_ref[3]
    total = None
    for table in range(TABLES):
        image = image_ref[table * IMG : (table + 1) * IMG, :]
        grads = jnp.concatenate(
            [dk0_ref[table], dk1_ref[table], dv0_ref[table], dv1_ref[table]], axis=0
        )
        part = dot(image, grads, 0, 1)
        total = part if total is None else total + part
    sum_image[...] = total
    spread_blocks(me, sum_image, near_ref, far_ref, 2 * width)
    sum_inner[...] = dot(o_ref[...], all_da[...], 1, 0)
    spread_blocks(me, sum_inner, near_ref, far_ref, 0)
    dq = jnp.concatenate([dq0_ref[...], dq1_ref[...]], axis=0)
    sum_inner[...] = dot(all_low[...], dq, 0, 1)
    spread_blocks(me, sum_inner, near_ref, far_ref, width)
    dnorm_ref[...] = sum_norm[...]


def image_grad_kernel(
    info_ref, dk0_ref, dk1_ref, dv0_ref, dv1_ref, near_ref, far_ref, out_ref, w_ref
):
    place_blocks(info_ref[3], near_ref, far_ref, w_ref)
    width = out_ref.shape[1]
    for table in range(TABLES):
        rows = slice(table * IMG, (table + 1) * IMG)
        grads = jnp.concatenate(
            [dk0_ref[table], dk1_ref[table], dv0_ref[table], dv1_ref[table]], axis=0
        )
        out_ref[rows, :] = dot(grads, w_ref[:, 2 * width : 4 * width], 0, 1)


def project_weight_kernel(
    info_ref, x_ref, dq0_ref, dq1_ref, dk0_ref, dk1_ref, dv0_ref, dv1_ref, inner_ref, feed_ref,
    near_ref, far_ref, total,
):
    width = x_ref.shape[1]
    refs = (dq0_ref, dq1_ref, dk0_ref, dk1_ref, dv0_ref, dv1_ref)
    grads = jnp.concatenate([ref[...] for ref in refs], axis=0)
    total[:, 0 : 3 * width] = dot(x_ref[...], grads, 0, 1)
    order = [inner_ref[0:1], feed_ref[1:2], feed_ref[2:3]]
    order += [inner_ref[1:2], feed_ref[4:5], feed_ref[5:6], jnp.zeros((122, width), F32)]
    total[:, 3 * width :] = jnp.transpose(jnp.concatenate(order, axis=0))
    spread_blocks(info_ref[3], total, near_ref, far_ref, 0)


def token_grad_kernel(
    info_ref, dq0_ref, dq1_ref, dk0_ref, dk1_ref, dv0_ref, dv1_ref, near_ref, far_ref, dh_ref,
    out_ref, w_ref,
):
    place_blocks(info_ref[3], near_ref, far_ref, w_ref)
    width = dh_ref.shape[1]
    refs = (dq0_ref, dq1_ref, dk0_ref, dk1_ref, dv0_ref, dv1_ref)
    for block in range(dh_ref.shape[0] // QB):
        rows = slice(block * QB, (block + 1) * QB)
        grads = jnp.concatenate([ref[:, rows] for ref in refs], axis=0)
        out_ref[rows, :] = dh_ref[rows, :] + dot(grads, w_ref[:, 0 : 3 * width], 0, 1)


def lamb_moments(weight, grad, first, second, decay):
    first_new = BETA_FIRST * first + (1.0 - BETA_FIRST) * grad
    second_new = BETA_SECOND * second + (1.0 - BETA_SECOND) * grad * grad
    first_hat = first_new / (1.0 - BETA_FIRST**STEP)
    second_hat = second_new / (1.0 - BETA_SECOND**STEP)
    update = first_hat / (jnp.sqrt(second_hat) + ADAM_EPSILON) + decay * weight
    return (first_new, second_new, update)


def total_of(value):
    return jnp.sum(jnp.sum(value * value, axis=0, keepdims=True), axis=1, keepdims=True)


def moments_kernel(per, *refs):
    both, last = refs[0:per], refs[per : 2 * per]
    wa, wf, wn, ma, va, mf, vf, mn, vn = refs[2 * per : 2 * per + 9]
    ga, gf, gn, oma, ova, omf, ovf, omn, ovn, ua, uf, un, sums = refs[2 * per + 9 :]
    width, hidden = wa.shape[2], wf.shape[2]
    lane = lax.broadcasted_iota(jnp.int32, (1, 128), 1)
    weights = jnp.zeros((1, 128), F32)
    updates = jnp.zeros((1, 128), F32)

    def grad(pieces, col, size):
        cols = slice(col, col + size)
        near = [ref[:, cols].astype(F32) for ref in pieces]
        total = near[0]
        for part in near[1:]:
            total += part
        return total

    def tensor(slot, value, index, weight, first, second, outs, decay):
        nonlocal weights, updates
        first_new, second_new, update = lamb_moments(
            weight[index], value, first[index], second[index], decay
        )
        for ref, part in zip(outs, (value, first_new, second_new, update)):
            ref[index] = part
        weights = jnp.where(lane == slot, total_of(weight[index]), weights)
        updates = jnp.where(lane == slot, total_of(update), updates)

    for slot in range(8):
        pieces, col = (last, slot) if slot < 3 else (both, 2 * hidden // width + slot - 2)
        if slot == 7:
            pieces, col = both, 2 * hidden // width
        value = grad(pieces, col * width, width)
        tensor(slot, value, slot, wa, ma, va, (ga, oma, ova, ua), WEIGHT_DECAY)
    for slot in range(2):
        value = grad(both, slot * hidden, hidden)
        tensor(8 + slot, value, slot, wf, mf, vf, (gf, omf, ovf, uf), WEIGHT_DECAY)
    norms = jnp.transpose(grad(last, 3 * width, 128))
    for slot in range(6):
        row = slice(slot, slot + 1)
        tensor(10 + slot, norms[row, :], row, wn, mn, vn, (gn, omn, ovn, un), 0.0)
    sums[...] = jnp.concatenate([weights, updates, jnp.zeros((6, 128), F32)], axis=0)


def apply_kernel(*refs):
    wa, wf, wn, ua, uf, un, na, nf, nn = refs[-10:-1]
    pieces, norms = refs[0:-10], refs[-1]
    total = pair_sum([ref[...] for ref in pieces])
    root = jnp.sqrt(total)
    norms[...] = root
    ratio = LEARN_RATE * (root[0:1, :] / root[1:2, :])
    for slot in range(8):
        na[slot] = wa[slot] - ratio[:, slot : slot + 1] * ua[slot]
    for slot in range(2):
        nf[slot] = wf[slot] - ratio[:, slot + 8 : slot + 9] * uf[slot]
    for slot in range(6):
        row = slice(slot, slot + 1)
        nn[row] = wn[row] - ratio[:, slot + 10 : slot + 11] * un[row]


def pair_sum(parts):
    while len(parts) > 1:
        parts = [parts[i] + parts[i + 1] for i in range(0, len(parts), 2)]
    return parts[0]


def shaped(*dims, kind=BF16):
    return jax.ShapeDtypeStruct(dims, kind)


def call(kernel, out_shape, operands, name, micros, info=True, scratch=(), grant=VMEM_GRANT):
    specs = [VMEM] * len(operands)
    if info:
        specs[0] = SMEM
    return pl.pallas_call(
        kernel,
        out_shape=out_shape,
        in_specs=specs,
        out_specs=jax.tree.map(lambda _: VMEM, out_shape),
        scratch_shapes=[
            pltpu.VMEM(dims[:-1], BF16) if dims[-1] is BF16 else pltpu.VMEM(dims, F32)
            for dims in scratch
        ],
        compiler_params=pltpu.CompilerParams(vmem_limit_bytes=grant),
        cost_estimate=pl.CostEstimate(
            flops=int(micros * 0.02e9), bytes_accessed=0, transcendentals=0
        ),
        name=name,
    )(*operands)


def device_index():
    return lax.axis_index("wide") * lax.axis_size("narrow") + lax.axis_index("narrow")


def device_count():
    return lax.axis_size("wide") * lax.axis_size("narrow")


def exchange_slot(k):
    return (k >> 3) * 4 + ((k >> 1) & 3)


def swap(value, mask):
    count = device_count()
    return lax.ppermute(value, AXES, [(i, i ^ mask) for i in range(count)])


def before(value, *others):
    return lax.optimization_barrier((value, others))[0]


def far_masks():
    return [k << 3 for k in range(1, device_count() >> 3)]


PLANE_MASKS = [2, 4, 6]


def gather_far(part):
    return jnp.stack([part] + [swap(part, mask) for mask in far_masks()])


def join_plane(parts):
    return jnp.stack(parts, axis=1).reshape((-1,) + parts[0].shape[1:])


def scatter_core(near, far):
    total = near.astype(F32) + swap(far, 1).astype(F32)
    total = total.reshape((-1, 4) + near.shape[1:])
    return [total[:, k] for k in range(4)]


def scatter_plane(parts):
    sends = [part.astype(BF16) for part in parts[1:]]
    return parts[0], sends


def scatter_plane_end(own, sends):
    total = own
    for mask, send in zip(PLANE_MASKS, sends):
        total = total + swap(send, mask).astype(F32)
    return total[0], [total[k].astype(BF16) for k in range(1, total.shape[0])]


def scatter_far_end(own, sends):
    return [own] + [swap(send, mask) for mask, send in zip(far_masks(), sends)]


def block_order():
    order = [0] * device_count()
    for k in range(device_count()):
        order[exchange_slot(k) + (k & 1) * (device_count() // 2)] = k
    return jnp.array(order, jnp.int32) ^ device_index()


def whole_blocks(near, far):
    if near.shape[1] % 16 == 0:
        return near, far
    blocks = jnp.concatenate([near, far])
    full = jnp.zeros_like(blocks).at[block_order()].set(blocks)
    return full.reshape(-1, near.shape[2]), jnp.zeros((16, 128), BF16)


def spread_shapes(shard, cols):
    if shard % 16 == 0:
        return [shaped(device_count() // 2, shard, cols)] * 2
    return [shaped(device_count() * shard, cols), shaped(16, 128)]


def split_blocks(near, far):
    if near.ndim == 3:
        return near, far
    blocks = near.reshape(device_count(), -1, near.shape[1])[block_order()]
    return blocks[: device_count() // 2], blocks[device_count() // 2 :]


def local(
    tokens,
    image,
    segments,
    valid_len,
    cotangent,
    w_attn,
    w_ffn,
    norm_params,
    momentum_attn,
    variance_attn,
    momentum_ffn,
    variance_ffn,
    momentum_norm,
    variance_norm,
):
    tags, width = tokens.shape
    hidden_width = w_ffn.shape[2]
    shard = w_attn.shape[1]
    segment = segments[0]
    info = jnp.stack(
        [jnp.sum(segment < 1), jnp.sum(segment < 2), valid_len[0], device_index()]
    ).astype(jnp.int32)

    first_part, second_part = call(
        pack_kernel,
        [shaped(shard, 3 * width + 128), shaped(shard, 5 * width + 2 * hidden_width)],
        (w_attn, w_ffn, norm_params),
        "pack",
        1,
        False,
        (),
        60 * 2**20,
    )
    first_far = gather_far(first_part)
    second_part = before(second_part, first_far)
    first_sent = [swap(first_far, mask) for mask in PLANE_MASKS]
    second_sent = [swap(second_part, mask) for mask in far_masks()]
    first_sent, second_sent, info = lax.optimization_barrier((first_sent, second_sent, info))
    second_far = jnp.stack([second_part] + second_sent)
    third_far = second_far[:, :, 4 * width :]
    second_far = second_far[:, :, 0 : 4 * width]
    first_plane = join_plane([first_far] + before(first_sent, second_far))
    first_core = swap(first_plane, 1)
    second_sent = [swap(second_far, mask) for mask in PLANE_MASKS]

    wide_shape = shaped(width, tags)
    half_shape = shaped(width // 2, tags)
    log_shape = shaped(HEADS, 1, tags, kind=F32)
    f32_rows = shaped(tags, width, kind=F32)
    first_blocks = whole_blocks(first_plane, first_core)
    norms, q, k, v = call(
        project_kernel,
        [shaped(8, width, kind=F32)] + [wide_shape] * 3,
        (info, tokens, *first_blocks),
        "project",
        3,
        True,
        [(width, 3 * width + 128, BF16)],
    )

    o, log_self = call(
        functools.partial(self_forward_kernel, 0),
        [wide_shape, log_shape],
        (before(info, second_far), q, k, v),
        "self_forward",
        8,
        True,
        [(3 * QB, QB), (2, 3 * QB, QB), (2, 3 * QB, QB, BF16)],
    )
    third_sent = [swap(third_far, mask) for mask in PLANE_MASKS]
    second_plane = join_plane([second_far] + before(second_sent, o))
    second_core = swap(second_plane, 1)
    image_shape = shaped(TABLES, width, IMG)
    image_half = shaped(TABLES, width // 2, IMG)
    second_blocks = whole_blocks(second_plane, second_core)
    w_second, kc, vc = call(
        image_kernel,
        [shaped(width, 4 * width)] + [image_shape] * 2,
        (before(info, third_far), image, *second_blocks),
        "image_project",
        6,
        True,
        (),
    )
    n1, r1, qc = call(
        mid_kernel,
        [f32_rows, shaped(8, tags, kind=F32), wide_shape],
        (tokens, o, w_second, norms),
        "mid",
        3,
        False,
        (),
    )
    oc, log_cross = call(
        cross_forward_kernel,
        [wide_shape, log_shape],
        (info, qc, kc, vc),
        "cross_forward",
        16,
        True,
        [(2, IMG, QB), (2, IMG, QB, BF16)],
    )
    third_plane = join_plane([third_far] + before(third_sent, oc))
    third_core = swap(third_plane, 1)
    feed_cols = 2 * hidden_width + width
    result, dh2, doc, feed_near, feed_far, norm_feed = call(
        feed_kernel,
        [
            shaped(tags, width),
            f32_rows,
            wide_shape,
            *spread_shapes(shard, feed_cols),
            shaped(8, width, kind=F32),
        ],
        (info, oc, n1, cotangent, *whole_blocks(third_plane, third_core), norms),
        "feed",
        15,
        True,
        [(width, hidden_width), (width, width), (8, width), (tags, width, BF16)]
        + [(tags, hidden_width, BF16)] * 2
        + [(tags, width, BF16)] * 2
        + [(width, feed_cols, BF16)],
    )

    def cross_backward(index, *deps):
        return call(
            functools.partial(cross_backward_kernel, index * HEADS // 2),
            [half_shape, image_half, image_half],
            [before(info, *deps), qc, kc, vc, oc, log_cross, doc],
            "cross_backward",
            14,
            True,
            [(TABLES, width // 2, IMG)] * 2 + [(2, IMG, QB)] * 2 + [(2, IMG, QB, BF16)] * 2,
        )

    def self_backward(index, *deps):
        return call(
            functools.partial(self_backward_kernel, index * HEADS // 2),
            [half_shape] * 3,
            [before(info, *deps), q, k, v, o, log_self, do],
            "self_backward",
            7,
            True,
            [(width // 2, tags)] * 2
            + [(3 * QB, QB)]
            + [(2, 3 * QB, QB)] * 2
            + [(2, 3 * QB, QB, BF16)] * 2,
        )

    feed_near, feed_far = split_blocks(feed_near, feed_far)
    dqc0, dkc0, dvc0 = cross_backward(0)
    feed_near = before(feed_near, dqc0)
    own_feed, send_feed = scatter_plane(scatter_core(feed_near, feed_far))
    dqc1, dkc1, dvc1 = cross_backward(1, send_feed)
    own_feed = before(own_feed, dqc1)
    own_feed, send_feed = scatter_plane_end(own_feed, send_feed)
    dh1, do, inner_near, inner_far, norm_inner = call(
        inner_kernel,
        [
            f32_rows,
            wide_shape,
            *spread_shapes(shard, 4 * width),
            shaped(8, width, kind=F32),
        ],
        (before(info, send_feed), dqc0, dqc1, dh2, n1, r1, o, *second_blocks, norms)
        + (image, dkc0, dkc1, dvc0, dvc1),
        "inner",
        10,
        True,
        [(width, 2 * width), (width, width), (8, width)]
        + [(tags, width, BF16)] * 2
        + [(width, 4 * width, BF16)],
    )
    inner_near, inner_far = split_blocks(inner_near, inner_far)
    dq0, dk0, dv0 = self_backward(0)
    inner_near = before(inner_near, dq0)
    own_inner, send_inner = scatter_plane(scatter_core(inner_near, inner_far))
    dq1, dk1, dv1 = self_backward(1, send_inner)
    grads = (dq0, dq1, dk0, dk1, dv0, dv1)
    last_cols = 3 * width + 128
    last_near, last_far = call(
        project_weight_kernel,
        spread_shapes(shard, last_cols),
        (info, tokens) + grads + (norm_inner, norm_feed),
        "project_weight",
        3,
        True,
        [(width, last_cols)],
    )
    last_near, last_far = split_blocks(last_near, last_far)
    own_inner, send_inner = scatter_plane_end(before(own_inner, dq1), send_inner)
    send_both = [jnp.concatenate(pair, axis=1) for pair in zip(send_feed, send_inner)]
    pieces_both = scatter_far_end(jnp.concatenate([own_feed, own_inner], axis=1), send_both)
    own_last, send_last = scatter_plane(scatter_core(before(last_near, send_both), last_far))
    image_grad = call(
        image_grad_kernel,
        shaped(image.shape[0], width, kind=F32),
        (before(info, send_last), dkc0, dkc1, dvc0, dvc1, *second_blocks),
        "image_grad",
        6,
        True,
        [(width, 4 * width, BF16)],
    )
    token_grad = call(
        token_grad_kernel,
        f32_rows,
        (before(info, image_grad),) + grads + (*first_blocks, dh1),
        "token_grad",
        4,
        True,
        [(width, 3 * width + 128, BF16)],
    )
    own_last, send_last = scatter_plane_end(before(own_last, token_grad, pieces_both), send_last)
    pieces_last = scatter_far_end(own_last, send_last)

    weights = (w_attn, w_ffn, norm_params)
    moments = (momentum_attn, variance_attn, momentum_ffn, variance_ffn)
    moments = moments + (momentum_norm, variance_norm)
    like = [shaped(*array.shape, kind=F32) for array in weights + moments + weights]
    pieces = [*pieces_both, *pieces_last]
    per_chunk = len(pieces) // 2
    outs = call(
        lambda *refs: moments_kernel(per_chunk, *refs),
        like + [shaped(8, 128, kind=F32)],
        (*pieces, *weights, *moments),
        "moments",
        3,
        False,
    )
    grad_attn, grad_ffn, grad_norm = outs[0:3]
    first_attn, second_attn, first_ffn, second_ffn, first_norm, second_norm = outs[3:9]
    sums = outs[12]
    sums = sums + swap(sums, 1)
    sums = pair_sum([sums] + [swap(sums, mask) for mask in PLANE_MASKS])
    pieces = [sums] + [swap(sums, mask) for mask in far_masks()]
    new_attn, new_ffn, new_norm, norms_both = call(
        apply_kernel,
        like[0:3] + [shaped(8, 128, kind=F32)],
        (*pieces, *weights, *outs[9:12]),
        "apply",
        2,
        False,
    )
    weight_norms = norms_both[0, 0:16]
    update_norms = norms_both[1, 0:16]
    return (
        result,
        token_grad,
        image_grad,
        grad_attn,
        grad_ffn,
        grad_norm,
        new_attn,
        new_ffn,
        new_norm,
        first_attn,
        second_attn,
        first_ffn,
        second_ffn,
        first_norm,
        second_norm,
        weight_norms,
        update_norms,
    )


def solution(mesh):
    rows = P(AXES, None)
    stack = P(None, AXES, None)
    flat = P(None, AXES)
    in_specs = (rows, rows, rows, P(AXES), rows) + (stack, stack, flat)
    in_specs = in_specs + (stack, stack, stack, stack, flat, flat)
    out_specs = (rows, rows, rows, stack, stack, flat, stack, stack, flat)
    out_specs = out_specs + (stack, stack, stack, stack, flat, flat, P(), P())
    return jax.shard_map(local, mesh=mesh, in_specs=in_specs, out_specs=out_specs, check_vma=False)
```

```python
import functools

import jax
import jax.numpy as jnp
from jax import lax
from jax.experimental import pallas as pl
from jax.experimental.pallas import tpu as pltpu
from jax.sharding import PartitionSpec as P

HD = 64
HEADS = 8
IMG = 784
TABLES = 3
STEP = 10
QB = 256

MASKED_SCORE = -1000000000.0
BETA_FIRST = 0.9
BETA_SECOND = 0.999
LEARN_RATE = 0.3
WEIGHT_DECAY = 0.01
ADAM_EPSILON = 1e-06
NORM_EPSILON = 1e-05

VMEM_GRANT = 32 * 2**20

AXES = ("wide", "narrow")
F32 = jnp.float32
BF16 = jnp.bfloat16
VMEM = pl.BlockSpec(memory_space=pltpu.VMEM)
SMEM = pl.BlockSpec(memory_space=pltpu.SMEM)


def dot(left, right, left_dim, right_dim):
    return lax.dot_general(
        left, right, (((left_dim,), (right_dim,)), ((), ())), preferred_element_type=F32
    )


def normalise(hidden):
    centre = hidden - jnp.mean(hidden, axis=-1, keepdims=True)
    scale = lax.rsqrt(jnp.mean(centre * centre, axis=-1, keepdims=True) + NORM_EPSILON)
    return centre * scale, scale


def norm_back(grad, gain, normed, scale):
    inner = grad * gain
    return scale * (
        inner
        - jnp.mean(inner, axis=-1, keepdims=True)
        - normed * jnp.mean(inner * normed, axis=-1, keepdims=True)
    )


def column_sum(value):
    return jnp.sum(value, axis=0, keepdims=True)


def pipeline(chains):
    done = object()
    live = []
    waiting = list(chains)
    while live or waiting:
        if waiting:
            live.insert(0, waiting.pop(0))
        live = [chain for chain in live if next(chain, done) is not done]


def place_blocks(me, near_ref, far_ref, out_ref):
    if near_ref.shape == out_ref.shape:
        out_ref[...] = near_ref[...]
        return
    size = near_ref.shape[1]
    for k in range(2 * near_ref.shape[0]):
        ref = far_ref if k & 1 else near_ref
        row = pl.multiple_of((me ^ k) * size, size)
        out_ref[pl.ds(row, size), :] = ref[exchange_slot(k, ref.shape[0])]


def spread_blocks(me, source, near_ref, far_ref, col):
    cols = slice(col, col + source.shape[1])
    if near_ref.shape[0] == source.shape[0]:
        near_ref[:, cols] = source[...].astype(BF16)
        far_ref[...] = jnp.zeros(far_ref.shape, BF16)
        return
    size = near_ref.shape[1]
    for k in range(2 * near_ref.shape[0]):
        ref = far_ref if k & 1 else near_ref
        row = pl.multiple_of((me ^ k) * size, size)
        ref[exchange_slot(k, ref.shape[0]), :, cols] = source[pl.ds(row, size), :].astype(BF16)


def pack_kernel(valid_ref, segment_ref, wa_ref, wf_ref, wn_ref, info_ref, first_ref, rest_ref):
    segment = segment_ref[...]
    info_ref[0] = jnp.sum((segment < 1).astype(jnp.int32))
    info_ref[1] = jnp.sum((segment < 2).astype(jnp.int32))
    info_ref[2] = valid_ref[0]
    info_ref[3] = device_index()
    width, hidden = wa_ref.shape[2], wf_ref.shape[2]
    for slot in range(3):
        first_ref[:, slot * width : (slot + 1) * width] = wa_ref[slot].astype(BF16)
    rows = [wn_ref[...], jnp.zeros((128 - wn_ref.shape[0], wn_ref.shape[1]), F32)]
    first_ref[:, 3 * width :] = jnp.transpose(jnp.concatenate(rows, axis=0)).astype(BF16)
    for slot in range(5):
        rest_ref[:, slot * width : (slot + 1) * width] = wa_ref[slot + 3].astype(BF16)
    for slot in range(2):
        begin = 5 * width + slot * hidden
        rest_ref[:, begin : begin + hidden] = wf_ref[slot].astype(BF16)


def project_kernel(info_ref, x_ref, near_ref, far_ref, norm_ref, q_ref, k_ref, v_ref, w_ref):
    place_blocks(info_ref[3], near_ref, far_ref, w_ref)
    width = x_ref.shape[1]
    norm_ref[...] = jnp.transpose(w_ref[:, 3 * width :].astype(F32))[0:8, :]
    for block in range(x_ref.shape[0] // QB):
        cols = slice(block * QB, (block + 1) * QB)
        x = x_ref[cols, :]
        q_ref[:, cols] = (dot(w_ref[:, 0:width], x, 0, 1).astype(BF16) * 0.125).astype(BF16)
        k_ref[:, cols] = dot(w_ref[:, width : 2 * width], x, 0, 1).astype(BF16)
        v_ref[:, cols] = dot(w_ref[:, 2 * width : 3 * width], x, 0, 1).astype(BF16)


def head_rows(index):
    return slice(index * HD, (index + 1) * HD)


def forward_heads(query, key, value, finish, heads, count, bias, score_ref, prob_ref):
    def chain(index):
        slot = index % 2
        scores = dot(key(index), query(index), 0, 0)
        score_ref[slot, 0:count] = scores if bias is None else scores + bias[0:count]
        yield
        scores = score_ref[slot, 0:count]
        highest = jnp.max(scores, axis=0, keepdims=True)
        prob_ref[slot, 0:count] = jnp.exp(scores - highest).astype(BF16)
        yield
        ones = jnp.ones((16, count), BF16)
        mixed = dot(jnp.concatenate([value(index), ones], axis=0), prob_ref[slot, 0:count], 1, 0)
        total = mixed[HD : HD + 1]
        finish(index, (mixed[0:HD] / total).astype(BF16), highest + jnp.log(total))

    pipeline([chain(index) for index in range(heads)])


def backward_heads(
    query, key, value, grad, mixed, logs, finish, heads, count, bias,
    score_ref, level_ref, prob_ref, delta_ref,
):
    def chain(index):
        slot = index % 2
        scores = dot(key(index), query(index), 0, 0)
        score_ref[slot, 0:count] = scores if bias is None else scores + bias[0:count]
        level_ref[slot, 0:count] = dot(value(index), grad(index), 0, 0)
        yield
        level = column_sum(grad(index).astype(F32) * mixed(index).astype(F32))
        probs = jnp.exp(score_ref[slot, 0:count] - logs(index))
        prob_ref[slot, 0:count] = probs.astype(BF16)
        delta_ref[slot, 0:count] = (probs * (level_ref[slot, 0:count] - level)).astype(BF16)
        yield
        delta = delta_ref[slot, 0:count]
        finish(
            index,
            (dot(key(index), delta, 1, 0) * 0.125).astype(BF16),
            dot(query(index), delta, 1, 1),
            dot(grad(index), prob_ref[slot, 0:count], 1, 1),
        )

    pipeline([chain(index) for index in range(heads)])


def self_blocks(info_ref, rows, bias, run):
    second, third, valid = info_ref[0], info_ref[1], info_ref[2]

    def step(block, carry):
        start = block * QB
        first = jnp.where(start < second, 0, jnp.where(start < third, second, third))
        back = block - first // QB
        for extent in range(3):

            @pl.when(back == extent)
            def _():
                begin = (block - extent) * QB
                count = (extent + 1) * QB
                place = start + lax.broadcasted_iota(jnp.int32, (1, QB), 1)
                low = jnp.where(place < second, 0, jnp.where(place < third, second, third))
                high = jnp.minimum(place, valid - 1)
                key = begin + lax.broadcasted_iota(jnp.int32, (count, QB), 0)
                allowed = (key >= low) & ((key <= high) | (key == place))
                bias[0:count] = jnp.where(allowed, 0.0, MASKED_SCORE)
                run(
                    pl.ds(pl.multiple_of(start, QB), QB),
                    pl.ds(pl.multiple_of(begin, QB), count),
                    count,
                )

        return carry

    lax.fori_loop(0, rows // QB, step, 0)


def self_forward_kernel(
    base, info_ref, q_ref, k_ref, v_ref, o_ref, log_ref, bias_ref, score_ref, prob_ref
):
    def run(cols, keys, count):
        def finish(index, mixed, logs):
            o_ref[head_rows(index), cols] = mixed
            log_ref[index, :, cols] = logs

        forward_heads(
            lambda index: q_ref[head_rows(base + index), cols],
            lambda index: k_ref[head_rows(base + index), keys],
            lambda index: v_ref[head_rows(base + index), keys],
            finish, o_ref.shape[0] // HD, count, bias_ref, score_ref, prob_ref,
        )

    self_blocks(info_ref, q_ref.shape[1], bias_ref, run)


def self_backward_kernel(
    base, info_ref, q_ref, k_ref, v_ref, o_ref, log_ref, do_ref, dq_ref, dk_ref, dv_ref,
    sum_k, sum_v, bias_ref, score_ref, level_ref, prob_ref, delta_ref,
):
    sum_k[...] = jnp.zeros(sum_k.shape, F32)
    sum_v[...] = jnp.zeros(sum_v.shape, F32)

    def run(cols, keys, count):
        def finish(index, grad_query, grad_key, grad_value):
            dq_ref[head_rows(index), cols] = grad_query
            sum_k[head_rows(index), keys] += grad_key
            sum_v[head_rows(index), keys] += grad_value

        backward_heads(
            lambda index: q_ref[head_rows(base + index), cols],
            lambda index: k_ref[head_rows(base + index), keys],
            lambda index: v_ref[head_rows(base + index), keys],
            lambda index: do_ref[head_rows(base + index), cols],
            lambda index: o_ref[head_rows(base + index), cols],
            lambda index: log_ref[base + index, :, cols],
            finish, dq_ref.shape[0] // HD, count, bias_ref,
            score_ref, level_ref, prob_ref, delta_ref,
        )

    self_blocks(info_ref, q_ref.shape[1], bias_ref, run)
    dk_ref[...] = sum_k[...].astype(BF16)
    dv_ref[...] = sum_v[...].astype(BF16)


def mid_kernel(x_ref, o_ref, w_ref, norm_ref, n_ref, nlow_ref, r_ref, q_ref):
    gain, shift = norm_ref[0:1, :], norm_ref[3:4, :]
    width = x_ref.shape[1]

    def chain(block):
        rows = slice(block * QB, (block + 1) * QB)
        branch = dot(o_ref[:, rows], w_ref[:, 0:width], 0, 0)
        yield
        normed, scale = normalise(x_ref[rows, :].astype(F32) + branch)
        n_ref[rows, :] = normed
        nlow_ref[rows, :] = normed.astype(BF16)
        r_ref[:, rows] = jnp.transpose(jnp.broadcast_to(scale, (QB, 128)))[0:8]
        low = (normed * gain + shift).astype(BF16)
        yield
        query = dot(w_ref[:, width : 2 * width], low, 0, 1).astype(BF16)
        q_ref[:, rows] = (query * 0.125).astype(BF16)

    pipeline([chain(block) for block in range(x_ref.shape[0] // QB)])


def image_kernel(info_ref, image_ref, near_ref, far_ref, w_ref, k_ref, v_ref):
    place_blocks(info_ref[3], near_ref, far_ref, w_ref)
    width = image_ref.shape[1]
    for table in range(TABLES):
        image = image_ref[table * IMG : (table + 1) * IMG, :]
        k_ref[table] = dot(w_ref[:, 2 * width : 3 * width], image, 0, 1).astype(BF16)
        v_ref[table] = dot(w_ref[:, 3 * width : 4 * width], image, 0, 1).astype(BF16)


def cross_blocks(info_ref, rows, run):
    def job(index, carry):
        table = index // 3
        step = index % 3
        second, third = info_ref[0], info_ref[1]
        begin = jnp.where(table == 0, 0, jnp.where(table == 1, second, third))
        end = jnp.where(table == 0, second, jnp.where(table == 1, third, rows))
        first = begin // QB
        last = (end - 1) // QB
        merged = (last > first) & (end % QB > 0) & (end % QB <= begin % QB)
        count = last - first + 1 - merged.astype(jnp.int32)

        @pl.when(step < count)
        def _():
            block = first + step
            other = jnp.where(merged & (step == 0), last, block)
            lane = lax.broadcasted_iota(jnp.int32, (1, QB), 1)
            place = block * QB + lane
            here = (place >= begin) & (place < end)
            place = other * QB + lane
            there = (place < end) & (place >= jnp.where(other == block, rows, begin))
            run(
                pl.ds(pl.multiple_of(block * QB, QB), QB),
                pl.ds(pl.multiple_of(other * QB, QB), QB),
                table, here, there,
            )

        return carry

    lax.fori_loop(0, TABLES * 3, job, 0)


def store_both(ref, index, value, cols, others, here, there):
    ref[index + (cols,)] = jnp.where(here, value, ref[index + (cols,)])
    ref[index + (others,)] = jnp.where(there, value, ref[index + (others,)])


def cross_forward_kernel(info_ref, q_ref, k_ref, v_ref, o_ref, log_ref, score_ref, prob_ref):
    def run(cols, others, table, here, there):
        def finish(index, mixed, logs):
            store_both(o_ref, (head_rows(index),), mixed, cols, others, here, there)
            store_both(log_ref, (index, slice(None)), logs, cols, others, here, there)

        def query(index):
            rows = head_rows(index)
            return jnp.where(there, q_ref[rows, others], q_ref[rows, cols])

        forward_heads(
            query,
            lambda index: k_ref[table, head_rows(index), :],
            lambda index: v_ref[table, head_rows(index), :],
            finish, q_ref.shape[0] // HD, IMG, None, score_ref, prob_ref,
        )

    cross_blocks(info_ref, q_ref.shape[1], run)


def cross_backward_kernel(
    base, info_ref, q_ref, k_ref, v_ref, o_ref, log_ref, do_ref, dq_ref, dk_ref, dv_ref,
    sum_k, sum_v, score_ref, level_ref, prob_ref, delta_ref,
):
    sum_k[...] = jnp.zeros(sum_k.shape, F32)
    sum_v[...] = jnp.zeros(sum_v.shape, F32)

    def run(cols, others, table, here, there):
        def finish(index, grad_query, grad_key, grad_value):
            rows = head_rows(index)
            store_both(dq_ref, (rows,), grad_query, cols, others, here, there)
            sum_k[table, rows, :] += grad_key
            sum_v[table, rows, :] += grad_value

        def both(ref):
            def read(index):
                rows = head_rows(base + index)
                return jnp.where(there, ref[rows, others], ref[rows, cols])

            return read

        def logs(index):
            far = jnp.where(there, log_ref[base + index, :, others], -MASKED_SCORE)
            return jnp.where(here, log_ref[base + index, :, cols], far)

        seen = here | there
        grads = both(do_ref)
        zero = jnp.zeros((), BF16)
        backward_heads(
            both(q_ref),
            lambda index: k_ref[table, head_rows(base + index), :],
            lambda index: v_ref[table, head_rows(base + index), :],
            lambda index: jnp.where(seen, grads(index), zero),
            both(o_ref), logs, finish, dq_ref.shape[0] // HD, IMG, None,
            score_ref, level_ref, prob_ref, delta_ref,
        )

    cross_blocks(info_ref, q_ref.shape[1], run)
    dk_ref[...] = sum_k[...].astype(BF16)
    dv_ref[...] = sum_v[...].astype(BF16)


def feed_kernel(
    info_ref, o_ref, n1_ref, cot_ref, wnear_ref, wfar_ref, norm_ref,
    result_ref, dh_ref, do_ref, near_ref, far_ref, dnorm_ref,
    sum_up, sum_out, sum_norm, all_x2, all_active, all_du, all_dz, all_dac, w_ref,
):
    place_blocks(info_ref[3], wnear_ref, wfar_ref, w_ref)
    valid = info_ref[2]
    width = cot_ref.shape[1]
    hidden_width = (w_ref.shape[1] - width) // 2
    co_ref = w_ref.at[:, 0:width]
    up_ref = w_ref.at[:, width : width + hidden_width]
    down_ref = w_ref.at[:, width + hidden_width :]
    sum_norm[...] = jnp.zeros(sum_norm.shape, F32)
    root = 0.7978845608028654

    def chain(block):
        rows = slice(block * QB, (block + 1) * QB)
        branch = dot(o_ref[:, rows], co_ref[...], 0, 0)
        yield
        first = n1_ref[rows, :] * norm_ref[0:1, :] + norm_ref[3:4, :]
        n2, r2 = normalise(first + branch)
        x2 = n2 * norm_ref[1:2, :] + norm_ref[4:5, :]
        x2_low = x2.astype(BF16)
        all_x2[rows, :] = x2_low
        yield
        u = dot(x2_low, up_ref[...], 1, 0)
        yield
        square = u * u
        curve = jnp.tanh(root * u * (1.0 + 0.044715 * square))
        half = 0.5 * (1.0 + curve)
        active = (u * half).astype(BF16)
        slope = half + 0.5 * u * (1.0 - curve * curve) * (root * (1.0 + 3 * 0.044715 * square))
        all_active[rows, :] = active
        yield
        down = dot(active, down_ref[...], 1, 1)
        yield
        n3, r3 = normalise(x2 + down)
        result_ref[rows, :] = (n3 * norm_ref[2:3, :] + norm_ref[5:6, :]).astype(BF16)
        place = block * QB + lax.broadcasted_iota(jnp.int32, (QB, 1), 0)
        dy = jnp.where(place < valid, cot_ref[rows, :].astype(F32), 0.0)
        sum_norm[2:3, :] += column_sum(dy * n3)
        sum_norm[5:6, :] += column_sum(dy)
        dh3 = norm_back(dy, norm_ref[2:3, :], n3, r3)
        dz = dh3.astype(BF16)
        all_dz[rows, :] = dz
        yield
        df = dot(dz, down_ref[...], 1, 0)
        yield
        du = (df * slope).astype(BF16)
        all_du[rows, :] = du
        yield
        back = dot(du, up_ref[...], 1, 1)
        yield
        dx2 = dh3 + back
        sum_norm[1:2, :] += column_sum(dx2 * n2)
        sum_norm[4:5, :] += column_sum(dx2)
        dh2 = norm_back(dx2, norm_ref[1:2, :], n2, r2)
        dh_ref[rows, :] = dh2
        dac = dh2.astype(BF16)
        all_dac[rows, :] = dac
        yield
        do_ref[:, rows] = dot(co_ref[...], dac, 1, 1).astype(BF16)

    pipeline([chain(block) for block in range(cot_ref.shape[0] // QB)])
    me = info_ref[3]
    sum_up[...] = dot(all_x2[...], all_du[...], 0, 0)
    spread_blocks(me, sum_up, near_ref, far_ref, 0)
    sum_up[...] = dot(all_dz[...], all_active[...], 0, 0)
    spread_blocks(me, sum_up, near_ref, far_ref, hidden_width)
    sum_out[...] = dot(o_ref[...], all_dac[...], 1, 0)
    spread_blocks(me, sum_out, near_ref, far_ref, 2 * hidden_width)
    dnorm_ref[...] = sum_norm[...]


def inner_kernel(
    info_ref, dq0_ref, dq1_ref, dh2_ref, n1_ref, r1_ref, o_ref, wnear_ref, wfar_ref,
    norm_ref, image_ref, dk0_ref, dk1_ref, dv0_ref, dv1_ref, feed_ref,
    dh_ref, do_ref, near_ref, far_ref,
    sum_image, sum_inner, sum_norm, all_low, all_da, w_ref, columns,
):
    place_blocks(info_ref[3], wnear_ref, wfar_ref, w_ref)
    sum_norm[...] = jnp.zeros(sum_norm.shape, F32)
    width = dh_ref.shape[1]
    gain, shift = norm_ref[0:1, :], norm_ref[3:4, :]

    def chain(block):
        rows = slice(block * QB, (block + 1) * QB)
        dq = jnp.concatenate([dq0_ref[:, rows], dq1_ref[:, rows]], axis=0)
        back = dot(dq, w_ref[:, width : 2 * width], 0, 1)
        yield
        normed = n1_ref[rows, :].astype(F32)
        all_low[rows, :] = (normed * gain + shift).astype(BF16)
        dx1 = dh2_ref[rows, :] + back
        sum_norm[0:1, :] += column_sum(dx1 * normed)
        sum_norm[1:2, :] += column_sum(dx1)
        dh1 = norm_back(dx1, gain, normed, jnp.transpose(jnp.broadcast_to(r1_ref[0:1, rows], (128, QB)))[:, 0:1])
        dh_ref[rows, :] = dh1
        da = dh1.astype(BF16)
        all_da[rows, :] = da
        yield
        do_ref[:, rows] = dot(w_ref[:, 0:width], da, 1, 1).astype(BF16)

    pipeline([chain(block) for block in range(dh2_ref.shape[0] // QB)])
    me = info_ref[3]
    total = None
    for table in range(TABLES):
        image = image_ref[table * IMG : (table + 1) * IMG, :]
        grads = jnp.concatenate(
            [dk0_ref[table], dk1_ref[table], dv0_ref[table], dv1_ref[table]], axis=0
        )
        part = dot(image, grads, 0, 1)
        total = part if total is None else total + part
    sum_image[...] = total
    spread_blocks(me, sum_image, near_ref, far_ref, 2 * width)
    sum_inner[...] = dot(o_ref[...], all_da[...], 1, 0)
    spread_blocks(me, sum_inner, near_ref, far_ref, 0)
    dq = jnp.concatenate([dq0_ref[...], dq1_ref[...]], axis=0)
    sum_inner[...] = dot(all_low[...], dq, 0, 1)
    spread_blocks(me, sum_inner, near_ref, far_ref, width)
    rows = [sum_norm[0:1], feed_ref[1:2], feed_ref[2:3]]
    rows += [sum_norm[1:2], feed_ref[4:5], feed_ref[5:6], jnp.zeros((122, width), F32)]
    columns[...] = jnp.transpose(jnp.concatenate(rows, axis=0))
    spread_blocks(me, columns, near_ref, far_ref, 4 * width)


def image_grad_kernel(
    info_ref, dk0_ref, dk1_ref, dv0_ref, dv1_ref, near_ref, far_ref, out_ref, w_ref
):
    place_blocks(info_ref[3], near_ref, far_ref, w_ref)
    width = out_ref.shape[1]
    for table in range(TABLES):
        rows = slice(table * IMG, (table + 1) * IMG)
        grads = jnp.concatenate(
            [dk0_ref[table], dk1_ref[table], dv0_ref[table], dv1_ref[table]], axis=0
        )
        out_ref[rows, :] = dot(grads, w_ref[:, 2 * width : 4 * width], 0, 1)


def project_weight_kernel(
    info_ref, x_ref, dq0_ref, dq1_ref, dk0_ref, dk1_ref, dv0_ref, dv1_ref, near_ref, far_ref, total
):
    width = x_ref.shape[1]
    refs = (dq0_ref, dq1_ref, dk0_ref, dk1_ref, dv0_ref, dv1_ref)
    grads = jnp.concatenate([ref[...] for ref in refs], axis=0)
    total[:, 0 : 3 * width] = dot(x_ref[...], grads, 0, 1)
    spread_blocks(info_ref[3], total, near_ref, far_ref, 0)


def token_grad_kernel(
    info_ref, dq0_ref, dq1_ref, dk0_ref, dk1_ref, dv0_ref, dv1_ref, near_ref, far_ref, dh_ref,
    out_ref, w_ref,
):
    place_blocks(info_ref[3], near_ref, far_ref, w_ref)
    width = dh_ref.shape[1]
    refs = (dq0_ref, dq1_ref, dk0_ref, dk1_ref, dv0_ref, dv1_ref)
    for block in range(dh_ref.shape[0] // QB):
        rows = slice(block * QB, (block + 1) * QB)
        grads = jnp.concatenate([ref[:, rows] for ref in refs], axis=0)
        out_ref[rows, :] = dh_ref[rows, :] + dot(grads, w_ref[:, 0 : 3 * width], 0, 1)


def lamb_moments(weight, grad, first, second, decay):
    first_new = BETA_FIRST * first + (1.0 - BETA_FIRST) * grad
    second_new = BETA_SECOND * second + (1.0 - BETA_SECOND) * grad * grad
    first_hat = first_new / (1.0 - BETA_FIRST**STEP)
    second_hat = second_new / (1.0 - BETA_SECOND**STEP)
    update = first_hat / (jnp.sqrt(second_hat) + ADAM_EPSILON) + decay * weight
    return (first_new, second_new, update)


def total_of(value):
    return jnp.sum(jnp.sum(value * value, axis=0, keepdims=True), axis=1, keepdims=True)


def moments_kernel(per, *refs):
    both, last = refs[0:per], refs[per : 2 * per]
    wa, wf, wn, ma, va, mf, vf, mn, vn = refs[2 * per : 2 * per + 9]
    ga, gf, gn, oma, ova, omf, ovf, omn, ovn, ua, uf, un, sums = refs[2 * per + 9 :]
    width, hidden = wa.shape[2], wf.shape[2]
    lane = lax.broadcasted_iota(jnp.int32, (1, 128), 1)
    weights = jnp.zeros((1, 128), F32)
    updates = jnp.zeros((1, 128), F32)

    def grad(pieces, col, size):
        cols = slice(col, col + size)
        near = [ref[:, cols].astype(F32) for ref in pieces]
        total = near[0]
        for part in near[1:]:
            total += part
        return total

    def tensor(slot, value, index, weight, first, second, outs, decay):
        nonlocal weights, updates
        first_new, second_new, update = lamb_moments(
            weight[index], value, first[index], second[index], decay
        )
        for ref, part in zip(outs, (value, first_new, second_new, update)):
            ref[index] = part
        weights = jnp.where(lane == slot, total_of(weight[index]), weights)
        updates = jnp.where(lane == slot, total_of(update), updates)

    for slot in range(8):
        pieces, col = (last, slot) if slot < 3 else (both, 2 * hidden // width + slot - 2)
        if slot == 7:
            pieces, col = both, 2 * hidden // width
        value = grad(pieces, col * width, width)
        tensor(slot, value, slot, wa, ma, va, (ga, oma, ova, ua), WEIGHT_DECAY)
    for slot in range(2):
        value = grad(both, slot * hidden, hidden)
        tensor(8 + slot, value, slot, wf, mf, vf, (gf, omf, ovf, uf), WEIGHT_DECAY)
    norms = jnp.transpose(grad(both, 2 * hidden + 5 * width, 128))
    for slot in range(6):
        row = slice(slot, slot + 1)
        tensor(10 + slot, norms[row, :], row, wn, mn, vn, (gn, omn, ovn, un), 0.0)
    sums[...] = jnp.concatenate([weights, updates, jnp.zeros((6, 128), F32)], axis=0)


def apply_kernel(*refs):
    wa, wf, wn, ua, uf, un, na, nf, nn = refs[-10:-1]
    pieces, norms = refs[0:-10], refs[-1]
    total = pair_sum([ref[...] for ref in pieces])
    root = jnp.sqrt(total)
    norms[...] = root
    ratio = LEARN_RATE * (root[0:1, :] / root[1:2, :])
    for slot in range(8):
        na[slot] = wa[slot] - ratio[:, slot : slot + 1] * ua[slot]
    for slot in range(2):
        nf[slot] = wf[slot] - ratio[:, slot + 8 : slot + 9] * uf[slot]
    for slot in range(6):
        row = slice(slot, slot + 1)
        nn[row] = wn[row] - ratio[:, slot + 10 : slot + 11] * un[row]


def pair_sum(parts):
    while len(parts) > 1:
        parts = [parts[i] + parts[i + 1] for i in range(0, len(parts), 2)]
    return parts[0]


def shaped(*dims, kind=BF16):
    return jax.ShapeDtypeStruct(dims, kind)


def call(kernel, out_shape, operands, name, micros, info=True, scratch=(), grant=VMEM_GRANT, told=False):
    specs = [VMEM] * len(operands)
    if info:
        specs[0] = SMEM
    return pl.pallas_call(
        kernel,
        out_shape=out_shape,
        in_specs=specs,
        out_specs=[SMEM] + [VMEM] * (len(out_shape) - 1) if told else jax.tree.map(lambda _: VMEM, out_shape),
        scratch_shapes=[
            pltpu.VMEM(dims[:-1], BF16) if dims[-1] is BF16 else pltpu.VMEM(dims, F32)
            for dims in scratch
        ],
        compiler_params=pltpu.CompilerParams(vmem_limit_bytes=grant),
        cost_estimate=pl.CostEstimate(
            flops=int(micros * 0.02e9), bytes_accessed=0, transcendentals=0
        ),
        name=name,
    )(*operands)


def device_index():
    return lax.axis_index("wide") * lax.axis_size("narrow") + lax.axis_index("narrow")


def device_count():
    return lax.axis_size("wide") * lax.axis_size("narrow")


def exchange_slot(k, slots):
    return ((k >> 1) & 3) * (slots // 4) + (k >> 3)


def swap(value, mask):
    count = device_count()
    return lax.ppermute(value, AXES, [(i, i ^ mask) for i in range(count)])


def before(value, *others):
    return lax.optimization_barrier((value, others))[0]


def far_masks():
    return [k << 3 for k in range(1, device_count() >> 3)]


PLANE_MASKS = [2, 4, 6]


def gather_far(part):
    return jnp.stack([part] + [swap(part, mask) for mask in far_masks()])


def join_plane(parts):
    return jnp.concatenate(parts, axis=0)


def scatter_core(near, far):
    far = swap(far, 1)
    size = near.shape[0] // 4
    parts = [slice(k * size, (k + 1) * size) for k in range(4)]
    return [near[part].astype(F32) + far[part].astype(F32) for part in parts]


def scatter_plane(parts):
    sends = [part.astype(BF16) for part in parts[1:]]
    return parts[0], sends


def scatter_plane_end(own, sends):
    total = own
    for mask, send in zip(PLANE_MASKS, sends):
        total = total + swap(send, mask).astype(F32)
    return total[0], [total[k].astype(BF16) for k in range(1, total.shape[0])]


def scatter_far_end(own, sends):
    return [own] + [swap(send, mask) for mask, send in zip(far_masks(), sends)]


def block_order():
    order = [0] * device_count()
    for k in range(device_count()):
        slots = device_count() // 2
        order[exchange_slot(k, slots) + (k & 1) * slots] = k
    return jnp.array(order, jnp.int32) ^ device_index()


def whole_blocks(near, far):
    if near.shape[1] % 16 == 0:
        return near, far
    blocks = jnp.concatenate([near, far])
    full = jnp.zeros_like(blocks).at[block_order()].set(blocks)
    return full.reshape(-1, near.shape[2]), jnp.zeros((16, 128), BF16)


def spread_shapes(shard, cols):
    if shard % 16 == 0:
        return [shaped(device_count() // 2, shard, cols)] * 2
    return [shaped(device_count() * shard, cols), shaped(16, 128)]


def split_blocks(near, far):
    if near.ndim == 3:
        return near, far
    blocks = near.reshape(device_count(), -1, near.shape[1])[block_order()]
    return blocks[: device_count() // 2], blocks[device_count() // 2 :]


def local(
    tokens,
    image,
    segments,
    valid_len,
    cotangent,
    w_attn,
    w_ffn,
    norm_params,
    momentum_attn,
    variance_attn,
    momentum_ffn,
    variance_ffn,
    momentum_norm,
    variance_norm,
):
    tags, width = tokens.shape
    hidden_width = w_ffn.shape[2]
    shard = w_attn.shape[1]
    info, first_part, second_part = call(
        pack_kernel,
        [shaped(4, kind=jnp.int32), shaped(shard, 3 * width + 128)]
        + [shaped(shard, 5 * width + 2 * hidden_width)],
        (valid_len, segments, w_attn, w_ffn, norm_params),
        "pack",
        1,
        True,
        (),
        60 * 2**20,
        True,
    )
    first_far = gather_far(first_part)
    second_part = before(second_part, first_far)
    first_sent = [swap(first_far, mask) for mask in PLANE_MASKS]
    second_sent = [swap(second_part, mask) for mask in far_masks()]
    first_sent, second_sent = lax.optimization_barrier((first_sent, second_sent))
    second_far = jnp.stack([second_part] + second_sent)
    third_far = second_far[:, :, 4 * width :]
    second_far = second_far[:, :, 0 : 4 * width]
    first_plane = join_plane([first_far] + before(first_sent, second_far))
    first_core = swap(first_plane, 1)
    second_sent = [swap(second_far, mask) for mask in PLANE_MASKS]

    wide_shape = shaped(width, tags)
    half_shape = shaped(width // 2, tags)
    log_shape = shaped(HEADS, 1, tags, kind=F32)
    f32_rows = shaped(tags, width, kind=F32)
    first_blocks = whole_blocks(first_plane, first_core)
    norms, q, k, v = call(
        project_kernel,
        [shaped(8, width, kind=F32)] + [wide_shape] * 3,
        (info, tokens, *first_blocks),
        "project",
        3,
        True,
        [(width, 3 * width + 128, BF16)],
    )

    o, log_self = call(
        functools.partial(self_forward_kernel, 0),
        [wide_shape, log_shape],
        (before(info, second_far), q, k, v),
        "self_forward",
        8,
        True,
        [(3 * QB, QB), (2, 3 * QB, QB), (2, 3 * QB, QB, BF16)],
    )
    third_sent = [swap(third_far, mask) for mask in PLANE_MASKS]
    second_plane = join_plane([second_far] + before(second_sent, o))
    second_core = swap(second_plane, 1)
    image_shape = shaped(TABLES, width, IMG)
    image_half = shaped(TABLES, width // 2, IMG)
    second_blocks = whole_blocks(second_plane, second_core)
    w_second, kc, vc = call(
        image_kernel,
        [shaped(width, 4 * width)] + [image_shape] * 2,
        (before(info, third_far), image, *second_blocks),
        "image_project",
        6,
        True,
        (),
    )
    n1, n1_low, r1, qc = call(
        mid_kernel,
        [f32_rows, shaped(tags, width), shaped(8, tags, kind=F32), wide_shape],
        (tokens, o, w_second, norms),
        "mid",
        3,
        False,
        (),
    )
    oc, log_cross = call(
        cross_forward_kernel,
        [wide_shape, log_shape],
        (info, qc, kc, vc),
        "cross_forward",
        16,
        True,
        [(2, IMG, QB), (2, IMG, QB, BF16)],
    )
    third_plane = join_plane([third_far] + before(third_sent, oc))
    third_core = swap(third_plane, 1)
    feed_cols = 2 * hidden_width + width
    result, dh2, doc, feed_near, feed_far, norm_feed = call(
        feed_kernel,
        [
            shaped(tags, width),
            f32_rows,
            wide_shape,
            *spread_shapes(shard, feed_cols),
            shaped(8, width, kind=F32),
        ],
        (info, oc, n1, cotangent, *whole_blocks(third_plane, third_core), norms),
        "feed",
        15,
        True,
        [(width, hidden_width), (width, width), (8, width), (tags, width, BF16)]
        + [(tags, hidden_width, BF16)] * 2
        + [(tags, width, BF16)] * 2
        + [(width, feed_cols, BF16)],
    )

    def cross_backward(index, *deps):
        return call(
            functools.partial(cross_backward_kernel, index * HEADS // 2),
            [half_shape, image_half, image_half],
            [before(info, *deps), qc, kc, vc, oc, log_cross, doc],
            "cross_backward",
            14,
            True,
            [(TABLES, width // 2, IMG)] * 2 + [(2, IMG, QB)] * 2 + [(2, IMG, QB, BF16)] * 2,
        )

    def self_backward(index, *deps):
        return call(
            functools.partial(self_backward_kernel, index * HEADS // 2),
            [half_shape] * 3,
            [before(info, *deps), q, k, v, o, log_self, do],
            "self_backward",
            7,
            True,
            [(width // 2, tags)] * 2
            + [(3 * QB, QB)]
            + [(2, 3 * QB, QB)] * 2
            + [(2, 3 * QB, QB, BF16)] * 2,
        )

    feed_near, feed_far = split_blocks(feed_near, feed_far)
    dqc0, dkc0, dvc0 = cross_backward(0)
    feed_near = before(feed_near, dqc0)
    own_feed, send_feed = scatter_plane(scatter_core(feed_near, feed_far))
    dqc1, dkc1, dvc1 = cross_backward(1, send_feed)
    own_feed = before(own_feed, dqc1)
    own_feed, send_feed = scatter_plane_end(own_feed, send_feed)
    dh1, do, inner_near, inner_far = call(
        inner_kernel,
        [
            f32_rows,
            wide_shape,
            *spread_shapes(shard, 4 * width + 128),
        ],
        (before(info, send_feed), dqc0, dqc1, dh2, n1_low, r1, o, *second_blocks, norms)
        + (image, dkc0, dkc1, dvc0, dvc1, norm_feed),
        "inner",
        10,
        True,
        [(width, 2 * width), (width, width), (8, width)]
        + [(tags, width, BF16)] * 2
        + [(width, 4 * width, BF16), (width, 128)],
    )
    inner_near, inner_far = split_blocks(inner_near, inner_far)
    dq0, dk0, dv0 = self_backward(0)
    inner_near = before(inner_near, dq0)
    own_inner, send_inner = scatter_plane(scatter_core(inner_near, inner_far))
    dq1, dk1, dv1 = self_backward(1, send_inner)
    grads = (dq0, dq1, dk0, dk1, dv0, dv1)
    last_cols = 3 * width
    last_near, last_far = call(
        project_weight_kernel,
        spread_shapes(shard, last_cols),
        (info, tokens) + grads,
        "project_weight",
        3,
        True,
        [(width, last_cols)],
    )
    last_near, last_far = split_blocks(last_near, last_far)
    own_inner, send_inner = scatter_plane_end(before(own_inner, dq1), send_inner)
    send_both = [jnp.concatenate(pair, axis=1) for pair in zip(send_feed, send_inner)]
    pieces_both = scatter_far_end(jnp.concatenate([own_feed, own_inner], axis=1), send_both)
    own_last, send_last = scatter_plane(scatter_core(before(last_near, send_both), last_far))
    image_grad = call(
        image_grad_kernel,
        shaped(image.shape[0], width, kind=F32),
        (before(info, send_last), dkc0, dkc1, dvc0, dvc1, *second_blocks),
        "image_grad",
        6,
        True,
        [(width, 4 * width, BF16)],
    )
    token_grad = call(
        token_grad_kernel,
        f32_rows,
        (before(info, image_grad),) + grads + (*first_blocks, dh1),
        "token_grad",
        4,
        True,
        [(width, 3 * width + 128, BF16)],
    )
    own_last, send_last = scatter_plane_end(before(own_last, token_grad, pieces_both), send_last)
    pieces_last = scatter_far_end(own_last, send_last)

    weights = (w_attn, w_ffn, norm_params)
    moments = (momentum_attn, variance_attn, momentum_ffn, variance_ffn)
    moments = moments + (momentum_norm, variance_norm)
    like = [shaped(*array.shape, kind=F32) for array in weights + moments + weights]
    pieces = [*pieces_both, *pieces_last]
    per_chunk = len(pieces) // 2
    outs = call(
        lambda *refs: moments_kernel(per_chunk, *refs),
        like + [shaped(8, 128, kind=F32)],
        (*pieces, *weights, *moments),
        "moments",
        3,
        False,
    )
    grad_attn, grad_ffn, grad_norm = outs[0:3]
    first_attn, second_attn, first_ffn, second_ffn, first_norm, second_norm = outs[3:9]
    sums = outs[12]
    sums = sums + swap(sums, 1)
    sums = pair_sum([sums] + [swap(sums, mask) for mask in PLANE_MASKS])
    pieces = [sums] + [swap(sums, mask) for mask in far_masks()]
    new_attn, new_ffn, new_norm, norms_both = call(
        apply_kernel,
        like[0:3] + [shaped(8, 128, kind=F32)],
        (*pieces, *weights, *outs[9:12]),
        "apply",
        2,
        False,
    )
    weight_norms = norms_both[0, 0:16]
    update_norms = norms_both[1, 0:16]
    return (
        result,
        token_grad,
        image_grad,
        grad_attn,
        grad_ffn,
        grad_norm,
        new_attn,
        new_ffn,
        new_norm,
        first_attn,
        second_attn,
        first_ffn,
        second_ffn,
        first_norm,
        second_norm,
        weight_norms,
        update_norms,
    )


def solution(mesh):
    rows = P(AXES, None)
    stack = P(None, AXES, None)
    flat = P(None, AXES)
    in_specs = (rows, rows, rows, P(AXES), rows) + (stack, stack, flat)
    in_specs = in_specs + (stack, stack, stack, stack, flat, flat)
    out_specs = (rows, rows, rows, stack, stack, flat, stack, stack, flat)
    out_specs = out_specs + (stack, stack, stack, stack, flat, flat, P(), P())
    return jax.shard_map(local, mesh=mesh, in_specs=in_specs, out_specs=out_specs, check_vma=False)
```

```python
import functools

import jax
import jax.numpy as jnp
from jax import lax
from jax.experimental import pallas as pl
from jax.experimental.pallas import tpu as pltpu
from jax.sharding import PartitionSpec as P

HD = 64
HEADS = 8
IMG = 784
TABLES = 3
STEP = 10
QB = 256

MASKED_SCORE = -1000000000.0
BETA_FIRST = 0.9
BETA_SECOND = 0.999
LEARN_RATE = 0.3
WEIGHT_DECAY = 0.01
ADAM_EPSILON = 1e-06
NORM_EPSILON = 1e-05

VMEM_GRANT = 32 * 2**20

AXES = ("wide", "narrow")
F32 = jnp.float32
BF16 = jnp.bfloat16
VMEM = pl.BlockSpec(memory_space=pltpu.VMEM)
SMEM = pl.BlockSpec(memory_space=pltpu.SMEM)


def dot(left, right, left_dim, right_dim):
    return lax.dot_general(
        left, right, (((left_dim,), (right_dim,)), ((), ())), preferred_element_type=F32
    )


def normalise(hidden):
    centre = hidden - jnp.mean(hidden, axis=-1, keepdims=True)
    scale = lax.rsqrt(jnp.mean(centre * centre, axis=-1, keepdims=True) + NORM_EPSILON)
    return centre * scale, scale


def norm_back(grad, gain, normed, scale):
    inner = grad * gain
    return scale * (
        inner
        - jnp.mean(inner, axis=-1, keepdims=True)
        - normed * jnp.mean(inner * normed, axis=-1, keepdims=True)
    )


def column_sum(value):
    return jnp.sum(value, axis=0, keepdims=True)


def pipeline(chains, oldest_first=False):
    done = object()
    live = []
    waiting = list(chains)
    while live or waiting:
        if waiting:
            live.insert(len(live) if oldest_first else 0, waiting.pop(0))
        live = [chain for chain in live if next(chain, done) is not done]


def place_blocks(me, near_ref, far_ref, out_ref):
    if near_ref.shape == out_ref.shape:
        out_ref[...] = near_ref[...]
        return
    size = near_ref.shape[1]
    for k in range(2 * near_ref.shape[0]):
        ref = far_ref if k & 1 else near_ref
        row = pl.multiple_of((me ^ k) * size, size)
        out_ref[pl.ds(row, size), :] = ref[exchange_slot(k, ref.shape[0])]


def spread_blocks(me, source, near_ref, far_ref, col):
    cols = slice(col, col + source.shape[1])
    if near_ref.shape[0] == source.shape[0]:
        near_ref[:, cols] = source[...].astype(BF16)
        far_ref[...] = jnp.zeros(far_ref.shape, BF16)
        return
    size = near_ref.shape[1]
    for k in range(2 * near_ref.shape[0]):
        ref = far_ref if k & 1 else near_ref
        row = pl.multiple_of((me ^ k) * size, size)
        ref[exchange_slot(k, ref.shape[0]), :, cols] = source[pl.ds(row, size), :].astype(BF16)


def pack_kernel(valid_ref, segment_ref, wa_ref, wf_ref, wn_ref, info_ref, first_ref, rest_ref):
    segment = segment_ref[...]
    info_ref[0] = jnp.sum((segment < 1).astype(jnp.int32))
    info_ref[1] = jnp.sum((segment < 2).astype(jnp.int32))
    info_ref[2] = valid_ref[0]
    info_ref[3] = device_index()
    width, hidden = wa_ref.shape[2], wf_ref.shape[2]
    for slot in range(3):
        first_ref[:, slot * width : (slot + 1) * width] = wa_ref[slot].astype(BF16)
    rows = [wn_ref[...], jnp.zeros((128 - wn_ref.shape[0], wn_ref.shape[1]), F32)]
    first_ref[:, 3 * width :] = jnp.transpose(jnp.concatenate(rows, axis=0)).astype(BF16)
    for slot in range(5):
        rest_ref[:, slot * width : (slot + 1) * width] = wa_ref[slot + 3].astype(BF16)
    for slot in range(2):
        begin = 5 * width + slot * hidden
        rest_ref[:, begin : begin + hidden] = wf_ref[slot].astype(BF16)


def project_kernel(info_ref, x_ref, near_ref, far_ref, norm_ref, q_ref, k_ref, v_ref, w_ref):
    place_blocks(info_ref[3], near_ref, far_ref, w_ref)
    width = x_ref.shape[1]
    norm_ref[...] = jnp.transpose(w_ref[:, 3 * width :].astype(F32))[0:8, :]
    for block in range(x_ref.shape[0] // QB):
        cols = slice(block * QB, (block + 1) * QB)
        x = x_ref[cols, :]
        q_ref[:, cols] = (dot(w_ref[:, 0:width], x, 0, 1).astype(BF16) * 0.125).astype(BF16)
        k_ref[:, cols] = dot(w_ref[:, width : 2 * width], x, 0, 1).astype(BF16)
        v_ref[:, cols] = dot(w_ref[:, 2 * width : 3 * width], x, 0, 1).astype(BF16)


def head_rows(index):
    return slice(index * HD, (index + 1) * HD)


def forward_heads(query, key, value, finish, heads, count, bias, score_ref, prob_ref):
    def chain(index):
        slot = index % 2
        scores = dot(key(index), query(index), 0, 0)
        score_ref[slot, 0:count] = scores if bias is None else scores + bias[0:count]
        yield
        scores = score_ref[slot, 0:count]
        highest = jnp.max(scores, axis=0, keepdims=True)
        prob_ref[slot, 0:count] = jnp.exp(scores - highest).astype(BF16)
        yield
        ones = jnp.ones((16, count), BF16)
        mixed = dot(jnp.concatenate([value(index), ones], axis=0), prob_ref[slot, 0:count], 1, 0)
        total = mixed[HD : HD + 1]
        finish(index, (mixed[0:HD] / total).astype(BF16), highest + jnp.log(total))

    pipeline([chain(index) for index in range(heads)])


def backward_heads(
    query, key, value, grad, mixed, logs, finish, heads, count, bias,
    score_ref, level_ref, prob_ref, delta_ref,
):
    def chain(index):
        slot = index % 2
        scores = dot(key(index), query(index), 0, 0)
        score_ref[slot, 0:count] = scores if bias is None else scores + bias[0:count]
        level_ref[slot, 0:count] = dot(value(index), grad(index), 0, 0)
        yield
        level = column_sum(grad(index).astype(F32) * mixed(index).astype(F32))
        probs = jnp.exp(score_ref[slot, 0:count] - logs(index))
        prob_ref[slot, 0:count] = probs.astype(BF16)
        delta_ref[slot, 0:count] = (probs * (level_ref[slot, 0:count] - level)).astype(BF16)
        yield
        delta = delta_ref[slot, 0:count]
        finish(
            index,
            (dot(key(index), delta, 1, 0) * 0.125).astype(BF16),
            dot(query(index), delta, 1, 1),
            dot(grad(index), prob_ref[slot, 0:count], 1, 1),
        )

    pipeline([chain(index) for index in range(heads)], oldest_first=True)


def self_blocks(info_ref, rows, bias, run):
    second, third, valid = info_ref[0], info_ref[1], info_ref[2]

    def step(block, carry):
        start = block * QB
        first = jnp.where(start < second, 0, jnp.where(start < third, second, third))
        back = block - first // QB
        for extent in range(3):

            @pl.when(back == extent)
            def _():
                begin = (block - extent) * QB
                count = (extent + 1) * QB
                place = start + lax.broadcasted_iota(jnp.int32, (1, QB), 1)
                low = jnp.where(place < second, 0, jnp.where(place < third, second, third))
                high = jnp.minimum(place, valid - 1)
                key = begin + lax.broadcasted_iota(jnp.int32, (count, QB), 0)
                allowed = (key >= low) & ((key <= high) | (key == place))
                bias[0:count] = jnp.where(allowed, 0.0, MASKED_SCORE)
                run(
                    pl.ds(pl.multiple_of(start, QB), QB),
                    pl.ds(pl.multiple_of(begin, QB), count),
                    count,
                )

        return carry

    lax.fori_loop(0, rows // QB, step, 0)


def self_forward_kernel(
    base, info_ref, q_ref, k_ref, v_ref, o_ref, log_ref, bias_ref, score_ref, prob_ref
):
    def run(cols, keys, count):
        def finish(index, mixed, logs):
            o_ref[head_rows(index), cols] = mixed
            log_ref[index, :, cols] = logs

        forward_heads(
            lambda index: q_ref[head_rows(base + index), cols],
            lambda index: k_ref[head_rows(base + index), keys],
            lambda index: v_ref[head_rows(base + index), keys],
            finish, o_ref.shape[0] // HD, count, bias_ref, score_ref, prob_ref,
        )

    self_blocks(info_ref, q_ref.shape[1], bias_ref, run)


def self_backward_kernel(
    base, info_ref, q_ref, k_ref, v_ref, o_ref, log_ref, do_ref, dq_ref, dk_ref, dv_ref,
    sum_k, sum_v, bias_ref, score_ref, level_ref, prob_ref, delta_ref,
):
    sum_k[...] = jnp.zeros(sum_k.shape, F32)
    sum_v[...] = jnp.zeros(sum_v.shape, F32)

    def run(cols, keys, count):
        def finish(index, grad_query, grad_key, grad_value):
            dq_ref[head_rows(index), cols] = grad_query
            sum_k[head_rows(index), keys] += grad_key
            sum_v[head_rows(index), keys] += grad_value

        backward_heads(
            lambda index: q_ref[head_rows(base + index), cols],
            lambda index: k_ref[head_rows(base + index), keys],
            lambda index: v_ref[head_rows(base + index), keys],
            lambda index: do_ref[head_rows(base + index), cols],
            lambda index: o_ref[head_rows(base + index), cols],
            lambda index: log_ref[base + index, :, cols],
            finish, dq_ref.shape[0] // HD, count, bias_ref,
            score_ref, level_ref, prob_ref, delta_ref,
        )

    self_blocks(info_ref, q_ref.shape[1], bias_ref, run)
    dk_ref[...] = sum_k[...].astype(BF16)
    dv_ref[...] = sum_v[...].astype(BF16)


def mid_kernel(x_ref, o_ref, w_ref, norm_ref, n_ref, nlow_ref, r_ref, q_ref):
    gain, shift = norm_ref[0:1, :], norm_ref[3:4, :]
    width = x_ref.shape[1]

    def chain(block):
        rows = slice(block * QB, (block + 1) * QB)
        branch = dot(o_ref[:, rows], w_ref[:, 0:width], 0, 0)
        yield
        normed, scale = normalise(x_ref[rows, :].astype(F32) + branch)
        n_ref[rows, :] = normed
        nlow_ref[rows, :] = normed.astype(BF16)
        r_ref[:, rows] = jnp.transpose(jnp.broadcast_to(scale, (QB, 128)))[0:8]
        low = (normed * gain + shift).astype(BF16)
        yield
        query = dot(w_ref[:, width : 2 * width], low, 0, 1).astype(BF16)
        q_ref[:, rows] = (query * 0.125).astype(BF16)

    pipeline([chain(block) for block in range(x_ref.shape[0] // QB)])


def image_kernel(info_ref, image_ref, near_ref, far_ref, w_ref, k_ref, v_ref):
    place_blocks(info_ref[3], near_ref, far_ref, w_ref)
    width = image_ref.shape[1]
    for table in range(TABLES):
        image = image_ref[table * IMG : (table + 1) * IMG, :]
        k_ref[table] = dot(w_ref[:, 2 * width : 3 * width], image, 0, 1).astype(BF16)
        v_ref[table] = dot(w_ref[:, 3 * width : 4 * width], image, 0, 1).astype(BF16)


def cross_blocks(info_ref, rows, run):
    def job(index, carry):
        table = index // 3
        step = index % 3
        second, third = info_ref[0], info_ref[1]
        begin = jnp.where(table == 0, 0, jnp.where(table == 1, second, third))
        end = jnp.where(table == 0, second, jnp.where(table == 1, third, rows))
        first = begin // QB
        last = (end - 1) // QB
        merged = (last > first) & (end % QB > 0) & (end % QB <= begin % QB)
        count = last - first + 1 - merged.astype(jnp.int32)

        @pl.when(step < count)
        def _():
            block = first + step
            other = jnp.where(merged & (step == 0), last, block)
            lane = lax.broadcasted_iota(jnp.int32, (1, QB), 1)
            place = block * QB + lane
            here = (place >= begin) & (place < end)
            place = other * QB + lane
            there = (place < end) & (place >= jnp.where(other == block, rows, begin))
            run(
                pl.ds(pl.multiple_of(block * QB, QB), QB),
                pl.ds(pl.multiple_of(other * QB, QB), QB),
                table, here, there,
            )

        return carry

    lax.fori_loop(0, TABLES * 3, job, 0)


def store_both(ref, index, value, cols, others, here, there):
    ref[index + (cols,)] = jnp.where(here, value, ref[index + (cols,)])
    ref[index + (others,)] = jnp.where(there, value, ref[index + (others,)])


def cross_forward_kernel(info_ref, q_ref, k_ref, v_ref, o_ref, log_ref, score_ref, prob_ref):
    def run(cols, others, table, here, there):
        def finish(index, mixed, logs):
            store_both(o_ref, (head_rows(index),), mixed, cols, others, here, there)
            store_both(log_ref, (index, slice(None)), logs, cols, others, here, there)

        def query(index):
            rows = head_rows(index)
            return jnp.where(there, q_ref[rows, others], q_ref[rows, cols])

        forward_heads(
            query,
            lambda index: k_ref[table, head_rows(index), :],
            lambda index: v_ref[table, head_rows(index), :],
            finish, q_ref.shape[0] // HD, IMG, None, score_ref, prob_ref,
        )

    cross_blocks(info_ref, q_ref.shape[1], run)


def cross_backward_kernel(
    base, info_ref, q_ref, k_ref, v_ref, o_ref, log_ref, do_ref, dq_ref, dk_ref, dv_ref,
    sum_k, sum_v, score_ref, level_ref, prob_ref, delta_ref,
):
    sum_k[...] = jnp.zeros(sum_k.shape, F32)
    sum_v[...] = jnp.zeros(sum_v.shape, F32)

    def run(cols, others, table, here, there):
        def finish(index, grad_query, grad_key, grad_value):
            rows = head_rows(index)
            store_both(dq_ref, (rows,), grad_query, cols, others, here, there)
            sum_k[table, rows, :] += grad_key
            sum_v[table, rows, :] += grad_value

        def both(ref):
            def read(index):
                rows = head_rows(base + index)
                return jnp.where(there, ref[rows, others], ref[rows, cols])

            return read

        def logs(index):
            far = jnp.where(there, log_ref[base + index, :, others], -MASKED_SCORE)
            return jnp.where(here, log_ref[base + index, :, cols], far)

        seen = here | there
        grads = both(do_ref)
        zero = jnp.zeros((), BF16)
        backward_heads(
            both(q_ref),
            lambda index: k_ref[table, head_rows(base + index), :],
            lambda index: v_ref[table, head_rows(base + index), :],
            lambda index: jnp.where(seen, grads(index), zero),
            both(o_ref), logs, finish, dq_ref.shape[0] // HD, IMG, None,
            score_ref, level_ref, prob_ref, delta_ref,
        )

    cross_blocks(info_ref, q_ref.shape[1], run)
    dk_ref[...] = sum_k[...].astype(BF16)
    dv_ref[...] = sum_v[...].astype(BF16)


def feed_kernel(
    info_ref, o_ref, n1_ref, cot_ref, wnear_ref, wfar_ref, norm_ref,
    result_ref, dh_ref, do_ref, near_ref, far_ref, dnorm_ref,
    sum_up, sum_out, sum_norm, all_x2, all_active, all_du, all_dz, all_dac, w_ref,
):
    place_blocks(info_ref[3], wnear_ref, wfar_ref, w_ref)
    valid = info_ref[2]
    width = cot_ref.shape[1]
    hidden_width = (w_ref.shape[1] - width) // 2
    co_ref = w_ref.at[:, 0:width]
    up_ref = w_ref.at[:, width : width + hidden_width]
    down_ref = w_ref.at[:, width + hidden_width :]
    sum_norm[...] = jnp.zeros(sum_norm.shape, F32)
    root = 0.7978845608028654

    def chain(block):
        rows = slice(block * QB, (block + 1) * QB)
        branch = dot(o_ref[:, rows], co_ref[...], 0, 0)
        yield
        first = n1_ref[rows, :] * norm_ref[0:1, :] + norm_ref[3:4, :]
        n2, r2 = normalise(first + branch)
        x2 = n2 * norm_ref[1:2, :] + norm_ref[4:5, :]
        x2_low = x2.astype(BF16)
        all_x2[rows, :] = x2_low
        yield
        u = dot(x2_low, up_ref[...], 1, 0)
        yield
        square = u * u
        curve = jnp.tanh(root * u * (1.0 + 0.044715 * square))
        half = 0.5 * (1.0 + curve)
        active = (u * half).astype(BF16)
        slope = half + 0.5 * u * (1.0 - curve * curve) * (root * (1.0 + 3 * 0.044715 * square))
        all_active[rows, :] = active
        yield
        down = dot(active, down_ref[...], 1, 1)
        yield
        n3, r3 = normalise(x2 + down)
        result_ref[rows, :] = (n3 * norm_ref[2:3, :] + norm_ref[5:6, :]).astype(BF16)
        place = block * QB + lax.broadcasted_iota(jnp.int32, (QB, 1), 0)
        dy = jnp.where(place < valid, cot_ref[rows, :].astype(F32), 0.0)
        sum_norm[2:3, :] += column_sum(dy * n3)
        sum_norm[5:6, :] += column_sum(dy)
        dh3 = norm_back(dy, norm_ref[2:3, :], n3, r3)
        dz = dh3.astype(BF16)
        all_dz[rows, :] = dz
        yield
        df = dot(dz, down_ref[...], 1, 0)
        yield
        du = (df * slope).astype(BF16)
        all_du[rows, :] = du
        yield
        back = dot(du, up_ref[...], 1, 1)
        yield
        dx2 = dh3 + back
        sum_norm[1:2, :] += column_sum(dx2 * n2)
        sum_norm[4:5, :] += column_sum(dx2)
        dh2 = norm_back(dx2, norm_ref[1:2, :], n2, r2)
        dh_ref[rows, :] = dh2
        dac = dh2.astype(BF16)
        all_dac[rows, :] = dac
        yield
        do_ref[:, rows] = dot(co_ref[...], dac, 1, 1).astype(BF16)

    pipeline([chain(block) for block in range(cot_ref.shape[0] // QB)])
    me = info_ref[3]
    sum_up[...] = dot(all_x2[...], all_du[...], 0, 0)
    spread_blocks(me, sum_up, near_ref, far_ref, 0)
    sum_up[...] = dot(all_dz[...], all_active[...], 0, 0)
    spread_blocks(me, sum_up, near_ref, far_ref, hidden_width)
    sum_out[...] = dot(o_ref[...], all_dac[...], 1, 0)
    spread_blocks(me, sum_out, near_ref, far_ref, 2 * hidden_width)
    dnorm_ref[...] = sum_norm[...]


def inner_kernel(
    info_ref, dq0_ref, dq1_ref, dh2_ref, n1_ref, r1_ref, o_ref, wnear_ref, wfar_ref,
    norm_ref, image_ref, dk0_ref, dk1_ref, dv0_ref, dv1_ref, feed_ref,
    dh_ref, do_ref, near_ref, far_ref,
    sum_image, sum_inner, sum_norm, all_low, all_da, w_ref, columns,
):
    place_blocks(info_ref[3], wnear_ref, wfar_ref, w_ref)
    sum_norm[...] = jnp.zeros(sum_norm.shape, F32)
    width = dh_ref.shape[1]
    gain, shift = norm_ref[0:1, :], norm_ref[3:4, :]

    def chain(block):
        rows = slice(block * QB, (block + 1) * QB)
        dq = jnp.concatenate([dq0_ref[:, rows], dq1_ref[:, rows]], axis=0)
        back = dot(dq, w_ref[:, width : 2 * width], 0, 1)
        yield
        normed = n1_ref[rows, :].astype(F32)
        all_low[rows, :] = (normed * gain + shift).astype(BF16)
        dx1 = dh2_ref[rows, :] + back
        sum_norm[0:1, :] += column_sum(dx1 * normed)
        sum_norm[1:2, :] += column_sum(dx1)
        dh1 = norm_back(dx1, gain, normed, jnp.transpose(jnp.broadcast_to(r1_ref[0:1, rows], (128, QB)))[:, 0:1])
        dh_ref[rows, :] = dh1
        da = dh1.astype(BF16)
        all_da[rows, :] = da
        yield
        do_ref[:, rows] = dot(w_ref[:, 0:width], da, 1, 1).astype(BF16)

    pipeline([chain(block) for block in range(dh2_ref.shape[0] // QB)])
    me = info_ref[3]
    total = None
    for table in range(TABLES):
        image = image_ref[table * IMG : (table + 1) * IMG, :]
        grads = jnp.concatenate(
            [dk0_ref[table], dk1_ref[table], dv0_ref[table], dv1_ref[table]], axis=0
        )
        part = dot(image, grads, 0, 1)
        total = part if total is None else total + part
    sum_image[...] = total
    spread_blocks(me, sum_image, near_ref, far_ref, 2 * width)
    sum_inner[...] = dot(o_ref[...], all_da[...], 1, 0)
    spread_blocks(me, sum_inner, near_ref, far_ref, 0)
    dq = jnp.concatenate([dq0_ref[...], dq1_ref[...]], axis=0)
    sum_inner[...] = dot(all_low[...], dq, 0, 1)
    spread_blocks(me, sum_inner, near_ref, far_ref, width)
    rows = [sum_norm[0:1], feed_ref[1:2], feed_ref[2:3]]
    rows += [sum_norm[1:2], feed_ref[4:5], feed_ref[5:6], jnp.zeros((122, width), F32)]
    columns[...] = jnp.transpose(jnp.concatenate(rows, axis=0))
    spread_blocks(me, columns, near_ref, far_ref, 4 * width)


def image_grad_kernel(
    info_ref, dk0_ref, dk1_ref, dv0_ref, dv1_ref, near_ref, far_ref, out_ref, w_ref
):
    place_blocks(info_ref[3], near_ref, far_ref, w_ref)
    width = out_ref.shape[1]
    for table in range(TABLES):
        rows = slice(table * IMG, (table + 1) * IMG)
        grads = jnp.concatenate(
            [dk0_ref[table], dk1_ref[table], dv0_ref[table], dv1_ref[table]], axis=0
        )
        out_ref[rows, :] = dot(grads, w_ref[:, 2 * width : 4 * width], 0, 1)


def project_weight_kernel(
    info_ref, x_ref, dq0_ref, dq1_ref, dk0_ref, dk1_ref, dv0_ref, dv1_ref, near_ref, far_ref, total
):
    width = x_ref.shape[1]
    refs = (dq0_ref, dq1_ref, dk0_ref, dk1_ref, dv0_ref, dv1_ref)
    grads = jnp.concatenate([ref[...] for ref in refs], axis=0)
    total[:, 0 : 3 * width] = dot(x_ref[...], grads, 0, 1)
    spread_blocks(info_ref[3], total, near_ref, far_ref, 0)


def token_grad_kernel(
    info_ref, dq0_ref, dq1_ref, dk0_ref, dk1_ref, dv0_ref, dv1_ref, near_ref, far_ref, dh_ref,
    out_ref, w_ref,
):
    place_blocks(info_ref[3], near_ref, far_ref, w_ref)
    width = dh_ref.shape[1]
    refs = (dq0_ref, dq1_ref, dk0_ref, dk1_ref, dv0_ref, dv1_ref)
    for block in range(dh_ref.shape[0] // QB):
        rows = slice(block * QB, (block + 1) * QB)
        grads = jnp.concatenate([ref[:, rows] for ref in refs], axis=0)
        out_ref[rows, :] = dh_ref[rows, :] + dot(grads, w_ref[:, 0 : 3 * width], 0, 1)


def lamb_moments(weight, grad, first, second, decay):
    first_new = BETA_FIRST * first + (1.0 - BETA_FIRST) * grad
    second_new = BETA_SECOND * second + (1.0 - BETA_SECOND) * grad * grad
    first_hat = first_new / (1.0 - BETA_FIRST**STEP)
    second_hat = second_new / (1.0 - BETA_SECOND**STEP)
    update = first_hat / (jnp.sqrt(second_hat) + ADAM_EPSILON) + decay * weight
    return (first_new, second_new, update)


def total_of(value):
    return jnp.sum(jnp.sum(value * value, axis=0, keepdims=True), axis=1, keepdims=True)


def moments_kernel(per, *refs):
    both, last = refs[0:per], refs[per : 2 * per]
    wa, wf, wn, ma, va, mf, vf, mn, vn = refs[2 * per : 2 * per + 9]
    ga, gf, gn, oma, ova, omf, ovf, omn, ovn, ua, uf, un, sums = refs[2 * per + 9 :]
    width, hidden = wa.shape[2], wf.shape[2]
    lane = lax.broadcasted_iota(jnp.int32, (1, 128), 1)
    weights = jnp.zeros((1, 128), F32)
    updates = jnp.zeros((1, 128), F32)

    def grad(pieces, col, size):
        cols = slice(col, col + size)
        near = [ref[:, cols].astype(F32) for ref in pieces]
        total = near[0]
        for part in near[1:]:
            total += part
        return total

    def tensor(slot, value, index, weight, first, second, outs, decay):
        nonlocal weights, updates
        first_new, second_new, update = lamb_moments(
            weight[index], value, first[index], second[index], decay
        )
        for ref, part in zip(outs, (value, first_new, second_new, update)):
            ref[index] = part
        weights = jnp.where(lane == slot, total_of(weight[index]), weights)
        updates = jnp.where(lane == slot, total_of(update), updates)

    for slot in range(8):
        pieces, col = (last, slot) if slot < 3 else (both, 2 * hidden // width + slot - 2)
        if slot == 7:
            pieces, col = both, 2 * hidden // width
        value = grad(pieces, col * width, width)
        tensor(slot, value, slot, wa, ma, va, (ga, oma, ova, ua), WEIGHT_DECAY)
    for slot in range(2):
        value = grad(both, slot * hidden, hidden)
        tensor(8 + slot, value, slot, wf, mf, vf, (gf, omf, ovf, uf), WEIGHT_DECAY)
    norms = jnp.transpose(grad(both, 2 * hidden + 5 * width, 128))
    for slot in range(6):
        row = slice(slot, slot + 1)
        tensor(10 + slot, norms[row, :], row, wn, mn, vn, (gn, omn, ovn, un), 0.0)
    sums[...] = jnp.concatenate([weights, updates, jnp.zeros((6, 128), F32)], axis=0)


def apply_kernel(*refs):
    wa, wf, wn, ua, uf, un, na, nf, nn = refs[-10:-1]
    pieces, norms = refs[0:-10], refs[-1]
    total = pair_sum([ref[...] for ref in pieces])
    root = jnp.sqrt(total)
    norms[...] = root
    ratio = LEARN_RATE * (root[0:1, :] / root[1:2, :])
    for slot in range(8):
        na[slot] = wa[slot] - ratio[:, slot : slot + 1] * ua[slot]
    for slot in range(2):
        nf[slot] = wf[slot] - ratio[:, slot + 8 : slot + 9] * uf[slot]
    for slot in range(6):
        row = slice(slot, slot + 1)
        nn[row] = wn[row] - ratio[:, slot + 10 : slot + 11] * un[row]


def pair_sum(parts):
    while len(parts) > 1:
        parts = [parts[i] + parts[i + 1] for i in range(0, len(parts), 2)]
    return parts[0]


def shaped(*dims, kind=BF16):
    return jax.ShapeDtypeStruct(dims, kind)


def call(kernel, out_shape, operands, name, micros, info=True, scratch=(), grant=VMEM_GRANT, told=False):
    specs = [VMEM] * len(operands)
    if info:
        specs[0] = SMEM
    return pl.pallas_call(
        kernel,
        out_shape=out_shape,
        in_specs=specs,
        out_specs=[SMEM] + [VMEM] * (len(out_shape) - 1) if told else jax.tree.map(lambda _: VMEM, out_shape),
        scratch_shapes=[
            pltpu.VMEM(dims[:-1], BF16) if dims[-1] is BF16 else pltpu.VMEM(dims, F32)
            for dims in scratch
        ],
        compiler_params=pltpu.CompilerParams(vmem_limit_bytes=grant),
        cost_estimate=pl.CostEstimate(
            flops=int(micros * 0.02e9), bytes_accessed=0, transcendentals=0
        ),
        name=name,
    )(*operands)


def device_index():
    return lax.axis_index("wide") * lax.axis_size("narrow") + lax.axis_index("narrow")


def device_count():
    return lax.axis_size("wide") * lax.axis_size("narrow")


def exchange_slot(k, slots):
    return ((k >> 1) & 3) * (slots // 4) + (k >> 3)


def swap(value, mask):
    count = device_count()
    return lax.ppermute(value, AXES, [(i, i ^ mask) for i in range(count)])


def before(value, *others):
    return lax.optimization_barrier((value, others))[0]


def far_masks():
    return [k << 3 for k in range(1, device_count() >> 3)]


PLANE_MASKS = [2, 4, 6]


def gather_far(part):
    return jnp.stack([part] + [swap(part, mask) for mask in far_masks()])


def join_plane(parts):
    return jnp.concatenate(parts, axis=0)


def scatter_core(near, far):
    far = swap(far, 1)
    size = near.shape[0] // 4
    parts = [slice(k * size, (k + 1) * size) for k in range(4)]
    return [near[part].astype(F32) + far[part].astype(F32) for part in parts]


def scatter_plane(parts):
    sends = [part.astype(BF16) for part in parts[1:]]
    return parts[0], sends


def scatter_plane_end(own, sends):
    total = own
    for mask, send in zip(PLANE_MASKS, sends):
        total = total + swap(send, mask).astype(F32)
    return total[0], [total[k].astype(BF16) for k in range(1, total.shape[0])]


def scatter_far_end(own, sends):
    return [own] + [swap(send, mask) for mask, send in zip(far_masks(), sends)]


def block_order():
    order = [0] * device_count()
    for k in range(device_count()):
        slots = device_count() // 2
        order[exchange_slot(k, slots) + (k & 1) * slots] = k
    return jnp.array(order, jnp.int32) ^ device_index()


def whole_blocks(near, far):
    if near.shape[1] % 16 == 0:
        return near, far
    blocks = jnp.concatenate([near, far])
    full = jnp.zeros_like(blocks).at[block_order()].set(blocks)
    return full.reshape(-1, near.shape[2]), jnp.zeros((16, 128), BF16)


def spread_shapes(shard, cols):
    if shard % 16 == 0:
        return [shaped(device_count() // 2, shard, cols)] * 2
    return [shaped(device_count() * shard, cols), shaped(16, 128)]


def split_blocks(near, far):
    if near.ndim == 3:
        return near, far
    blocks = near.reshape(device_count(), -1, near.shape[1])[block_order()]
    return blocks[: device_count() // 2], blocks[device_count() // 2 :]


def local(
    tokens,
    image,
    segments,
    valid_len,
    cotangent,
    w_attn,
    w_ffn,
    norm_params,
    momentum_attn,
    variance_attn,
    momentum_ffn,
    variance_ffn,
    momentum_norm,
    variance_norm,
):
    tags, width = tokens.shape
    hidden_width = w_ffn.shape[2]
    shard = w_attn.shape[1]
    info, first_part, second_part = call(
        pack_kernel,
        [shaped(4, kind=jnp.int32), shaped(shard, 3 * width + 128)]
        + [shaped(shard, 5 * width + 2 * hidden_width)],
        (valid_len, segments, w_attn, w_ffn, norm_params),
        "pack",
        1,
        True,
        (),
        60 * 2**20,
        True,
    )
    first_far = gather_far(first_part)
    second_part = before(second_part, first_far)
    first_sent = [swap(first_far, mask) for mask in PLANE_MASKS]
    second_sent = [swap(second_part, mask) for mask in far_masks()]
    first_sent, second_sent = lax.optimization_barrier((first_sent, second_sent))
    second_far = jnp.stack([second_part] + second_sent)
    third_far = second_far[:, :, 4 * width :]
    second_far = second_far[:, :, 0 : 4 * width]
    first_plane = join_plane([first_far] + before(first_sent, second_far))
    first_core = swap(first_plane, 1)
    second_sent = [swap(second_far, mask) for mask in PLANE_MASKS]

    wide_shape = shaped(width, tags)
    half_shape = shaped(width // 2, tags)
    log_shape = shaped(HEADS, 1, tags, kind=F32)
    f32_rows = shaped(tags, width, kind=F32)
    first_blocks = whole_blocks(first_plane, first_core)
    norms, q, k, v = call(
        project_kernel,
        [shaped(8, width, kind=F32)] + [wide_shape] * 3,
        (info, tokens, *first_blocks),
        "project",
        3,
        True,
        [(width, 3 * width + 128, BF16)],
    )

    o, log_self = call(
        functools.partial(self_forward_kernel, 0),
        [wide_shape, log_shape],
        (before(info, second_far), q, k, v),
        "self_forward",
        8,
        True,
        [(3 * QB, QB), (2, 3 * QB, QB), (2, 3 * QB, QB, BF16)],
    )
    third_sent = [swap(third_far, mask) for mask in PLANE_MASKS]
    second_plane = join_plane([second_far] + before(second_sent, o))
    second_core = swap(second_plane, 1)
    image_shape = shaped(TABLES, width, IMG)
    image_half = shaped(TABLES, width // 2, IMG)
    second_blocks = whole_blocks(second_plane, second_core)
    w_second, kc, vc = call(
        image_kernel,
        [shaped(width, 4 * width)] + [image_shape] * 2,
        (before(info, third_far), image, *second_blocks),
        "image_project",
        6,
        True,
        (),
    )
    n1, n1_low, r1, qc = call(
        mid_kernel,
        [f32_rows, shaped(tags, width), shaped(8, tags, kind=F32), wide_shape],
        (tokens, o, w_second, norms),
        "mid",
        3,
        False,
        (),
    )
    oc, log_cross = call(
        cross_forward_kernel,
        [wide_shape, log_shape],
        (info, qc, kc, vc),
        "cross_forward",
        16,
        True,
        [(2, IMG, QB), (2, IMG, QB, BF16)],
    )
    third_plane = join_plane([third_far] + before(third_sent, oc))
    third_core = swap(third_plane, 1)
    feed_cols = 2 * hidden_width + width
    result, dh2, doc, feed_near, feed_far, norm_feed = call(
        feed_kernel,
        [
            shaped(tags, width),
            f32_rows,
            wide_shape,
            *spread_shapes(shard, feed_cols),
            shaped(8, width, kind=F32),
        ],
        (info, oc, n1, cotangent, *whole_blocks(third_plane, third_core), norms),
        "feed",
        15,
        True,
        [(width, hidden_width), (width, width), (8, width), (tags, width, BF16)]
        + [(tags, hidden_width, BF16)] * 2
        + [(tags, width, BF16)] * 2
        + [(width, feed_cols, BF16)],
    )

    def cross_backward(index, *deps):
        return call(
            functools.partial(cross_backward_kernel, index * HEADS // 2),
            [half_shape, image_half, image_half],
            [before(info, *deps), qc, kc, vc, oc, log_cross, doc],
            "cross_backward",
            14,
            True,
            [(TABLES, width // 2, IMG)] * 2 + [(2, IMG, QB)] * 2 + [(2, IMG, QB, BF16)] * 2,
        )

    def self_backward(index, *deps):
        return call(
            functools.partial(self_backward_kernel, index * HEADS // 2),
            [half_shape] * 3,
            [before(info, *deps), q, k, v, o, log_self, do],
            "self_backward",
            7,
            True,
            [(width // 2, tags)] * 2
            + [(3 * QB, QB)]
            + [(2, 3 * QB, QB)] * 2
            + [(2, 3 * QB, QB, BF16)] * 2,
        )

    feed_near, feed_far = split_blocks(feed_near, feed_far)
    dqc0, dkc0, dvc0 = cross_backward(0)
    feed_near = before(feed_near, dqc0)
    own_feed, send_feed = scatter_plane(scatter_core(feed_near, feed_far))
    dqc1, dkc1, dvc1 = cross_backward(1, send_feed)
    own_feed = before(own_feed, dqc1)
    own_feed, send_feed = scatter_plane_end(own_feed, send_feed)
    dh1, do, inner_near, inner_far = call(
        inner_kernel,
        [
            f32_rows,
            wide_shape,
            *spread_shapes(shard, 4 * width + 128),
        ],
        (before(info, send_feed), dqc0, dqc1, dh2, n1_low, r1, o, *second_blocks, norms)
        + (image, dkc0, dkc1, dvc0, dvc1, norm_feed),
        "inner",
        10,
        True,
        [(width, 2 * width), (width, width), (8, width)]
        + [(tags, width, BF16)] * 2
        + [(width, 4 * width, BF16), (width, 128)],
    )
    inner_near, inner_far = split_blocks(inner_near, inner_far)
    dq0, dk0, dv0 = self_backward(0)
    inner_near = before(inner_near, dq0)
    own_inner, send_inner = scatter_plane(scatter_core(inner_near, inner_far))
    dq1, dk1, dv1 = self_backward(1, send_inner)
    grads = (dq0, dq1, dk0, dk1, dv0, dv1)
    last_cols = 3 * width
    last_near, last_far = call(
        project_weight_kernel,
        spread_shapes(shard, last_cols),
        (info, tokens) + grads,
        "project_weight",
        3,
        True,
        [(width, last_cols)],
    )
    last_near, last_far = split_blocks(last_near, last_far)
    own_inner, send_inner = scatter_plane_end(before(own_inner, dq1), send_inner)
    send_both = [jnp.concatenate(pair, axis=1) for pair in zip(send_feed, send_inner)]
    pieces_both = scatter_far_end(jnp.concatenate([own_feed, own_inner], axis=1), send_both)
    own_last, send_last = scatter_plane(scatter_core(before(last_near, send_both), last_far))
    image_grad = call(
        image_grad_kernel,
        shaped(image.shape[0], width, kind=F32),
        (before(info, send_last), dkc0, dkc1, dvc0, dvc1, *second_blocks),
        "image_grad",
        6,
        True,
        [(width, 4 * width, BF16)],
    )
    token_grad = call(
        token_grad_kernel,
        f32_rows,
        (before(info, image_grad),) + grads + (*first_blocks, dh1),
        "token_grad",
        4,
        True,
        [(width, 3 * width + 128, BF16)],
    )
    own_last, send_last = scatter_plane_end(before(own_last, token_grad, pieces_both), send_last)
    pieces_last = scatter_far_end(own_last, send_last)

    weights = (w_attn, w_ffn, norm_params)
    moments = (momentum_attn, variance_attn, momentum_ffn, variance_ffn)
    moments = moments + (momentum_norm, variance_norm)
    like = [shaped(*array.shape, kind=F32) for array in weights + moments + weights]
    pieces = [*pieces_both, *pieces_last]
    per_chunk = len(pieces) // 2
    outs = call(
        lambda *refs: moments_kernel(per_chunk, *refs),
        like + [shaped(8, 128, kind=F32)],
        (*pieces, *weights, *moments),
        "moments",
        3,
        False,
    )
    grad_attn, grad_ffn, grad_norm = outs[0:3]
    first_attn, second_attn, first_ffn, second_ffn, first_norm, second_norm = outs[3:9]
    sums = outs[12]
    sums = sums + swap(sums, 1)
    sums = pair_sum([sums] + [swap(sums, mask) for mask in PLANE_MASKS])
    pieces = [sums] + [swap(sums, mask) for mask in far_masks()]
    new_attn, new_ffn, new_norm, norms_both = call(
        apply_kernel,
        like[0:3] + [shaped(8, 128, kind=F32)],
        (*pieces, *weights, *outs[9:12]),
        "apply",
        2,
        False,
    )
    weight_norms = norms_both[0, 0:16]
    update_norms = norms_both[1, 0:16]
    return (
        result,
        token_grad,
        image_grad,
        grad_attn,
        grad_ffn,
        grad_norm,
        new_attn,
        new_ffn,
        new_norm,
        first_attn,
        second_attn,
        first_ffn,
        second_ffn,
        first_norm,
        second_norm,
        weight_norms,
        update_norms,
    )


def solution(mesh):
    rows = P(AXES, None)
    stack = P(None, AXES, None)
    flat = P(None, AXES)
    in_specs = (rows, rows, rows, P(AXES), rows) + (stack, stack, flat)
    in_specs = in_specs + (stack, stack, stack, stack, flat, flat)
    out_specs = (rows, rows, rows, stack, stack, flat, stack, stack, flat)
    out_specs = out_specs + (stack, stack, stack, stack, flat, flat, P(), P())
    return jax.shard_map(local, mesh=mesh, in_specs=in_specs, out_specs=out_specs, check_vma=False)
```
